32 devices in a mesh: row: 4 (over z), col: 8 (over y, x, core).
Axes of the slice: x: 2, y: 2, z: 4, core: 2. Of those that a mesh axis runs over, the one named last changes fastest.
Arguments:
- tokens: bfloat16 [32768, 1024], P(('row', 'col')), may hold values from -6 to 6
- condition: bfloat16 [32, 1024], P('row', 'col'), may hold values from -6 to 6
- mod_weight: bfloat16 [1024, 6, 1024], P('row', None, 'col'), may hold values from -0.1875 to 0.1875
- mod_bias: bfloat16 [6, 1024], P(None, 'col'), may hold values from -4 to 4
- qkv_weight: bfloat16 [1024, 16, 192], P('row', 'col'), may hold values from -0.1875 to 0.1875
- qv_bias: bfloat16 [16, 128], P('col'), may hold values from -4 to 4
- out_weight: bfloat16 [16, 64, 1024], P('col', None, 'row'), may hold values from -0.75 to 0.75
- out_bias: bfloat16 [1024], P('col'), may hold values from -4 to 4
- fc1_weight: bfloat16 [1024, 4096], P('row', 'col'), may hold values from -0.1875 to 0.1875
- fc1_bias: bfloat16 [4096], P('col'), may hold values from -4 to 4
- fc2_weight: bfloat16 [4096, 1024], P('col', 'row'), may hold values from -0.09375 to 0.09375
- fc2_bias: bfloat16 [1024], P('col'), may hold values from -4 to 4
- cotangent: bfloat16 [32768, 1024], P(('row', 'col')), may hold values from -6 to 6
Outputs:
- layer_out: bfloat16 [32768, 1024], P(('row', 'col'))
- tokens_grad: float32 [32768, 1024], P(('row', 'col'))
- condition_grad: float32 [32, 1024], P('row', 'col')
- mod_weight_grad: float32 [1024, 6, 1024], P('row', None, 'col')
- mod_bias_grad: float32 [6, 1024], P(None, 'col')
- qkv_weight_grad: float32 [1024, 16, 192], P('row', 'col')
- qv_bias_grad: float32 [16, 128], P('col')
- out_weight_grad: float32 [16, 64, 1024], P('col', None, 'row')
- out_bias_grad: float32 [1024], P('col')
- fc1_weight_grad: float32 [1024, 4096], P('row', 'col')
- fc1_bias_grad: float32 [4096], P('col')
- fc2_weight_grad: float32 [4096, 1024], P('col', 'row')
- fc2_bias_grad: float32 [1024], P('col')
The draws below stay inside these ranges and needn't reach their ends.
All inputs are finite; a program needn't handle non-finite values.
Results may differ from the reference program's by a relative error of at most 0.02.
Values may be sent and summed in bfloat16 or wider, within the bound.
No kernel may reach another device: no remote copies, remote signals or barrier semaphores. Data moves between devices by JAX's collectives and lax.ppermute only.
A program may use at most 320 MiB of HBM per device.

```python
import math
import jax
import jax.numpy as jnp
from jax import lax

D = 1024
HEADS = 16
HD = 64
FF = 4096
LEN = 1024
SEQS = 32
TOKENS = 32768
N_COL = 8


def steps_of(stream_key, dims, cuts, smallest, largest):
    def one(position, parts):
        heights = jax.random.uniform(jax.random.fold_in(jax.random.fold_in(stream_key, 6), position), (parts,), jnp.float32, smallest / len(cuts), largest / len(cuts))
        return jnp.repeat(jnp.exp(heights), dims[position] // parts).reshape((-1,) + (1,) * (len(dims) - position - 1))

    factor_of = one(*cuts[0])
    for cut in cuts[1:]:
        factor_of = factor_of * one(*cut)
    return factor_of


def bell_draw(own_key, dims, scale, bound, pieces=(), held_as=jnp.bfloat16):
    values = jax.random.normal(own_key, dims, jnp.float32) * scale
    if len(pieces) > 0:
        values = steps_of(own_key, dims, pieces, -0.22, 0.18) * values
    return jnp.clip(values, min=-bound, max=bound).astype(held_as)


def setup_inputs(seed: int = 0) -> dict:
    key_list = jax.random.split(jax.random.key(seed), 14)
    tokens = bell_draw(key_list[0], (TOKENS, D), 1.0, 6.0, ((0, 32),))
    condition = bell_draw(key_list[1], (SEQS, D), 1.0, 6.0, ((0, 4), (1, 8)))
    mod_weight = bell_draw(key_list[2], (D, 6, D), D ** -0.5, 0.1875, ((0, 4), (2, 8)))
    mod_bias = bell_draw(key_list[3], (6, D), 0.3, 4.0, ((1, 8),))
    qkv_weight = bell_draw(key_list[4], (D, HEADS, 3 * HD), D ** -0.5, 0.1875, ((0, 4), (1, 8)))
    qv_bias = bell_draw(key_list[5], (HEADS, 2 * HD), 0.3, 4.0, ((0, 8),))
    out_weight = bell_draw(key_list[6], (HEADS, HD, D), HD ** -0.5, 0.75, ((0, 8), (2, 4)))
    out_bias = bell_draw(key_list[7], (D,), 0.3, 4.0, ((0, 8),))
    fc1_weight = bell_draw(key_list[8], (D, FF), D ** -0.5, 0.1875, ((0, 4), (1, 8)))
    fc1_bias = bell_draw(key_list[9], (FF,), 0.3, 4.0, ((0, 8),))
    fc2_weight = bell_draw(key_list[10], (FF, D), FF ** -0.5, 0.09375, ((0, 8), (1, 4)))
    fc2_bias = bell_draw(key_list[11], (D,), 0.3, 4.0, ((0, 8),))
    cotangent = bell_draw(key_list[12], (TOKENS, D), 1.0, 6.0, ((0, 32),))
    return dict(tokens=tokens, condition=condition, mod_weight=mod_weight, mod_bias=mod_bias, qkv_weight=qkv_weight, qv_bias=qv_bias, out_weight=out_weight, out_bias=out_bias, fc1_weight=fc1_weight, fc1_bias=fc1_bias, fc2_weight=fc2_weight, fc2_bias=fc2_bias, cotangent=cotangent)


@jax.custom_vjp
def low(v):
    return lax.optimization_barrier(v.astype(jnp.bfloat16)).astype(jnp.float32)

@jax.custom_vjp
def low_back(v):
    return v

def low_keep(v):
    return (low(v), None)

def low_pass(kept, grad):
    return (grad,)

def back_keep(v):
    return (v, None)

def back_low(kept, grad):
    return (low(grad),)
low.defvjp(low_keep, low_pass)
low_back.defvjp(back_keep, back_low)
PRECISE = lax.Precision.HIGHEST
EPSILON = 1e-06

def silu_fn(values):
    return values * jax.nn.sigmoid(values)

def gelu_tanh(values):
    return 0.5 * values * (1.0 + jnp.tanh(math.sqrt(2.0 / math.pi) * (values + 0.044715 * values * values * values)))

def normalize(matrix):
    average = lax.optimization_barrier(jnp.mean(matrix, -1, keepdims=True))
    spread = lax.optimization_barrier(jnp.mean(matrix * matrix, -1, keepdims=True)) - average * average
    return (matrix - average) * lax.rsqrt(spread + EPSILON)

def attention(queries, key_rows, value_rows):
    scores = jnp.einsum('gqhe,gkhe->ghqk', queries, key_rows, precision=PRECISE) * HD ** (-0.5)
    scores = low_back(scores)
    row_max = lax.optimization_barrier(jnp.max(scores, -1, keepdims=True))
    expon = jnp.exp(scores - row_max)
    prob_rows = low(expon / lax.optimization_barrier(jnp.sum(expon, -1, keepdims=True)))
    mixed_rows = jnp.einsum('ghqk,gkhe->gqhe', prob_rows, value_rows, precision=PRECISE)
    return low(low_back(mixed_rows))

def layer_group(group_rows, group_mod, weights):
    qkv_w, qv_b, out_w, out_b, fc1_w, fc1_b, fc2_w, fc2_b = weights
    group_len = group_rows.shape[0]
    seq_group = group_len // LEN
    per_token = jnp.repeat(group_mod, LEN, axis=0)
    shift_attn, scale_attn, gate_attn = (per_token[:, 0], per_token[:, 1], per_token[:, 2])
    shift_feed, scale_feed, gate_feed = (per_token[:, 3], per_token[:, 4], per_token[:, 5])
    hidden_attn = low(normalize(group_rows) * (1.0 + scale_attn) + shift_attn)
    hidden_copies = low_back(jnp.broadcast_to(hidden_attn, (N_COL, group_len, D)))
    projected = jnp.einsum('ctd,dcj->tcj', hidden_copies, qkv_w.reshape(D, N_COL, -1), precision=PRECISE)
    projected = projected.reshape(group_len, HEADS, 3 * HD)
    queries = low(low_back(projected[..., :HD] + qv_b[:, :HD]))
    key_rows = low(low_back(projected[..., HD:2 * HD]))
    value_rows = low(low_back(projected[..., 2 * HD:] + qv_b[:, HD:]))
    item_shape = (seq_group, LEN, HEADS, HD)
    mixed_rows = attention(queries.reshape(item_shape), key_rows.reshape(item_shape), value_rows.reshape(item_shape))
    mixed_rows = mixed_rows.reshape(group_len, N_COL, -1)
    partials = low(jnp.einsum('tcm,cmd->ctd', mixed_rows, out_w.reshape(N_COL, -1, D), precision=PRECISE))
    attention_out = low_back(lax.optimization_barrier(jnp.sum(partials, 0))) + out_b
    resid_mid = group_rows + gate_attn * attention_out
    hidden_feed = low(normalize(resid_mid) * (1.0 + scale_feed) + shift_feed)
    feed_copies = low_back(jnp.broadcast_to(hidden_feed, (N_COL, group_len, D)))
    pre_act = jnp.einsum('ctd,dcf->tcf', feed_copies, fc1_w.reshape(D, N_COL, -1), precision=PRECISE)
    pre_act = low_back(pre_act + fc1_b.reshape(N_COL, -1))
    activation = low(gelu_tanh(pre_act))
    feed_parts = low(jnp.einsum('tcf,cfd->ctd', activation, fc2_w.reshape(N_COL, -1, D), precision=PRECISE))
    feed_out = low_back(lax.optimization_barrier(jnp.sum(feed_parts, 0))) + fc2_b
    return resid_mid + gate_feed * feed_out

def forward(tokens, condition, mod_weight, mod_bias, qkv_w, qv_b, out_w, out_b, fc1_w, fc1_b, fc2_w, fc2_b):
    weights = (qkv_w, qv_b, out_w, out_b, fc1_w, fc1_b, fc2_w, fc2_b)
    cond_act = low(silu_fn(condition))
    modulation = jnp.einsum('sd,dke->ske', cond_act, mod_weight, precision=PRECISE) + mod_bias
    seq_group = math.gcd(SEQS, max(1, 4096 // LEN))
    grouped_tokens = tokens.reshape(SEQS // seq_group, seq_group * LEN, D)
    grouped_mod = modulation.reshape(SEQS // seq_group, seq_group, 6, D)
    group_step = jax.checkpoint(lambda bundle: layer_group(bundle[0], bundle[1], weights))
    layer_rows = lax.map(group_step, (grouped_tokens, grouped_mod))
    return layer_rows.reshape(SEQS * LEN, D)

def reference(tokens, condition, mod_weight, mod_bias, qkv_weight, qv_bias, out_weight, out_bias, fc1_weight, fc1_bias, fc2_weight, fc2_bias, cotangent):
    inputs = tuple((entry.astype(jnp.float32) for entry in (tokens, condition, mod_weight, mod_bias, qkv_weight, qv_bias, out_weight, out_bias, fc1_weight, fc1_bias, fc2_weight, fc2_bias)))
    result, pullback = jax.vjp(forward, *inputs)
    gradients = pullback(cotangent.astype(jnp.float32))
    return (result.astype(jnp.bfloat16), gradients[0], gradients[1], gradients[2], gradients[3], gradients[4], gradients[5], gradients[6], gradients[7], gradients[8], gradients[9], gradients[10], gradients[11])
```

```python
import functools
import math

import jax
import jax.numpy as jnp
from jax import lax
from jax.experimental import pallas as pl
from jax.experimental.pallas import tpu as pltpu
from jax.sharding import PartitionSpec as P

D = 1024
HD = 64
LEN = 1024
PAIR = 2 * HD

EPSILON = 1e-06
PRECISE = lax.Precision.HIGHEST
NN = (((1,), (0,)), ((), ()))
NT = (((1,), (1,)), ((), ()))
TN = (((0,), (0,)), ((), ()))
F32 = jnp.float32
BF16 = jnp.bfloat16
QUERY_ROWS = 512
VMEM_BYTES = 56 * 1024 * 1024


def dot(left, right, dims=NN):
    return lax.dot_general(left, right, dims, preferred_element_type=F32)


def silu_fn(values):
    return values * jax.nn.sigmoid(values)


def gelu_both(values):
    c = math.sqrt(2.0 / math.pi)
    square = values * values
    t = jnp.tanh(c * values * (1.0 + 0.044715 * square))
    half = 0.5 * (1.0 + t)
    slope = half + 0.5 * values * (1.0 - t * t) * (c * (1.0 + 3.0 * 0.044715 * square))
    return values * half, slope


def normalize(resid):
    average = jnp.mean(resid, 1, keepdims=True)
    spread = jnp.mean(resid * resid, 1, keepdims=True) - average * average
    inv_std = lax.rsqrt(spread + EPSILON)
    return ((resid - average) * inv_std, inv_std)


def normalize_back(grad_norm, normed, inv_std):
    average = jnp.mean(grad_norm, 1, keepdims=True)
    crossed = jnp.mean(grad_norm * normed, 1, keepdims=True)
    return inv_std * (grad_norm - average - normed * crossed)


def after(array, *earlier):
    return lax.optimization_barrier((array, *earlier))[0]


def head_lanes(shape, head):
    lane = lax.broadcasted_iota(jnp.int32, shape, 1)
    return lane < HD if head == 0 else lane >= HD


def attend_kernel(q_ref, k_ref, v_ref, mixed_ref, log_ref):
    queries = q_ref[...] * jnp.asarray(HD**-0.5, BF16)
    key_rows = k_ref[...]
    value_rows = v_ref[...]
    mask = head_lanes(key_rows.shape, 0)
    zero = jnp.zeros_like(key_rows)
    keys = (jnp.where(mask, key_rows, zero), jnp.where(mask, zero, key_rows))
    length = queries.shape[0]
    for start in range(0, length, QUERY_ROWS):
        stop = start + QUERY_ROWS
        q_part = queries[start:stop]
        outs = []
        for head in range(2):
            scores = dot(keys[head], q_part, NT)
            top = jnp.max(scores, 0, keepdims=True)
            expon = jnp.exp(scores - top)
            total = jnp.sum(expon, 0, keepdims=True)
            out = dot(value_rows, expon.astype(BF16), TN) / total
            outs.append(out[head * HD : (head + 1) * HD])
            log_ref[0, 0, head : head + 1, start:stop] = top + jnp.log(total)
        mixed_ref[start:stop, :] = jnp.concatenate(outs, 0).T.astype(BF16)


def attend_back_kernel(q_ref, k_ref, v_ref, mixed_ref, grad_ref, log_ref, out_ref):
    scale = jnp.asarray(HD**-0.5, BF16)
    queries = q_ref[...] * scale
    key_rows = k_ref[...]
    value_rows = v_ref[...]
    grad_rows = grad_ref[...]
    mask = head_lanes(key_rows.shape, 0)
    zero = jnp.zeros_like(key_rows)
    keys = (jnp.where(mask, key_rows, zero), jnp.where(mask, zero, key_rows))
    values = (jnp.where(mask, value_rows, zero), jnp.where(mask, zero, value_rows))
    keys_scaled = key_rows * scale
    product = grad_rows.astype(F32) * mixed_ref[...].astype(F32)
    picks = (
        lax.broadcasted_iota(jnp.int32, (8, PAIR), 0)
        == lax.broadcasted_iota(jnp.int32, (8, PAIR), 1) // HD
    ).astype(F32)
    inner = lax.dot_general(picks, product, NT, precision=PRECISE, preferred_element_type=F32)
    length = queries.shape[0]
    grad_k = [None, None]
    grad_v = [None, None]
    for start in range(0, length, QUERY_ROWS):
        stop = start + QUERY_ROWS
        q_part = queries[start:stop]
        g_part = grad_rows[start:stop]
        outs = []
        for head in range(2):
            scores = dot(keys[head], q_part, NT)
            probs = jnp.exp(scores - log_ref[0, 0, head : head + 1, start:stop])
            grad_probs = dot(values[head], g_part, NT)
            grad_scores = (probs * (grad_probs - inner[head : head + 1, start:stop])).astype(BF16)
            part_v = dot(probs.astype(BF16), g_part)
            part_k = dot(grad_scores, q_part)
            grad_v[head] = part_v if grad_v[head] is None else grad_v[head] + part_v
            grad_k[head] = part_k if grad_k[head] is None else grad_k[head] + part_k
            out = dot(keys_scaled, grad_scores, TN)
            outs.append(out[head * HD : (head + 1) * HD])
        out_ref[start:stop, 0:PAIR] = jnp.concatenate(outs, 0).T.astype(BF16)
    out_ref[:, PAIR : 2 * PAIR] = jnp.where(mask, grad_k[0], grad_k[1]).astype(BF16)
    out_ref[:, 2 * PAIR :] = jnp.where(mask, grad_v[0], grad_v[1]).astype(BF16)


def attention_specs(latents, pairs):
    part = lambda offset: pl.BlockSpec((LEN, PAIR), lambda s, p: (s, 3 * p + offset))
    plain = pl.BlockSpec((LEN, PAIR), lambda s, p: (s, p))
    logs = pl.BlockSpec((1, 1, 2, LEN), lambda s, p: (s, p, 0, 0))
    return [part(0), part(1), part(2)], plain, logs


def attend(projected, latents, pairs):
    parts, plain, logs = attention_specs(latents, pairs)
    rows = projected.shape[0]
    return pl.pallas_call(
        attend_kernel,
        grid=(latents, pairs),
        in_specs=parts,
        out_specs=[plain, logs],
        out_shape=[
            jax.ShapeDtypeStruct((rows, pairs * PAIR), BF16),
            jax.ShapeDtypeStruct((latents, pairs, 2, LEN), F32),
        ],
        compiler_params=pltpu.CompilerParams(vmem_limit_bytes=VMEM_BYTES),
        cost_estimate=pl.CostEstimate(
            flops=latents * pairs * 2 * 2 * 2 * LEN * LEN * PAIR,
            bytes_accessed=rows * pairs * PAIR * 8,
            transcendentals=latents * pairs * 2 * LEN * LEN,
        ),
        name="attend",
    )(projected, projected, projected)


def attend_back(projected, mixed, grad_mixed, log_totals, latents, pairs):
    parts, plain, logs = attention_specs(latents, pairs)
    rows = projected.shape[0]
    return pl.pallas_call(
        attend_back_kernel,
        grid=(latents, pairs),
        in_specs=[*parts, plain, plain, logs],
        out_specs=pl.BlockSpec((LEN, 3 * PAIR), lambda s, p: (s, p)),
        out_shape=jax.ShapeDtypeStruct((rows, pairs * 3 * PAIR), BF16),
        compiler_params=pltpu.CompilerParams(vmem_limit_bytes=VMEM_BYTES),
        cost_estimate=pl.CostEstimate(
            flops=latents * pairs * 2 * 5 * 2 * LEN * LEN * PAIR,
            bytes_accessed=rows * pairs * PAIR * 16,
            transcendentals=latents * pairs * 2 * LEN * LEN,
        ),
        name="attend_back",
    )(projected, projected, projected, mixed, grad_mixed, log_totals)


class Grid:
    def __init__(self):
        self.rows = lax.axis_size("row")
        self.cols = lax.axis_size("col")
        self.chips = self.cols // 2
        self.bits = [1 << b for b in range(self.chips.bit_length() - 1)]
        self.orders = (self.bits, self.bits[::-1])
        self.row = lax.axis_index("row")
        self.col = lax.axis_index("col")
        self.core = self.col % 2
        source = lax.iota(jnp.int32, self.chips) ^ (self.col // 2)
        self.choose = (
            (2 * source + self.core)[:, None] == lax.iota(jnp.int32, self.cols)[None, :]
        ).astype(F32)

    def swap(self, array, flip):
        pairs = [(i, i ^ flip) for i in range(self.cols)]
        return lax.ppermute(array, "col", pairs)

    def swap_core(self, array):
        return self.swap(array, 1)

    def swap_chip(self, array, bit):
        return self.swap(array, 2 * bit)

    def to_relative(self, blocks):
        flat = blocks.reshape(self.cols, -1).astype(F32)
        picked = lax.dot_general(
            self.choose, flat, NN, precision=PRECISE, preferred_element_type=F32
        )
        return picked.reshape((self.chips,) + blocks.shape[1:])

    def to_absolute(self, blocks):
        flat = blocks.reshape(self.chips, -1)
        placed = lax.dot_general(
            self.choose, flat, TN, precision=PRECISE, preferred_element_type=F32
        )
        return placed.reshape((self.cols,) + blocks.shape[1:])

    def gather_rows(self, block):
        count = self.rows
        got = [block]
        for step in range(1, count):
            got.append(
                lax.ppermute(block, "row", [(i, (i + step) % count) for i in range(count)])
            )
        stacked = jnp.stack(got)
        ordered = [
            lax.dynamic_index_in_dim(stacked, (self.row - i) % count, 0, keepdims=False)
            for i in range(count)
        ]
        return jnp.concatenate(ordered, 0), got[-1]

    def scatter_rows(self, whole):
        count = self.rows
        blocks = whole.reshape(count, whole.shape[0] // count, whole.shape[1])
        total = lax.dynamic_index_in_dim(blocks, self.row, 0, keepdims=False).astype(F32)
        for step in range(1, count):
            sent = lax.dynamic_index_in_dim(blocks, (self.row + step) % count, 0, keepdims=False)
            total = total + lax.ppermute(
                sent, "row", [(i, (i + step) % count) for i in range(count)]
            ).astype(F32)
        return total

    def gather_chips(self, block, order):
        held, ids = block, [0]
        for number, bit in enumerate(order):
            got = self.swap_chip(held, bit)
            new_ids = [bit ^ i for i in ids]
            if number == len(order) - 1:
                return held, ids, got, new_ids
            held, ids = jnp.concatenate([held, got], 1), ids + new_ids

    def scatter_chips(self, keep, send, order):
        for number, bit in enumerate(order[::-1]):
            total = keep + self.swap_chip(send, bit).astype(F32)
            if number == len(order) - 1:
                return total
            half = total.shape[1] // 2
            keep, send = total[:, :half], total[:, half:].astype(BF16)


def split_columns(array, ids):
    width = array.shape[1] // len(ids)
    return {i: array[:, n * width : (n + 1) * width] for n, i in enumerate(ids)}


def all_exchange(pieces):
    return lax.all_to_all(pieces, ("row", "col"), 0, 0, tiled=True)


def per_device(
    tokens,
    condition,
    mod_weight,
    mod_bias,
    qkv_weight,
    qv_bias,
    out_weight,
    out_bias,
    fc1_weight,
    fc1_bias,
    fc2_weight,
    fc2_bias,
    cotangent,
):
    grid = Grid()
    rows, cols, chips = grid.rows, grid.cols, grid.chips
    devices = rows * cols
    local_rows = tokens.shape[0]
    both_rows = 2 * local_rows
    latents = both_rows // LEN
    span = LEN // local_rows
    seq_rows = condition.shape[0]
    seqs = seq_rows * rows
    row_width = D // rows
    col_width = D // cols
    local_heads = qkv_weight.shape[1]
    local_units = fc1_weight.shape[1]
    plane_heads = local_heads * chips
    pairs = plane_heads // 2
    qkv_width = local_heads * 3 * HD
    out_width = local_heads * HD

    if local_heads % 2 == 0:
        qkv_local = (
            qkv_weight.reshape(row_width, local_heads // 2, 2, 3, HD)
            .transpose(0, 1, 3, 2, 4)
            .reshape(row_width, qkv_width)
        )
    else:
        qkv_local = qkv_weight.reshape(row_width, qkv_width)
    attn_local = jnp.concatenate(
        [qkv_local, out_weight.reshape(out_width, row_width).T], 1
    )
    attn_width = qkv_width + out_width
    fc1_local = fc1_weight
    fc2_local = fc2_weight.T

    small = jnp.concatenate(
        [
            condition.reshape(-1),
            fc1_bias,
            qv_bias.reshape(-1),
            out_bias,
            fc2_bias,
        ]
    )
    small_all = all_exchange(
        jnp.broadcast_to(small.reshape(1, -1, 128), (devices, small.size // 128, 128))
    ).reshape(rows, cols, -1)
    cut = seq_rows * col_width
    cond_all = (
        small_all[:, :, :cut]
        .reshape(rows, cols, seq_rows, col_width)
        .transpose(0, 2, 1, 3)
        .reshape(seqs, D)
    )
    biases = small_all[0, :, cut:]
    fc1_bias_all = biases[:, :local_units]
    qv_bias_all = biases[:, local_units : local_units + local_heads * PAIR]
    out_bias_all = biases[:, -2 * col_width : -col_width].reshape(1, D).astype(F32)
    fc2_bias_all = biases[:, -col_width:].reshape(1, D).astype(F32)

    cond_act = silu_fn(cond_all.astype(F32)).astype(BF16)
    cond_act = lax.dynamic_slice_in_dim(cond_act, grid.row * row_width, row_width, 1)
    mod_flat = mod_weight.reshape(row_width, 6 * col_width)
    own_bias = jnp.where(grid.row == 0, mod_bias.astype(F32), 0.0)
    mod_part = dot(cond_act, mod_flat).reshape(seqs, 6, col_width) + own_bias
    mod_part = jnp.broadcast_to(
        mod_part[:, None], (seqs, span, 6, col_width)
    ).reshape(devices, 6, col_width)
    modulation = (
        all_exchange(mod_part)
        .reshape(rows, cols, 6, col_width)
        .sum(0)
        .transpose(1, 0, 2)
        .reshape(6, 1, D)
    )
    shift_attn, scale_attn, gate_attn, shift_feed, scale_feed, gate_feed = modulation

    attn_rows, mark = grid.gather_rows(attn_local)
    fc1_rows, mark = grid.gather_rows(after(fc1_local, mark))
    fc2_rows, mark = grid.gather_rows(after(fc2_local, mark))
    half = D // 2
    top = grid.gather_chips(attn_rows[:half], grid.orders[0])
    low = grid.gather_chips(attn_rows[half:], grid.orders[1])
    attn_top = {**split_columns(top[0], top[1]), **split_columns(top[2], top[3])}
    attn_low = {**split_columns(low[0], low[1]), **split_columns(low[2], low[3])}
    attn_blocks = [jnp.concatenate([attn_top[i], attn_low[i]], 0) for i in range(chips)]
    if local_heads % 2 == 0:
        qkv_w = jnp.concatenate([b[:, :qkv_width] for b in attn_blocks], 1)
    else:
        qkv_w = (
            jnp.stack([b[:, :qkv_width] for b in attn_blocks], 1)
            .reshape(D, pairs, 2, 3, HD)
            .transpose(0, 1, 3, 2, 4)
            .reshape(D, pairs * 3 * PAIR)
        )
    out_w = jnp.concatenate([b[:, qkv_width:] for b in attn_blocks], 1)

    def gather_units(rows_held, earlier):
        rows_held = after(rows_held, *earlier)
        middle = local_units // 2
        first = grid.gather_chips(rows_held[:, :middle], grid.orders[0])
        second = grid.gather_chips(rows_held[:, middle:], grid.orders[1])
        groups = [first[0], first[2], second[0], second[2]]
        ids = [(0, first[1]), (0, first[3]), (1, second[1]), (1, second[3])]
        return groups, ids

    fc1_groups, unit_ids = gather_units(fc1_rows, (top[2], low[2]))
    fc2_groups, unit_ids = gather_units(fc2_rows, (fc1_groups[1], fc1_groups[3]))

    fc1_bias_rel = grid.to_relative(fc1_bias_all).reshape(chips, 2, local_units // 2)
    fc1_bias_groups = [
        jnp.concatenate([fc1_bias_rel[i, part] for i in ids]) for part, ids in unit_ids
    ]
    qv_rel = grid.to_relative(qv_bias_all).reshape(pairs, 2, 2, HD).transpose(0, 2, 1, 3)
    qkv_bias_rel = jnp.concatenate(
        [qv_rel[:, :1], jnp.zeros_like(qv_rel[:, :1]), qv_rel[:, 1:]], 1
    ).reshape(1, pairs * 3 * PAIR)

    def both(mine):
        return jnp.concatenate([mine, grid.swap_core(mine)], 0)

    def own_total(partial):
        theirs = partial[local_rows:].astype(BF16)
        return partial[:local_rows] + grid.swap_core(theirs).astype(F32)

    resid = tokens.astype(F32)
    normed_attn, inv_attn = normalize(resid)
    hidden_attn = both((normed_attn * (1.0 + scale_attn) + shift_attn).astype(BF16))
    upstream = cotangent.astype(F32)
    grad_feed = upstream * gate_feed
    bias_fc2 = jnp.sum(grad_feed, 0)
    grad_feed_low = both(grad_feed.astype(BF16))

    projected = (dot(hidden_attn, qkv_w) + qkv_bias_rel).astype(BF16)
    mixed, log_totals = attend(projected, latents, pairs)
    attention_out = own_total(dot(mixed, out_w, NT)) + out_bias_all
    resid_mid = resid + gate_attn * attention_out
    normed_feed, inv_feed = normalize(resid_mid)
    hidden_feed = both((normed_feed * (1.0 + scale_feed) + shift_feed).astype(BF16))
    acts, slopes = [], []
    for weight, bias in zip(fc1_groups, fc1_bias_groups):
        act, slope = gelu_both(dot(hidden_feed, weight) + bias)
        acts.append(act.astype(BF16))
        slopes.append(slope.astype(BF16))

    def scatter_units(left, rights):
        sums = []
        for number, order in enumerate(grid.orders):
            send = dot(left, rights[2 * number + 1], TN).astype(BF16)
            keep = dot(left, rights[2 * number], TN)
            sums.append(grid.scatter_chips(keep, send, order))
        return grid.scatter_rows(jnp.concatenate(sums, 1).astype(BF16))

    fc2_part = scatter_units(grad_feed_low, acts).T
    grad_pres = [
        (dot(grad_feed_low, weight) * slope.astype(F32)).astype(BF16)
        for weight, slope in zip(fc2_groups, slopes)
    ]
    bias_fc1 = [jnp.sum(g.astype(F32), 0) for g in grad_pres]
    fc1_part = scatter_units(hidden_feed, grad_pres)
    grad_hidden_feed = own_total(
        sum(dot(g, weight, NT) for g, weight in zip(grad_pres, fc1_groups))
    )
    feed_out = (
        own_total(sum(dot(a, weight, NT) for a, weight in zip(acts, fc2_groups))) + fc2_bias_all
    )
    layer_out = (resid_mid + gate_feed * feed_out).astype(BF16)

    grad_resid_mid = upstream + normalize_back(
        grad_hidden_feed * (1.0 + scale_feed), normed_feed, inv_feed
    )
    grad_attention = grad_resid_mid * gate_attn
    bias_out = jnp.sum(grad_attention, 0)
    grad_attention_low = both(grad_attention.astype(BF16))

    grad_mixed = dot(grad_attention_low, out_w).astype(BF16)
    grad_out = dot(grad_attention_low, mixed, TN)
    grad_projected = attend_back(projected, mixed, grad_mixed, log_totals, latents, pairs)
    bias_qkv = jnp.sum(grad_projected.astype(F32), 0)
    grad_qkv = dot(hidden_attn, grad_projected, TN)
    if local_heads % 2 == 0:
        grad_qkv = grad_qkv.reshape(D, chips, qkv_width)
    else:
        grad_qkv = (
            grad_qkv.reshape(D, pairs, 3, 2, HD).transpose(0, 1, 3, 2, 4).reshape(D, chips, qkv_width)
        )
    grad_out = grad_out.reshape(D, chips, out_width)

    def pick(part, ids):
        lines = slice(0, half) if part == 0 else slice(half, D)
        return jnp.concatenate(
            [jnp.concatenate([grad_qkv[lines, i], grad_out[lines, i]], 1) for i in ids], 1
        )

    attn_sums = []
    for number, gathered in enumerate((top, low)):
        attn_sums.append(
            grid.scatter_chips(
                pick(number, gathered[1]),
                pick(number, gathered[3]).astype(BF16),
                grid.orders[number],
            )
        )
    attn_part = grid.scatter_rows(jnp.concatenate(attn_sums, 0).astype(BF16))
    qkv_part = attn_part[:, :qkv_width]
    if local_heads % 2 == 0:
        qkv_part = qkv_part.reshape(row_width, local_heads // 2, 3, 2, HD).transpose(0, 1, 3, 2, 4)
    qkv_part = qkv_part.reshape(row_width, local_heads, 3 * HD)
    out_part = attn_part[:, qkv_width:].T.reshape(local_heads, HD, row_width)

    grad_hidden_attn = own_total(dot(grad_projected, qkv_w, NT))
    tokens_grad = grad_resid_mid + normalize_back(
        grad_hidden_attn * (1.0 + scale_attn), normed_attn, inv_attn
    )

    mod_rows = jnp.stack(
        [
            jnp.sum(grad_hidden_attn, 0),
            jnp.sum(grad_hidden_attn * normed_attn, 0),
            jnp.sum(grad_resid_mid * attention_out, 0),
            jnp.sum(grad_hidden_feed, 0),
            jnp.sum(grad_hidden_feed * normed_feed, 0),
            jnp.sum(upstream * feed_out, 0),
            bias_out,
            bias_fc2,
        ]
    )
    mod_rows = mod_rows.reshape(8, cols, col_width).transpose(1, 0, 2)
    fc1_split = [split_columns(b[None], ids) for b, (_, ids) in zip(bias_fc1, unit_ids)]
    first_half = {**fc1_split[0], **fc1_split[1]}
    second_half = {**fc1_split[2], **fc1_split[3]}
    fc1_rel = jnp.concatenate(
        [jnp.concatenate([first_half[i], second_half[i]], 1) for i in range(chips)], 0
    )
    qkv_rel = bias_qkv.reshape(pairs, 3, 2, HD)
    qv_rel = jnp.stack([qkv_rel[:, 0], qkv_rel[:, 2]], 2).reshape(chips, local_heads * PAIR)
    hidden_rows = grid.to_absolute(jnp.concatenate([fc1_rel, qv_rel], 1)).reshape(
        cols, -1, col_width
    )
    pieces = jnp.concatenate([mod_rows, hidden_rows], 1)
    pieces = jnp.broadcast_to(pieces[None], (rows,) + pieces.shape).reshape(
        devices, -1, col_width
    )
    arrived = all_exchange(pieces)
    grad_modulation = arrived[:, :6].reshape(seqs, span, 6, col_width).sum(1)
    sums = arrived[:, 6:].sum(0)
    out_bias_grad = sums[0]
    fc2_bias_grad = sums[1]
    hidden_sums = sums[2:].reshape(-1)
    fc1_bias_grad = hidden_sums[:local_units]
    qv_bias_grad = hidden_sums[local_units:].reshape(local_heads, PAIR)
    mod_bias_grad = jnp.sum(grad_modulation, 0)
    grad_mod_flat = grad_modulation.reshape(seqs, 6 * col_width)
    mod_part_grad = lax.dot_general(
        cond_act.astype(F32), grad_mod_flat, TN, precision=PRECISE, preferred_element_type=F32
    ).reshape(row_width, 6, col_width)
    cond_part = lax.dot_general(
        grad_mod_flat,
        mod_flat.astype(F32),
        NT,
        precision=PRECISE,
        preferred_element_type=F32,
    )
    cond_pieces = lax.dynamic_update_slice_in_dim(
        jnp.zeros((seqs, D), F32), cond_part, grid.row * row_width, 1
    )
    cond_pieces = (
        cond_pieces.reshape(rows, seq_rows, cols, col_width)
        .transpose(0, 2, 1, 3)
        .reshape(devices, seq_rows, col_width)
    )
    grad_cond_act = all_exchange(cond_pieces).sum(0)
    _, silu_pull = jax.vjp(silu_fn, condition.astype(F32))
    condition_grad = silu_pull(grad_cond_act)[0]
    return (
        layer_out,
        tokens_grad,
        condition_grad,
        mod_part_grad,
        mod_bias_grad,
        qkv_part,
        qv_bias_grad,
        out_part,
        out_bias_grad,
        fc1_part,
        fc1_bias_grad,
        fc2_part,
        fc2_bias_grad,
    )


def solution(mesh):
    return jax.shard_map(
        per_device,
        mesh=mesh,
        in_specs=(
            P(("row", "col"), None),
            P("row", "col"),
            P("row", None, "col"),
            P(None, "col"),
            P("row", "col", None),
            P("col", None),
            P("col", None, "row"),
            P("col"),
            P("row", "col"),
            P("col"),
            P("col", "row"),
            P("col"),
            P(("row", "col"), None),
        ),
        out_specs=(
            P(("row", "col"), None),
            P(("row", "col"), None),
            P("row", "col"),
            P("row", None, "col"),
            P(None, "col"),
            P("row", "col", None),
            P("col", None),
            P("col", None, "row"),
            P("col"),
            P("row", "col"),
            P("col"),
            P("col", "row"),
            P("col"),
        ),
        check_vma=False,
    )
```

```python
import functools
import math

import jax
import jax.numpy as jnp
from jax import lax
from jax.experimental import pallas as pl
from jax.experimental.pallas import tpu as pltpu
from jax.sharding import PartitionSpec as P

D = 1024
HD = 64
LEN = 1024
PAIR = 2 * HD

EPSILON = 1e-06
PRECISE = lax.Precision.HIGHEST
NN = (((1,), (0,)), ((), ()))
NT = (((1,), (1,)), ((), ()))
TN = (((0,), (0,)), ((), ()))
F32 = jnp.float32
BF16 = jnp.bfloat16
QUERY_ROWS = 512
VMEM_BYTES = 56 * 1024 * 1024
SMALL_COST = pl.CostEstimate(flops=1000, bytes_accessed=1000, transcendentals=0)


def dot(left, right, dims=NN):
    return lax.dot_general(left, right, dims, preferred_element_type=F32)


def silu_fn(values):
    return values * jax.nn.sigmoid(values)


def gelu_both(values):
    c = math.sqrt(2.0 / math.pi)
    square = values * values
    half = 0.5 + 0.5 * jnp.tanh(values * (c + (c * 0.044715) * square))
    gelu = values * half
    slope = half + gelu * (1.0 - half) * (2.0 * c + (6.0 * c * 0.044715) * square)
    return gelu, slope


def normalize(resid):
    average = jnp.mean(resid, 1, keepdims=True)
    spread = jnp.mean(resid * resid, 1, keepdims=True) - average * average
    inv_std = lax.rsqrt(spread + EPSILON)
    return ((resid - average) * inv_std, inv_std)


def normalize_back(grad_norm, normed, inv_std):
    average = jnp.mean(grad_norm, 1, keepdims=True)
    crossed = jnp.mean(grad_norm * normed, 1, keepdims=True)
    return inv_std * (grad_norm - average - normed * crossed)


def after(array, *earlier):
    return lax.optimization_barrier((array, *earlier))[0]


def head_lanes(shape, head):
    lane = lax.broadcasted_iota(jnp.int32, shape, 1)
    return lane < HD if head == 0 else lane >= HD


def attend_kernel(q_ref, k_ref, v_ref, *refs):
    mixed_ref, log_ref = refs[-2:]
    queries = q_ref[...] * jnp.asarray(HD**-0.5, BF16)
    key_rows = k_ref[...]
    values_across = v_ref[...].T
    mask = head_lanes(key_rows.shape, 0)
    zero = jnp.zeros_like(key_rows)
    keys = (jnp.where(mask, key_rows, zero), jnp.where(mask, zero, key_rows))
    length = queries.shape[0]
    for start in range(0, length, QUERY_ROWS):
        stop = start + QUERY_ROWS
        q_part = queries[start:stop]
        outs = []
        for head in range(2):
            scores = dot(keys[head], q_part, NT)
            top = jnp.max(scores, 0, keepdims=True)
            expon = jnp.exp(scores - top)
            total = jnp.sum(expon, 0, keepdims=True)
            out = dot(values_across[head * HD : (head + 1) * HD], expon.astype(BF16))
            outs.append(out / total)
            log_ref[0, 0, head : head + 1, start:stop] = top + jnp.log(total)
        mixed_ref[start:stop, :] = jnp.concatenate(outs, 0).T.astype(BF16)


def attend_back_kernel(q_ref, k_ref, v_ref, mixed_ref, grad_ref, log_ref, out_ref, sums_ref):
    scale = jnp.asarray(HD**-0.5, BF16)
    queries = q_ref[...] * scale
    key_rows = k_ref[...]
    value_rows = v_ref[...]
    grad_rows = grad_ref[...]
    mask = head_lanes(value_rows.shape, 0)
    zero = jnp.zeros_like(value_rows)
    keys = (jnp.where(mask, key_rows, zero), jnp.where(mask, zero, key_rows))
    values = (jnp.where(mask, value_rows, zero), jnp.where(mask, zero, value_rows))
    keys_across = (key_rows * scale).T
    product = grad_rows.astype(F32) * mixed_ref[...].astype(F32)
    picks = (
        lax.broadcasted_iota(jnp.int32, (8, PAIR), 0)
        == lax.broadcasted_iota(jnp.int32, (8, PAIR), 1) // HD
    ).astype(F32)
    inner = lax.dot_general(picks, product, NT, precision=PRECISE, preferred_element_type=F32)
    length = queries.shape[0]
    grad_k = [None, None]
    grad_v = [None, None]
    for start in range(0, length, QUERY_ROWS):
        stop = start + QUERY_ROWS
        q_part = queries[start:stop]
        g_part = grad_rows[start:stop]
        outs = []
        for head in range(2):
            scores = dot(keys[head], q_part, NT)
            probs = jnp.exp(scores - log_ref[0, 0, head : head + 1, start:stop])
            grad_probs = dot(values[head], g_part, NT)
            grad_scores = (probs * (grad_probs - inner[head : head + 1, start:stop])).astype(BF16)
            part_v = dot(probs.astype(BF16), g_part)
            part_k = dot(grad_scores, q_part)
            grad_v[head] = part_v if grad_v[head] is None else grad_v[head] + part_v
            grad_k[head] = part_k if grad_k[head] is None else grad_k[head] + part_k
            outs.append(dot(keys_across[head * HD : (head + 1) * HD], grad_scores))
        out_ref[start:stop, 0:PAIR] = jnp.concatenate(outs, 0).T.astype(BF16)
    out_ref[:, PAIR : 2 * PAIR] = jnp.where(mask, grad_k[0], grad_k[1]).astype(BF16)
    out_ref[:, 2 * PAIR :] = jnp.where(mask, grad_v[0], grad_v[1]).astype(BF16)
    sums_ref[0, 0] = jnp.sum(out_ref[...].astype(F32).reshape(length // 8, 8, 3 * PAIR), 0)


def attention_specs(first):
    part = lambda offset: pl.BlockSpec((LEN, PAIR), lambda s, p: (s, 3 * (p + first) + offset))
    plain = pl.BlockSpec((LEN, PAIR), lambda s, p: (s, p + first))
    logs = pl.BlockSpec((1, 1, 2, LEN), lambda s, p: (s, p + first, 0, 0))
    return [part(0), part(1), part(2)], plain, logs


def attend(projected, latents, pairs, first, count, earlier=()):
    parts, plain, logs = attention_specs(first)
    rows = projected.shape[0]
    return pl.pallas_call(
        attend_kernel,
        grid=(latents, count),
        in_specs=parts + [pl.BlockSpec(memory_space=pl.ANY)] * len(earlier),
        out_specs=[plain, logs],
        out_shape=[
            jax.ShapeDtypeStruct((rows, pairs * PAIR), BF16),
            jax.ShapeDtypeStruct((latents, pairs, 2, LEN), F32),
        ],
        input_output_aliases={3 + i: i for i in range(len(earlier))},
        compiler_params=pltpu.CompilerParams(vmem_limit_bytes=VMEM_BYTES),
        cost_estimate=SMALL_COST,
        name="attend",
    )(projected, projected, projected, *earlier)


def attend_back(projected, mixed, grad_mixed, log_totals, latents, first, count):
    parts, plain, logs = attention_specs(first)
    rows = projected.shape[0]
    return pl.pallas_call(
        attend_back_kernel,
        grid=(latents, count),
        in_specs=[*parts, plain, plain, logs],
        out_specs=[
            pl.BlockSpec((LEN, 3 * PAIR), lambda s, p: (s, p)),
            pl.BlockSpec((1, 1, 8, 3 * PAIR), lambda s, p: (s, p, 0, 0)),
        ],
        out_shape=[
            jax.ShapeDtypeStruct((rows, count * 3 * PAIR), BF16),
            jax.ShapeDtypeStruct((latents, count, 8, 3 * PAIR), F32),
        ],
        compiler_params=pltpu.CompilerParams(vmem_limit_bytes=VMEM_BYTES),
        cost_estimate=SMALL_COST,
        name="attend_back",
    )(projected, projected, projected, mixed, grad_mixed, log_totals)


def kernel_call(body, grid, in_specs, out_specs, out_shape, name):
    return pl.pallas_call(
        body,
        grid=grid,
        in_specs=in_specs,
        out_specs=out_specs,
        out_shape=out_shape,
        compiler_params=pltpu.CompilerParams(vmem_limit_bytes=VMEM_BYTES),
        cost_estimate=SMALL_COST,
        name=name,
    )


def whole(array):
    return pl.BlockSpec(array.shape, lambda *step: (0,) * array.ndim)


def row_specs(local_rows, tile, width):
    count = local_rows // tile
    mine = pl.BlockSpec((tile, width), lambda i: (jnp.minimum(i, count - 1), 0))
    theirs = pl.BlockSpec((tile, width), lambda i: (jnp.maximum(i - count, 0), 0))
    return count, mine, theirs


def rows_product(pair, weights, extra, kind):
    local_rows, depth = pair[0].shape
    tile = min(512, local_rows)
    count, mine, theirs = row_specs(local_rows, tile, depth)
    widths = [w.shape[1] for w in weights]
    width = sum(widths)
    total = 2 * local_rows

    def body(*refs):
        mine_ref, theirs_ref = refs[:2]
        weight_refs = refs[2 : 2 + len(weights)]
        extra_ref = refs[2 + len(weights)]
        out_refs = refs[3 + len(weights) :]
        step = pl.program_id(0)
        left = jnp.where(step < count, mine_ref[...], theirs_ref[...])
        if kind == "slope":

            @pl.when(step == 0)
            def _():
                out_refs[1][...] = jnp.zeros(out_refs[1].shape, F32)

        start = 0
        for ref, span in zip(weight_refs, widths):
            for low in range(0, span, 256):
                cols = slice(start + low, start + low + 256)
                product = dot(left, ref[:, low : low + 256])
                if kind == "bias":
                    out_refs[0][:, cols] = (product + extra_ref[:, cols]).astype(BF16)
                elif kind == "gelu":
                    act, slope = gelu_both(product + extra_ref[:, cols])
                    out_refs[0][:, cols] = act.astype(BF16)
                    out_refs[1][:, cols] = slope.astype(BF16)
                else:
                    grad = (product * extra_ref[:, cols].astype(F32)).astype(BF16)
                    out_refs[0][:, cols] = grad
                    out_refs[1][:, cols] += jnp.sum(
                        grad.astype(F32).reshape(tile // 8, 8, 256), 0
                    )
            start += span

    rows_out = pl.BlockSpec((tile, width), lambda i: (i, 0))
    low_shape = jax.ShapeDtypeStruct((total, width), BF16)
    if kind == "bias":
        out_specs, out_shape = [rows_out], [low_shape]
    elif kind == "gelu":
        out_specs, out_shape = [rows_out, rows_out], [low_shape, low_shape]
    else:
        out_specs = [rows_out, pl.BlockSpec((8, width), lambda i: (0, 0))]
        out_shape = [low_shape, jax.ShapeDtypeStruct((8, width), F32)]
    extra_spec = rows_out if kind == "slope" else whole(extra)
    return kernel_call(
        body,
        (2 * count,),
        [mine, theirs, *[whole(w) for w in weights], extra_spec],
        out_specs,
        out_shape,
        "rows_" + kind,
    )(*pair, *weights, extra)


def columns_of(refs, start, stop):
    for ref in refs:
        if start < ref.shape[1]:
            return ref[:, start:stop]
        start, stop = start - ref.shape[1], stop - ref.shape[1]


def rows_total(lefts, weights):
    local_rows = lefts[0].shape[0] // 2
    tile = min(512, local_rows)
    count = local_rows // tile
    width = weights[0].shape[0]
    ends = set()
    for arrays in (lefts, weights):
        end = 0
        for array in arrays:
            end += array.shape[1]
            ends.add(end)
    ends = sorted(ends)

    def body(*refs):
        left_refs = refs[: len(lefts)]
        weight_refs = refs[len(lefts) : -2]
        mine_ref, theirs_ref = refs[-2:]
        total = None
        for start, stop in zip([0] + ends, ends):
            part = dot(columns_of(left_refs, start, stop), columns_of(weight_refs, start, stop), NT)
            total = part if total is None else total + part
        step = pl.program_id(0)

        @pl.when(step < count)
        def _():
            mine_ref[...] = total

        @pl.when(step >= count)
        def _():
            theirs_ref[...] = total.astype(BF16)

    return kernel_call(
        body,
        (2 * count,),
        [pl.BlockSpec((tile, a.shape[1]), lambda i: (i, 0)) for a in lefts]
        + [whole(w) for w in weights],
        [
            pl.BlockSpec((tile, width), lambda i: (jnp.minimum(i, count - 1), 0)),
            pl.BlockSpec((tile, width), lambda i: (jnp.maximum(i - count, 0), 0)),
        ],
        [
            jax.ShapeDtypeStruct((local_rows, width), F32),
            jax.ShapeDtypeStruct((local_rows, width), BF16),
        ],
        "rows_total",
    )(*lefts, *weights)


def token_kernel(body, arrays, rows_of, out_types, sums, name):
    tokens = arrays[0].shape[0]
    tile = min(256, tokens)
    outs = len(out_types)

    def kernel(*refs):
        values = [ref[...].astype(F32) for ref in refs[: len(arrays)]]
        rows_ref = refs[len(arrays)]
        rows = [rows_ref[i : i + 1, :] for i in range(8)]
        results, columns = body(values, rows)
        out_refs = refs[len(arrays) + 1 :]
        for ref, result in zip(out_refs, results):
            ref[...] = result.astype(ref.dtype)
        if sums:
            sum_ref = out_refs[outs]

            @pl.when(pl.program_id(0) == 0)
            def _():
                sum_ref[...] = jnp.zeros(sum_ref.shape, F32)

            for i, column in enumerate(columns):
                sum_ref[i] += jnp.sum(column.reshape(tile // 8, 8, D), 0)

    tokens_spec = pl.BlockSpec((tile, D), lambda i: (i, 0))
    out_specs = [tokens_spec] * outs
    out_shape = [jax.ShapeDtypeStruct((tokens, D), t) for t in out_types]
    if sums:
        out_specs = out_specs + [pl.BlockSpec((sums, 8, D), lambda i: (0, 0, 0))]
        out_shape = out_shape + [jax.ShapeDtypeStruct((sums, 8, D), F32)]
    return kernel_call(
        kernel,
        (tokens // tile,),
        [tokens_spec] * len(arrays) + [whole(rows_of)],
        out_specs,
        out_shape,
        name,
    )(*arrays, rows_of)


def middle_body(values, rows):
    mine, theirs, tokens = values
    gate, shift, scale, bias = rows[2], rows[3], rows[4], rows[6]
    attention_out = mine + theirs + bias
    normed, _ = normalize(tokens + gate * attention_out)
    return [attention_out, normed * (1.0 + scale) + shift], []


def middle_back_body(values, rows):
    mine, theirs, upstream, tokens, attention_out = values
    gate, scale = rows[2], rows[4]
    grad_hidden = mine + theirs
    normed, inv_std = normalize(tokens + gate * attention_out)
    grad = upstream + normalize_back(grad_hidden * (1.0 + scale), normed, inv_std)
    grad_attention = grad * gate
    return [grad, grad_attention], [
        grad_hidden,
        grad_hidden * normed,
        grad * attention_out,
        grad_attention,
    ]


def first_back_body(values, rows):
    mine, theirs, tokens, grad_resid = values
    scale = rows[1]
    grad_hidden = mine + theirs
    normed, inv_std = normalize(tokens)
    grad = grad_resid + normalize_back(grad_hidden * (1.0 + scale), normed, inv_std)
    return [grad], [grad_hidden, grad_hidden * normed]


def last_body(values, rows):
    mine, theirs, tokens, attention_out, upstream = values
    gate_attn, gate_feed, bias = rows[2], rows[5], rows[7]
    feed_out = mine + theirs + bias
    resid_mid = tokens + gate_attn * attention_out
    return [resid_mid + gate_feed * feed_out], [upstream * feed_out, upstream * gate_feed]


def columns_product(pair, right, added, cuts):
    local_rows, depth = pair[0].shape
    width = right.shape[1]
    tile = 256
    starts = [sum(cuts[:i]) for i in range(len(cuts))]
    add_width = width // max(1, len(added))

    def body(mine_ref, theirs_ref, right_ref, *refs):
        add_refs = refs[: len(added)]
        out_refs = refs[len(added) :]
        mine, theirs = mine_ref[...].T, theirs_ref[...].T
        for ref, start, span in zip(out_refs, starts, cuts):
            total = dot(mine, right_ref[:local_rows, start : start + span])
            total = total + dot(theirs, right_ref[local_rows:, start : start + span])
            if added:
                place = start % add_width
                total = total + add_refs[start // add_width][:, place : place + span].astype(F32)
            ref[...] = total.astype(BF16)

    token_spec = pl.BlockSpec((local_rows, tile), lambda i: (0, i))
    outs = kernel_call(
        body,
        (depth // tile,),
        [token_spec, token_spec, whole(right)]
        + [pl.BlockSpec((tile, add_width), lambda i: (i, 0)) for _ in added],
        [pl.BlockSpec((tile, span), lambda i: (i, 0)) for span in cuts],
        [jax.ShapeDtypeStruct((depth, span), BF16) for span in cuts],
        "columns_product",
    )(*pair, right, *added)
    return outs


def assemble(top, low, qkv_width, out_width):
    parts = [top[0], top[2], low[0], low[2]]
    ids = [top[1], top[3], low[1], low[3]]
    half, width = parts[0].shape
    block = qkv_width + out_width
    blocks = 2 * width // block
    tile = 128

    def body(a_ref, b_ref, c_ref, d_ref, qkv_ref, out_ref):
        for number, ref in enumerate((a_ref, b_ref, c_ref, d_ref)):
            for place, i in enumerate(ids[number]):
                start = place * block
                qkv_ref[number // 2, :, i * qkv_width : (i + 1) * qkv_width] = ref[
                    :, start : start + qkv_width
                ]
                out_ref[number // 2, :, i * out_width : (i + 1) * out_width] = ref[
                    :, start + qkv_width : start + block
                ]

    qkv, out = kernel_call(
        body,
        (half // tile,),
        [pl.BlockSpec((tile, width), lambda i: (i, 0))] * 4,
        [
            pl.BlockSpec((2, tile, blocks * qkv_width), lambda i: (0, i, 0)),
            pl.BlockSpec((2, tile, blocks * out_width), lambda i: (0, i, 0)),
        ],
        [
            jax.ShapeDtypeStruct((2, half, blocks * qkv_width), BF16),
            jax.ShapeDtypeStruct((2, half, blocks * out_width), BF16),
        ],
        "assemble",
    )(*parts)
    return qkv.reshape(2 * half, -1), out.reshape(2 * half, -1)


class Grid:
    def __init__(self):
        self.rows = lax.axis_size("row")
        self.cols = lax.axis_size("col")
        self.chips = self.cols // 2
        self.bits = [1 << b for b in range(self.chips.bit_length() - 1)]
        self.orders = (self.bits, self.bits[::-1])
        self.row = lax.axis_index("row")
        self.col = lax.axis_index("col")
        self.core = self.col % 2
        source = lax.iota(jnp.int32, self.chips) ^ (self.col // 2)
        self.choose = (
            (2 * source + self.core)[:, None] == lax.iota(jnp.int32, self.cols)[None, :]
        ).astype(F32)

    def swap(self, array, flip):
        pairs = [(i, i ^ flip) for i in range(self.cols)]
        return lax.ppermute(array, "col", pairs)

    def swap_core(self, array):
        return self.swap(array, 1)

    def swap_chip(self, array, bit):
        return self.swap(array, 2 * bit)

    def to_relative(self, blocks):
        flat = blocks.reshape(self.cols, -1).astype(F32)
        picked = lax.dot_general(
            self.choose, flat, NN, precision=PRECISE, preferred_element_type=F32
        )
        return picked.reshape((self.chips,) + blocks.shape[1:])

    def to_absolute(self, blocks):
        flat = blocks.reshape(self.chips, -1)
        placed = lax.dot_general(
            self.choose, flat, TN, precision=PRECISE, preferred_element_type=F32
        )
        return placed.reshape((self.cols,) + blocks.shape[1:])

    def gather_rows(self, block):
        count = self.rows
        got = [block]
        for step in range(1, count):
            got.append(
                lax.ppermute(block, "row", [(i, (i + step) % count) for i in range(count)])
            )
        stacked = jnp.stack(got)
        ordered = [
            lax.dynamic_index_in_dim(stacked, (self.row - i) % count, 0, keepdims=False)
            for i in range(count)
        ]
        return jnp.concatenate(ordered, 0), got[-1]

    def scatter_rows(self, whole):
        count = self.rows
        blocks = whole.reshape(count, whole.shape[0] // count, whole.shape[1])
        total = lax.dynamic_index_in_dim(blocks, self.row, 0, keepdims=False).astype(F32)
        for step in range(1, count):
            sent = lax.dynamic_index_in_dim(blocks, (self.row + step) % count, 0, keepdims=False)
            total = total + lax.ppermute(
                sent, "row", [(i, (i + step) % count) for i in range(count)]
            ).astype(F32)
        return total

    def gather_early(self, block, order, late=()):
        held, ids = block, [0]
        for bit in order[:-1]:
            got = self.swap_chip(held, bit)
            if bit == order[-2]:
                got = after(got, *late)
            held = jnp.concatenate([held, got], 1)
            ids = ids + [bit ^ i for i in ids]
        return held, ids

    def early_ids(self, order):
        ids = [0]
        for bit in order[:-1]:
            ids = ids + [bit ^ i for i in ids]
        return ids

    def gather_last(self, held, ids, order):
        return self.swap_chip(held, order[-1]), [order[-1] ^ i for i in ids]

    def scatter_chips(self, keep, send, order, late=()):
        for bit in order[-2::-1]:
            got = self.swap_chip(send, bit)
            if bit == order[-2]:
                got = after(got, *late)
            total = keep.astype(F32) + got.astype(F32)
            if bit == order[0]:
                return total
            half = total.shape[1] // 2
            keep, send = total[:, :half], total[:, half:].astype(BF16)


def split_columns(array, ids):
    width = array.shape[1] // len(ids)
    return {i: array[:, n * width : (n + 1) * width] for n, i in enumerate(ids)}


def all_exchange(pieces):
    return lax.all_to_all(pieces, ("row", "col"), 0, 0, tiled=True)


def per_device(
    tokens,
    condition,
    mod_weight,
    mod_bias,
    qkv_weight,
    qv_bias,
    out_weight,
    out_bias,
    fc1_weight,
    fc1_bias,
    fc2_weight,
    fc2_bias,
    cotangent,
):
    grid = Grid()
    rows, cols, chips = grid.rows, grid.cols, grid.chips
    devices = rows * cols
    local_rows = tokens.shape[0]
    both_rows = 2 * local_rows
    latents = both_rows // LEN
    span = LEN // local_rows
    seq_rows = condition.shape[0]
    seqs = seq_rows * rows
    row_width = D // rows
    col_width = D // cols
    local_heads = qkv_weight.shape[1]
    local_units = fc1_weight.shape[1]
    plane_heads = local_heads * chips
    pairs = plane_heads // 2
    qkv_width = local_heads * 3 * HD
    out_width = local_heads * HD

    if local_heads % 2 == 0:
        qkv_local = (
            qkv_weight.reshape(row_width, local_heads // 2, 2, 3, HD)
            .transpose(0, 1, 3, 2, 4)
            .reshape(row_width, qkv_width)
        )
    else:
        qkv_local = qkv_weight.reshape(row_width, qkv_width)
    attn_local = jnp.concatenate(
        [qkv_local, out_weight.reshape(out_width, row_width).T], 1
    )
    attn_width = qkv_width + out_width
    fc1_local = fc1_weight
    fc2_local = fc2_weight.T

    small = jnp.concatenate(
        [
            condition.reshape(-1),
            fc1_bias,
            qv_bias.reshape(-1),
            out_bias,
            fc2_bias,
        ]
    )
    small_all = all_exchange(
        jnp.broadcast_to(small.reshape(1, -1, 128), (devices, small.size // 128, 128))
    ).reshape(rows, cols, -1)
    cut = seq_rows * col_width
    cond_all = (
        small_all[:, :, :cut]
        .reshape(rows, cols, seq_rows, col_width)
        .transpose(0, 2, 1, 3)
        .reshape(seqs, D)
    )
    biases = small_all[0, :, cut:]
    fc1_bias_all = biases[:, :local_units]
    qv_bias_all = biases[:, local_units : local_units + local_heads * PAIR]
    out_bias_all = biases[:, -2 * col_width : -col_width].reshape(1, D).astype(F32)
    fc2_bias_all = biases[:, -col_width:].reshape(1, D).astype(F32)

    cond_act = silu_fn(cond_all.astype(F32)).astype(BF16)
    cond_act = lax.dynamic_slice_in_dim(cond_act, grid.row * row_width, row_width, 1)
    mod_flat = mod_weight.reshape(row_width, 6 * col_width)
    own_bias = jnp.where(grid.row == 0, mod_bias.astype(F32), 0.0)
    mod_part = dot(cond_act, mod_flat).reshape(seqs, 6, col_width) + own_bias
    mod_part = jnp.broadcast_to(
        mod_part[:, None], (seqs, span, 6, col_width)
    ).reshape(devices, 6, col_width)
    modulation = (
        all_exchange(mod_part)
        .reshape(rows, cols, 6, col_width)
        .sum(0)
        .transpose(1, 0, 2)
        .reshape(6, 1, D)
    )
    shift_attn, scale_attn, gate_attn, shift_feed, scale_feed, gate_feed = modulation
    token_rows = jnp.concatenate([modulation.reshape(6, D), out_bias_all, fc2_bias_all], 0)

    attn_rows, mark = grid.gather_rows(attn_local)
    fc1_rows = lax.all_gather(after(fc1_local, mark), "row", axis=0, tiled=True)
    fc2_rows = lax.all_gather(after(fc2_local, fc1_rows), "row", axis=0, tiled=True)
    half = D // 2
    top = grid.gather_early(attn_rows[:half], grid.orders[0])
    low = grid.gather_early(attn_rows[half:], grid.orders[1])
    top = top + grid.gather_last(*top, grid.orders[0])
    low = low + grid.gather_last(*low, grid.orders[1])
    if local_heads % 2 == 0:
        qkv_w, out_w = assemble(top, low, qkv_width, out_width)
    else:
        attn_top = {**split_columns(top[0], top[1]), **split_columns(top[2], top[3])}
        attn_low = {**split_columns(low[0], low[1]), **split_columns(low[2], low[3])}
        attn_blocks = [jnp.concatenate([attn_top[i], attn_low[i]], 0) for i in range(chips)]
        qkv_w = (
            jnp.stack([b[:, :qkv_width] for b in attn_blocks], 1)
            .reshape(D, pairs, 2, 3, HD)
            .transpose(0, 1, 3, 2, 4)
            .reshape(D, pairs * 3 * PAIR)
        )
        out_w = jnp.concatenate([b[:, qkv_width:] for b in attn_blocks], 1)

    middle = local_units // 2

    def units_early(rows_held, earlier, late):
        rows_held = after(rows_held, *earlier)
        parts = (rows_held[:, :middle], rows_held[:, middle:])
        held = [grid.gather_early(p, order, late) for p, order in zip(parts, grid.orders)]
        return [h[0] for h in held], [h[1] for h in held]

    def units_last(held, ids, *earlier):
        got = [
            grid.gather_last(after(h, *earlier), i, order)
            for h, i, order in zip(held, ids, grid.orders)
        ]
        return [g[0] for g in got], [g[1] for g in got]

    ids_a = [grid.early_ids(order) for order in grid.orders]
    fc1_bias_rel = grid.to_relative(fc1_bias_all).reshape(chips, 2, local_units // 2)
    ids_b = [[order[-1] ^ i for i in ids] for ids, order in zip(ids_a, grid.orders)]
    unit_ids = (ids_a, ids_b)
    fc1_bias_groups = [
        jnp.concatenate([fc1_bias_rel[i, part] for part in range(2) for i in ids[part]])[None]
        for ids in unit_ids
    ]
    qv_rel = grid.to_relative(qv_bias_all).reshape(pairs, 2, 2, HD).transpose(0, 2, 1, 3)
    qkv_bias_rel = jnp.concatenate(
        [qv_rel[:, :1], jnp.zeros_like(qv_rel[:, :1]), qv_rel[:, 1:]], 1
    ).reshape(1, pairs * 3 * PAIR)

    def both(mine):
        return (mine, grid.swap_core(mine))

    def own_total(lefts, weights):
        mine, theirs = rows_total(lefts, weights)
        return mine, grid.swap_core(theirs)

    def send_units(left, right):
        width = right.shape[1]
        sent = columns_product(left, right, [], [width // 2] * 2)
        got = [grid.swap_chip(a, order[-1]) for a, order in zip(sent, grid.orders)]
        return got, sent[0]

    def sum_chips(kept, late):
        sums = [
            grid.scatter_chips(kept[2 * n], kept[2 * n + 1], order, late)
            for n, order in enumerate(grid.orders)
        ]
        return jnp.concatenate(sums, 1).astype(BF16)

    def sum_rows(parts):
        return lax.psum_scatter(parts, "row", scatter_dimension=0, tiled=True)

    resid = tokens.astype(F32)
    normed_attn, _ = normalize(resid)
    hidden_attn = both((normed_attn * (1.0 + scale_attn) + shift_attn).astype(BF16))
    grad_feed_low = both((cotangent.astype(F32) * gate_feed).astype(BF16))

    (projected,) = rows_product(hidden_attn, [qkv_w], qkv_bias_rel, "bias")
    fc1_a, _ = units_early(fc1_rows, (top[2], low[2]), (projected,))
    fc1_b, _ = units_last(fc1_a, ids_a)
    projected = after(projected, *fc1_a)
    middle_pair = pairs // 2
    first_half = attend(projected, latents, pairs, 0, middle_pair)
    fc2_a, _ = units_early(fc2_rows, (first_half[0], *fc1_b), ())
    mixed, log_totals = attend(
        after(projected, first_half[0], *fc1_b),
        latents,
        pairs,
        middle_pair,
        pairs - middle_pair,
        first_half,
    )
    fc2_b, _ = units_last(fc2_a, ids_a, mixed)
    mixed = after(mixed, *fc2_a)
    totals = own_total([mixed], [out_w])
    attention_out, hidden_feed = token_kernel(
        middle_body, [*totals, tokens], token_rows, [F32, BF16], 0, "middle"
    )
    hidden_feed = both(hidden_feed)
    act_a, slope_a = rows_product(hidden_feed, fc1_a, fc1_bias_groups[0], "gelu")
    act_b, slope_b = rows_product(
        (after(hidden_feed[0], act_a), hidden_feed[1]), fc1_b, fc1_bias_groups[1], "gelu"
    )
    act_b = after(act_b, *fc2_b)

    fc2_got, _ = send_units(grad_feed_low, act_b)
    grad_a, bias_a = rows_product(
        (after(grad_feed_low[0], act_b), grad_feed_low[1]), fc2_a, slope_a, "slope"
    )
    grad_b, bias_b = rows_product(
        (after(grad_feed_low[0], grad_a), grad_feed_low[1]), fc2_b, slope_b, "slope"
    )
    bias_fc1 = [bias_a, bias_b]
    grad_b = after(grad_b, *fc2_got)
    totals = own_total([grad_a, grad_b], fc1_a + fc1_b)
    fc1_got, sent = send_units(hidden_feed, after(grad_b, totals[0]))
    grad_resid_mid, grad_attention_low, middle_sums = token_kernel(
        middle_back_body,
        [after(totals[0], sent), totals[1], cotangent, tokens, attention_out],
        token_rows,
        [F32, BF16],
        4,
        "middle_back",
    )
    grad_attention_low = both(grad_attention_low)
    fc2_kept = columns_product(
        grad_feed_low, after(act_a, grad_attention_low[0]), fc2_got, [act_a.shape[1] // 4] * 4
    )

    (grad_mixed,) = rows_product(
        grad_attention_low, [out_w], jnp.zeros((1, out_w.shape[1]), F32), "bias"
    )
    fc1_kept = columns_product(
        hidden_feed, after(grad_a, grad_mixed), fc1_got, [grad_a.shape[1] // 4] * 4
    )
    (grad_out,) = columns_product(
        grad_attention_low, after(mixed, grad_mixed), [], [mixed.shape[1]]
    )
    grad_mixed = after(grad_mixed, grad_out, fc1_kept[0])
    grad_late, bias_late = attend_back(
        projected, mixed, grad_mixed, log_totals, latents, 1, pairs - 1
    )
    fc2_sums = sum_chips(fc2_kept, (grad_late,))
    fc1_sums = sum_chips(fc1_kept, (grad_late,))
    late_chips = chips * (pairs - 1) // pairs
    qkv_late = columns_product(hidden_attn, grad_late, [], [qkv_width] * late_chips) if (
        local_heads % 2 == 0
    ) else None
    early_input = after(grad_mixed, grad_late, fc2_sums, fc1_sums)
    grad_early, bias_early = attend_back(
        projected, mixed, early_input, log_totals, latents, 0, 1
    )
    fc2_part = sum_rows(fc2_sums)
    fc1_part = sum_rows(fc1_sums)
    bias_qkv = jnp.concatenate([bias_early, bias_late], 1).sum((0, 2))
    if local_heads % 2 == 0:
        qkv_early = columns_product(hidden_attn, grad_early, [], [qkv_width])
        grad_qkv = [*qkv_early, *qkv_late]
    else:
        grad_projected = jnp.concatenate([grad_early, grad_late], 1)
        (grad_qkv,) = columns_product(hidden_attn, grad_projected, [], [3 * PAIR * pairs])
        grad_qkv = (
            grad_qkv.reshape(D, pairs, 3, 2, HD).transpose(0, 1, 3, 2, 4).reshape(D, chips, qkv_width)
        )
        grad_qkv = [grad_qkv[:, i] for i in range(chips)]

    def pick(part, ids):
        lines = slice(0, half) if part == 0 else slice(half, D)
        return jnp.concatenate(
            [
                array
                for i in ids
                for array in (
                    grad_qkv[i][lines],
                    grad_out[lines, i * out_width : (i + 1) * out_width],
                )
            ],
            1,
        )

    attn_got = [
        grid.swap_chip(pick(number, gathered[3]), grid.orders[number][-1])
        for number, gathered in enumerate((top, low))
    ]
    attn_sums = []
    for number, gathered in enumerate((top, low)):
        order = grid.orders[number]
        kept = pick(number, gathered[1]).astype(F32) + attn_got[number].astype(F32)
        middle = kept.shape[1] // 2
        attn_sums.append(
            grid.scatter_chips(kept[:, :middle], kept[:, middle:].astype(BF16), order)
        )
    attn_part = grid.scatter_rows(jnp.concatenate(attn_sums, 0).astype(BF16))
    qkv_part = attn_part[:, :qkv_width]
    if local_heads % 2 == 0:
        qkv_part = qkv_part.reshape(row_width, local_heads // 2, 3, 2, HD).transpose(0, 1, 3, 2, 4)
    qkv_part = qkv_part.reshape(row_width, local_heads, 3 * HD)
    out_part = attn_part[:, qkv_width:].T.reshape(local_heads, HD, row_width)

    totals = own_total([after(grad_early, *attn_got), grad_late], [qkv_w])
    tokens_grad, first_sums = token_kernel(
        first_back_body, [*totals, tokens, grad_resid_mid], token_rows, [F32], 2, "first_back"
    )
    totals = own_total([after(act_a, totals[0], fc2_part, *attn_sums), act_b], fc2_a + fc2_b)
    layer_out, last_sums = token_kernel(
        last_body, [after(totals[0], fc1_part), totals[1], tokens, attention_out, cotangent], token_rows, [BF16], 2, "last"
    )

    first_sums, middle_sums, last_sums = (
        sums.sum(1) for sums in (first_sums, middle_sums, last_sums)
    )
    mod_rows = jnp.concatenate(
        [first_sums, middle_sums[2:3], middle_sums[:2], last_sums[:1], middle_sums[3:], last_sums[1:]]
    )
    mod_rows = mod_rows.reshape(8, cols, col_width).transpose(1, 0, 2)
    bias_fc1 = [b.sum(0, keepdims=True) for b in bias_fc1]
    first_half, second_half = {}, {}
    for sums, ids in zip(bias_fc1, unit_ids):
        middle = sums.shape[1] // 2
        first_half.update(split_columns(sums[:, :middle], ids[0]))
        second_half.update(split_columns(sums[:, middle:], ids[1]))
    fc1_rel = jnp.concatenate(
        [jnp.concatenate([first_half[i], second_half[i]], 1) for i in range(chips)], 0
    )
    qkv_rel = bias_qkv.reshape(pairs, 3, 2, HD)
    qv_rel = jnp.stack([qkv_rel[:, 0], qkv_rel[:, 2]], 2).reshape(chips, local_heads * PAIR)
    hidden_rows = grid.to_absolute(jnp.concatenate([fc1_rel, qv_rel], 1)).reshape(
        cols, -1, col_width
    )
    pieces = jnp.concatenate([mod_rows, hidden_rows], 1)
    pieces = jnp.broadcast_to(pieces[None], (rows,) + pieces.shape).reshape(
        devices, -1, col_width
    )
    arrived = all_exchange(pieces)
    grad_modulation = arrived[:, :6].reshape(seqs, span, 6, col_width).sum(1)
    sums = arrived[:, 6:].sum(0)
    out_bias_grad = sums[0]
    fc2_bias_grad = sums[1]
    hidden_sums = sums[2:].reshape(-1)
    fc1_bias_grad = hidden_sums[:local_units]
    qv_bias_grad = hidden_sums[local_units:].reshape(local_heads, PAIR)
    mod_bias_grad = jnp.sum(grad_modulation, 0)
    grad_mod_flat = grad_modulation.reshape(seqs, 6 * col_width)
    mod_part_grad = lax.dot_general(
        cond_act.astype(F32), grad_mod_flat, TN, precision=PRECISE, preferred_element_type=F32
    ).reshape(row_width, 6, col_width)
    cond_part = lax.dot_general(
        grad_mod_flat,
        mod_flat.astype(F32),
        NT,
        precision=PRECISE,
        preferred_element_type=F32,
    )
    cond_pieces = lax.dynamic_update_slice_in_dim(
        jnp.zeros((seqs, D), F32), cond_part, grid.row * row_width, 1
    )
    cond_pieces = (
        cond_pieces.reshape(rows, seq_rows, cols, col_width)
        .transpose(0, 2, 1, 3)
        .reshape(devices, seq_rows, col_width)
    )
    grad_cond_act = all_exchange(cond_pieces).sum(0)
    _, silu_pull = jax.vjp(silu_fn, condition.astype(F32))
    condition_grad = silu_pull(grad_cond_act)[0]
    return (
        layer_out,
        tokens_grad,
        condition_grad,
        mod_part_grad,
        mod_bias_grad,
        qkv_part,
        qv_bias_grad,
        out_part,
        out_bias_grad,
        fc1_part.astype(F32),
        fc1_bias_grad,
        fc2_part.astype(F32).T,
        fc2_bias_grad,
    )


def solution(mesh):
    return jax.shard_map(
        per_device,
        mesh=mesh,
        in_specs=(
            P(("row", "col"), None),
            P("row", "col"),
            P("row", None, "col"),
            P(None, "col"),
            P("row", "col", None),
            P("col", None),
            P("col", None, "row"),
            P("col"),
            P("row", "col"),
            P("col"),
            P("col", "row"),
            P("col"),
            P(("row", "col"), None),
        ),
        out_specs=(
            P(("row", "col"), None),
            P(("row", "col"), None),
            P("row", "col"),
            P("row", None, "col"),
            P(None, "col"),
            P("row", "col", None),
            P("col", None),
            P("col", None, "row"),
            P("col"),
            P("row", "col"),
            P("col"),
            P("col", "row"),
            P("col"),
        ),
        check_vma=False,
    )
```

```python
import functools
import math

import jax
import jax.numpy as jnp
from jax import lax
from jax.experimental import pallas as pl
from jax.experimental.pallas import tpu as pltpu
from jax.sharding import PartitionSpec as P

D = 1024
HD = 64
LEN = 1024
PAIR = 2 * HD

EPSILON = 1e-06
PRECISE = lax.Precision.HIGHEST
NN = (((1,), (0,)), ((), ()))
NT = (((1,), (1,)), ((), ()))
TN = (((0,), (0,)), ((), ()))
F32 = jnp.float32
BF16 = jnp.bfloat16
QUERY_ROWS = 512
TOKEN_ROWS = 32
VMEM_BYTES = 40 * 1024 * 1024
SMALL_COST = pl.CostEstimate(flops=1000, bytes_accessed=1000, transcendentals=0)


def dot(left, right, dims=NN):
    return lax.dot_general(left, right, dims, preferred_element_type=F32)


def silu_fn(values):
    return values * jax.nn.sigmoid(values)


def gelu_both(values):
    c = math.sqrt(2.0 / math.pi)
    square = values * values
    half = 0.5 + 0.5 * jnp.tanh(values * (c + (c * 0.044715) * square))
    gelu = values * half
    slope = half + gelu * (1.0 - half) * (2.0 * c + (6.0 * c * 0.044715) * square)
    return gelu, slope


def normalize(resid):
    average = jnp.mean(resid, 1, keepdims=True)
    spread = jnp.mean(resid * resid, 1, keepdims=True) - average * average
    inv_std = lax.rsqrt(spread + EPSILON)
    return ((resid - average) * inv_std, inv_std)


def normalize_back(grad_norm, normed, inv_std):
    average = jnp.mean(grad_norm, 1, keepdims=True)
    crossed = jnp.mean(grad_norm * normed, 1, keepdims=True)
    return inv_std * (grad_norm - average - normed * crossed)


def after(array, *earlier):
    return lax.optimization_barrier((array, *earlier))[0]


def head_lanes(shape, head):
    lane = lax.broadcasted_iota(jnp.int32, shape, 1)
    return lane < HD if head == 0 else lane >= HD


def attend_kernel(q_ref, k_ref, v_ref, *refs):
    mixed_ref, log_ref = refs[-2:]
    queries = q_ref[...] * jnp.asarray(HD**-0.5, BF16)
    key_rows = k_ref[...]
    values_across = v_ref[...].T
    mask = head_lanes(key_rows.shape, 0)
    zero = jnp.zeros_like(key_rows)
    keys = (jnp.where(mask, key_rows, zero), jnp.where(mask, zero, key_rows))
    length = queries.shape[0]
    for start in range(0, length, QUERY_ROWS):
        stop = start + QUERY_ROWS
        q_part = queries[start:stop]
        outs = []
        for head in range(2):
            scores = dot(keys[head], q_part, NT)
            top = jnp.max(scores, 0, keepdims=True)
            expon = jnp.exp(scores - top)
            total = jnp.sum(expon, 0, keepdims=True)
            out = dot(values_across[head * HD : (head + 1) * HD], expon.astype(BF16))
            outs.append(out / total)
            log_ref[0, 0, head : head + 1, start:stop] = top + jnp.log(total)
        mixed_ref[start:stop, :] = jnp.concatenate(outs, 0).T.astype(BF16)


def attend_back_kernel(q_ref, k_ref, v_ref, mixed_ref, grad_ref, log_ref, out_ref, sums_ref):
    scale = jnp.asarray(HD**-0.5, BF16)
    queries = q_ref[...] * scale
    key_rows = k_ref[...]
    value_rows = v_ref[...]
    grad_rows = grad_ref[...]
    mask = head_lanes(value_rows.shape, 0)
    zero = jnp.zeros_like(value_rows)
    keys = (jnp.where(mask, key_rows, zero), jnp.where(mask, zero, key_rows))
    values = (jnp.where(mask, value_rows, zero), jnp.where(mask, zero, value_rows))
    keys_across = (key_rows * scale).T
    product = grad_rows.astype(F32) * mixed_ref[...].astype(F32)
    picks = (
        lax.broadcasted_iota(jnp.int32, (8, PAIR), 0)
        == lax.broadcasted_iota(jnp.int32, (8, PAIR), 1) // HD
    ).astype(F32)
    inner = lax.dot_general(picks, product, NT, precision=PRECISE, preferred_element_type=F32)
    length = queries.shape[0]
    grad_k = [None, None]
    grad_v = [None, None]
    for start in range(0, length, QUERY_ROWS):
        stop = start + QUERY_ROWS
        q_part = queries[start:stop]
        g_part = grad_rows[start:stop]
        outs = []
        for head in range(2):
            scores = dot(keys[head], q_part, NT)
            probs = jnp.exp(scores - log_ref[0, 0, head : head + 1, start:stop])
            grad_probs = dot(values[head], g_part, NT)
            grad_scores = (probs * (grad_probs - inner[head : head + 1, start:stop])).astype(BF16)
            part_v = dot(probs.astype(BF16), g_part)
            part_k = dot(grad_scores, q_part)
            grad_v[head] = part_v if grad_v[head] is None else grad_v[head] + part_v
            grad_k[head] = part_k if grad_k[head] is None else grad_k[head] + part_k
            outs.append(dot(keys_across[head * HD : (head + 1) * HD], grad_scores))
        out_ref[start:stop, 0:PAIR] = jnp.concatenate(outs, 0).T.astype(BF16)
    out_ref[:, PAIR : 2 * PAIR] = jnp.where(mask, grad_k[0], grad_k[1]).astype(BF16)
    out_ref[:, 2 * PAIR :] = jnp.where(mask, grad_v[0], grad_v[1]).astype(BF16)
    sums_ref[0, 0] = jnp.sum(out_ref[...].astype(F32).reshape(length // 8, 8, 3 * PAIR), 0)


def attention_specs(first):
    part = lambda offset: pl.BlockSpec((LEN, PAIR), lambda s, p: (s, 3 * (p + first) + offset))
    plain = pl.BlockSpec((LEN, PAIR), lambda s, p: (s, p + first))
    logs = pl.BlockSpec((1, 1, 2, LEN), lambda s, p: (s, p + first, 0, 0))
    return [part(0), part(1), part(2)], plain, logs


def attend(projected, latents, pairs, first, count, earlier=()):
    parts, plain, logs = attention_specs(first)
    rows = projected.shape[0]
    return pl.pallas_call(
        attend_kernel,
        grid=(latents, count),
        in_specs=parts + [pl.BlockSpec(memory_space=pl.ANY)] * len(earlier),
        out_specs=[plain, logs],
        out_shape=[
            jax.ShapeDtypeStruct((rows, pairs * PAIR), BF16),
            jax.ShapeDtypeStruct((latents, pairs, 2, LEN), F32),
        ],
        input_output_aliases={3 + i: i for i in range(len(earlier))},
        compiler_params=pltpu.CompilerParams(vmem_limit_bytes=VMEM_BYTES),
        cost_estimate=SMALL_COST,
        name="attend",
    )(projected, projected, projected, *earlier)


def attend_back(projected, mixed, grad_mixed, log_totals, latents, first, count):
    parts, plain, logs = attention_specs(first)
    rows = projected.shape[0]
    return pl.pallas_call(
        attend_back_kernel,
        grid=(latents, count),
        in_specs=[*parts, plain, plain, logs],
        out_specs=[
            pl.BlockSpec((LEN, 3 * PAIR), lambda s, p: (s, p)),
            pl.BlockSpec((1, 1, 8, 3 * PAIR), lambda s, p: (s, p, 0, 0)),
        ],
        out_shape=[
            jax.ShapeDtypeStruct((rows, count * 3 * PAIR), BF16),
            jax.ShapeDtypeStruct((latents, count, 8, 3 * PAIR), F32),
        ],
        compiler_params=pltpu.CompilerParams(vmem_limit_bytes=VMEM_BYTES),
        cost_estimate=SMALL_COST,
        name="attend_back",
    )(projected, projected, projected, mixed, grad_mixed, log_totals)


def kernel_call(body, grid, in_specs, out_specs, out_shape, name):
    return pl.pallas_call(
        body,
        grid=grid,
        in_specs=in_specs,
        out_specs=out_specs,
        out_shape=out_shape,
        compiler_params=pltpu.CompilerParams(vmem_limit_bytes=VMEM_BYTES),
        cost_estimate=SMALL_COST,
        name=name,
    )


def whole(array):
    return pl.BlockSpec(array.shape, lambda *step: (0,) * array.ndim)


def pieces_of(array, ids, width):
    return {i: (array, place, width) for place, i in enumerate(ids)}


def piece_spec(piece):
    array, block, width = piece
    return pl.BlockSpec((array.shape[0], width), lambda *step: (0, block))


def row_specs(local_rows, tile, width):
    count = local_rows // tile
    mine = pl.BlockSpec((tile, width), lambda i: (jnp.minimum(i, count - 1), 0))
    theirs = pl.BlockSpec((tile, width), lambda i: (jnp.maximum(i - count, 0), 0))
    return count, mine, theirs


def rows_product(pair, weights, extra, kind):
    local_rows, depth = pair[0].shape
    tile = min(512, local_rows)
    count, mine, theirs = row_specs(local_rows, tile, depth)
    widths = [piece[2] for piece in weights]
    width = sum(widths)
    total = 2 * local_rows

    def body(*refs):
        mine_ref, theirs_ref = refs[:2]
        weight_refs = refs[2 : 2 + len(weights)]
        extra_ref = refs[2 + len(weights)]
        out_refs = refs[3 + len(weights) :]
        step = pl.program_id(0)
        left = jnp.where(step < count, mine_ref[...], theirs_ref[...])
        if kind == "slope":

            @pl.when(step == 0)
            def _():
                out_refs[1][...] = jnp.zeros(out_refs[1].shape, F32)

        start = 0
        for ref, span in zip(weight_refs, widths):
            for low in range(0, span, 256):
                cols = slice(start + low, start + low + 256)
                product = dot(left, ref[:, low : low + 256])
                if kind == "bias":
                    out_refs[0][:, cols] = (product + extra_ref[:, cols]).astype(BF16)
                elif kind == "gelu":
                    act, slope = gelu_both(product + extra_ref[:, cols])
                    out_refs[0][:, cols] = act.astype(BF16)
                    out_refs[1][:, cols] = slope.astype(BF16)
                else:
                    grad = (product * extra_ref[:, cols].astype(F32)).astype(BF16)
                    out_refs[0][:, cols] = grad
                    out_refs[1][:, cols] += jnp.sum(
                        grad.astype(F32).reshape(tile // 8, 8, 256), 0
                    )
            start += span

    rows_out = pl.BlockSpec((tile, width), lambda i: (i, 0))
    low_shape = jax.ShapeDtypeStruct((total, width), BF16)
    if kind == "bias":
        out_specs, out_shape = [rows_out], [low_shape]
    elif kind == "gelu":
        out_specs, out_shape = [rows_out, rows_out], [low_shape, low_shape]
    else:
        out_specs = [rows_out, pl.BlockSpec((8, width), lambda i: (0, 0))]
        out_shape = [low_shape, jax.ShapeDtypeStruct((8, width), F32)]
    extra_spec = rows_out if kind == "slope" else whole(extra)
    return kernel_call(
        body,
        (2 * count,),
        [mine, theirs, *[piece_spec(w) for w in weights], extra_spec],
        out_specs,
        out_shape,
        "rows_" + kind,
    )(*pair, *[w[0] for w in weights], extra)


def columns_of(refs, start, stop):
    for ref in refs:
        if start < ref.shape[1]:
            return ref[:, start:stop]
        start, stop = start - ref.shape[1], stop - ref.shape[1]


def rows_total(lefts, weights):
    local_rows = lefts[0].shape[0] // 2
    tile = min(512, local_rows)
    count = local_rows // tile
    width = weights[0][0].shape[0]
    ends = set()
    for spans in ([a.shape[1] for a in lefts], [w[2] for w in weights]):
        end = 0
        for span in spans:
            end += span
            ends.add(end)
    ends = sorted(ends)

    def body(*refs):
        left_refs = refs[: len(lefts)]
        weight_refs = refs[len(lefts) : -2]
        mine_ref, theirs_ref = refs[-2:]
        total = None
        for start, stop in zip([0] + ends, ends):
            part = dot(columns_of(left_refs, start, stop), columns_of(weight_refs, start, stop), NT)
            total = part if total is None else total + part
        step = pl.program_id(0)

        @pl.when(step < count)
        def _():
            mine_ref[...] = total

        @pl.when(step >= count)
        def _():
            theirs_ref[...] = total.astype(BF16)

    return kernel_call(
        body,
        (2 * count,),
        [pl.BlockSpec((tile, a.shape[1]), lambda i: (i, 0)) for a in lefts]
        + [piece_spec(w) for w in weights],
        [
            pl.BlockSpec((tile, width), lambda i: (jnp.minimum(i, count - 1), 0)),
            pl.BlockSpec((tile, width), lambda i: (jnp.maximum(i - count, 0), 0)),
        ],
        [
            jax.ShapeDtypeStruct((local_rows, width), F32),
            jax.ShapeDtypeStruct((local_rows, width), BF16),
        ],
        "rows_total",
    )(*lefts, *[w[0] for w in weights])


def token_kernel(body, arrays, rows_of, out_types, sums, name):
    tokens = arrays[0].shape[0]
    tile = min(256, tokens)
    outs = len(out_types)

    def kernel(*refs):
        rows_ref = refs[len(arrays)]
        out_refs = refs[len(arrays) + 1 :]
        rows = [rows_ref[i : i + 1, :] for i in range(8)]
        if sums:
            sum_ref = out_refs[outs]

            @pl.when(pl.program_id(0) == 0)
            def _():
                sum_ref[...] = jnp.zeros(sum_ref.shape, F32)

        for start in range(0, tile, TOKEN_ROWS):
            lines = slice(start, start + TOKEN_ROWS)
            values = [ref[lines, :].astype(F32) for ref in refs[: len(arrays)]]
            results, columns = body(values, rows)
            for ref, result in zip(out_refs, results):
                ref[lines, :] = result.astype(ref.dtype)
            for i, column in enumerate(columns):
                sum_ref[i] += jnp.sum(column.reshape(TOKEN_ROWS // 8, 8, D), 0)

    tokens_spec = pl.BlockSpec((tile, D), lambda i: (i, 0))
    out_specs = [tokens_spec] * outs
    out_shape = [jax.ShapeDtypeStruct((tokens, D), t) for t in out_types]
    if sums:
        out_specs = out_specs + [pl.BlockSpec((sums, 8, D), lambda i: (0, 0, 0))]
        out_shape = out_shape + [jax.ShapeDtypeStruct((sums, 8, D), F32)]
    return kernel_call(
        kernel,
        (tokens // tile,),
        [tokens_spec] * len(arrays) + [whole(rows_of)],
        out_specs,
        out_shape,
        name,
    )(*arrays, rows_of)


def middle_body(values, rows):
    mine, theirs, tokens = values
    gate, shift, scale, bias = rows[2], rows[3], rows[4], rows[6]
    attention_out = mine + theirs + bias
    normed, _ = normalize(tokens + gate * attention_out)
    return [attention_out, normed * (1.0 + scale) + shift], []


def middle_back_body(values, rows):
    mine, theirs, upstream, tokens, attention_out = values
    gate, scale = rows[2], rows[4]
    grad_hidden = mine + theirs
    normed, inv_std = normalize(tokens + gate * attention_out)
    grad = upstream + normalize_back(grad_hidden * (1.0 + scale), normed, inv_std)
    grad_attention = grad * gate
    return [grad, grad_attention], [
        grad_hidden,
        grad_hidden * normed,
        grad * attention_out,
        grad_attention,
    ]


def first_back_body(values, rows):
    mine, theirs, tokens, grad_resid = values
    scale = rows[1]
    grad_hidden = mine + theirs
    normed, inv_std = normalize(tokens)
    grad = grad_resid + normalize_back(grad_hidden * (1.0 + scale), normed, inv_std)
    return [grad], [grad_hidden, grad_hidden * normed]


def last_body(values, rows):
    mine, theirs, tokens, attention_out, upstream = values
    gate_attn, gate_feed, bias = rows[2], rows[5], rows[7]
    feed_out = mine + theirs + bias
    resid_mid = tokens + gate_attn * attention_out
    return [resid_mid + gate_feed * feed_out], [upstream * feed_out, upstream * gate_feed]


def columns_product(pair, right, added, outs, width):
    local_rows, depth = pair[0].shape
    rows = right.shape[0]
    tile = 256
    blocks = [i for ids in outs for i in ids]
    extra = list(added)
    per_extra = len(blocks) // max(1, len(extra))

    def body(mine_ref, theirs_ref, *refs):
        right_refs = refs[: len(blocks)]
        add_refs = refs[len(blocks) : len(blocks) + len(extra)]
        out_refs = refs[len(blocks) + len(extra) :]
        mine, theirs = mine_ref[...].T, theirs_ref[...].T
        number = 0
        for ref, ids in zip(out_refs, outs):
            for place in range(len(ids)):
                total = dot(mine, right_refs[number][:local_rows])
                total = total + dot(theirs, right_refs[number][local_rows:])
                if extra:
                    start = number % per_extra * width
                    part = add_refs[number // per_extra][:, start : start + width]
                    total = total + part.astype(F32)
                ref[:, place * width : (place + 1) * width] = total.astype(BF16)
                number += 1

    token_spec = pl.BlockSpec((local_rows, tile), lambda i: (0, i))

    def out_spec(count):
        return pl.BlockSpec((tile, count * width), lambda i: (i, 0))

    return kernel_call(
        body,
        (depth // tile,),
        [token_spec, token_spec]
        + [pl.BlockSpec((rows, width), lambda i, b=b: (0, b)) for b in blocks]
        + [out_spec(per_extra) for _ in extra],
        [out_spec(len(ids)) for ids in outs],
        [jax.ShapeDtypeStruct((depth, len(ids) * width), BF16) for ids in outs],
        "columns_product",
    )(*pair, *[right] * len(blocks), *extra)


def assemble(top, low, qkv_width, out_width):
    parts = [top[0], top[2], low[0], low[2]]
    ids = [top[1], top[3], low[1], low[3]]
    half, width = parts[0].shape
    block = qkv_width + out_width
    blocks = 2 * width // block
    tile = 128

    def body(a_ref, b_ref, c_ref, d_ref, qkv_ref, out_ref):
        for number, ref in enumerate((a_ref, b_ref, c_ref, d_ref)):
            for place, i in enumerate(ids[number]):
                start = place * block
                qkv_ref[number // 2, :, i * qkv_width : (i + 1) * qkv_width] = ref[
                    :, start : start + qkv_width
                ]
                out_ref[number // 2, :, i * out_width : (i + 1) * out_width] = ref[
                    :, start + qkv_width : start + block
                ]

    qkv, out = kernel_call(
        body,
        (half // tile,),
        [pl.BlockSpec((tile, width), lambda i: (i, 0))] * 4,
        [
            pl.BlockSpec((2, tile, blocks * qkv_width), lambda i: (0, i, 0)),
            pl.BlockSpec((2, tile, blocks * out_width), lambda i: (0, i, 0)),
        ],
        [
            jax.ShapeDtypeStruct((2, half, blocks * qkv_width), BF16),
            jax.ShapeDtypeStruct((2, half, blocks * out_width), BF16),
        ],
        "assemble",
    )(*parts)
    return qkv.reshape(2 * half, -1), out.reshape(2 * half, -1)


class Grid:
    def __init__(self):
        self.rows = lax.axis_size("row")
        self.cols = lax.axis_size("col")
        self.chips = self.cols // 2
        self.bits = [1 << b for b in range(self.chips.bit_length() - 1)]
        self.orders = (self.bits, self.bits[::-1])
        self.row = lax.axis_index("row")
        self.col = lax.axis_index("col")
        self.core = self.col % 2
        source = lax.iota(jnp.int32, self.chips) ^ (self.col // 2)
        self.choose = (
            (2 * source + self.core)[:, None] == lax.iota(jnp.int32, self.cols)[None, :]
        ).astype(F32)

    def swap(self, array, flip):
        pairs = [(i, i ^ flip) for i in range(self.cols)]
        return lax.ppermute(array, "col", pairs)

    def swap_core(self, array):
        return self.swap(array, 1)

    def swap_chip(self, array, bit):
        return self.swap(array, 2 * bit)

    def to_relative(self, blocks):
        flat = blocks.reshape(self.cols, -1).astype(F32)
        picked = lax.dot_general(
            self.choose, flat, NN, precision=PRECISE, preferred_element_type=F32
        )
        return picked.reshape((self.chips,) + blocks.shape[1:])

    def to_absolute(self, blocks):
        flat = blocks.reshape(self.chips, -1)
        placed = lax.dot_general(
            self.choose, flat, TN, precision=PRECISE, preferred_element_type=F32
        )
        return placed.reshape((self.cols,) + blocks.shape[1:])

    def gather_rows(self, block):
        count = self.rows
        got = [block]
        for step in range(1, count):
            got.append(
                lax.ppermute(block, "row", [(i, (i + step) % count) for i in range(count)])
            )
        stacked = jnp.stack(got)
        ordered = [
            lax.dynamic_index_in_dim(stacked, (self.row - i) % count, 0, keepdims=False)
            for i in range(count)
        ]
        return jnp.concatenate(ordered, 0), got[-1]

    def scatter_rows(self, whole):
        count = self.rows
        blocks = whole.reshape(count, whole.shape[0] // count, whole.shape[1])
        total = lax.dynamic_index_in_dim(blocks, self.row, 0, keepdims=False).astype(F32)
        for step in range(1, count):
            sent = lax.dynamic_index_in_dim(blocks, (self.row + step) % count, 0, keepdims=False)
            total = total + lax.ppermute(
                sent, "row", [(i, (i + step) % count) for i in range(count)]
            ).astype(F32)
        return total

    def gather_early(self, block, order, late=()):
        held, ids = block, [0]
        for bit in order[:-1]:
            got = self.swap_chip(held, bit)
            if bit == order[-2]:
                got = after(got, *late)
            held = jnp.concatenate([held, got], 1)
            ids = ids + [bit ^ i for i in ids]
        return held, ids

    def early_ids(self, order):
        ids = [0]
        for bit in order[:-1]:
            ids = ids + [bit ^ i for i in ids]
        return ids

    def gather_last(self, held, ids, order):
        return self.swap_chip(held, order[-1]), [order[-1] ^ i for i in ids]

    def scatter_chips(self, keep, send, order, late=()):
        for bit in order[-2::-1]:
            got = self.swap_chip(send, bit)
            if bit == order[-2]:
                got = after(got, *late)
            total = keep.astype(F32) + got.astype(F32)
            if bit == order[0]:
                return total
            half = total.shape[1] // 2
            keep, send = total[:, :half], total[:, half:].astype(BF16)


def split_columns(array, ids):
    width = array.shape[1] // len(ids)
    return {i: array[:, n * width : (n + 1) * width] for n, i in enumerate(ids)}


def all_exchange(pieces):
    return lax.all_to_all(pieces, ("row", "col"), 0, 0, tiled=True)


def per_device(
    tokens,
    condition,
    mod_weight,
    mod_bias,
    qkv_weight,
    qv_bias,
    out_weight,
    out_bias,
    fc1_weight,
    fc1_bias,
    fc2_weight,
    fc2_bias,
    cotangent,
):
    grid = Grid()
    rows, cols, chips = grid.rows, grid.cols, grid.chips
    devices = rows * cols
    local_rows = tokens.shape[0]
    both_rows = 2 * local_rows
    latents = both_rows // LEN
    span = LEN // local_rows
    seq_rows = condition.shape[0]
    seqs = seq_rows * rows
    row_width = D // rows
    col_width = D // cols
    local_heads = qkv_weight.shape[1]
    local_units = fc1_weight.shape[1]
    plane_heads = local_heads * chips
    pairs = plane_heads // 2
    qkv_width = local_heads * 3 * HD
    out_width = local_heads * HD

    if local_heads % 2 == 0:
        qkv_local = (
            qkv_weight.reshape(row_width, local_heads // 2, 2, 3, HD)
            .transpose(0, 1, 3, 2, 4)
            .reshape(row_width, qkv_width)
        )
    else:
        qkv_local = qkv_weight.reshape(row_width, qkv_width)
    attn_local = jnp.concatenate(
        [qkv_local, out_weight.reshape(out_width, row_width).T], 1
    )
    attn_width = qkv_width + out_width
    fc1_local = fc1_weight
    fc2_local = fc2_weight.T

    small = jnp.concatenate(
        [
            condition.reshape(-1),
            fc1_bias,
            qv_bias.reshape(-1),
            out_bias,
            fc2_bias,
        ]
    )
    small_all = all_exchange(
        jnp.broadcast_to(small.reshape(1, -1, 128), (devices, small.size // 128, 128))
    )

    attn_rows, mark = grid.gather_rows(after(attn_local, small_all))
    fc1_rows = lax.all_gather(fc1_local, "row", axis=0, tiled=True)
    fc2_rows = lax.all_gather(after(fc2_local, mark), "row", axis=0, tiled=True)
    half = D // 2
    top = grid.gather_early(attn_rows[:half], grid.orders[0])
    low = grid.gather_early(attn_rows[half:], grid.orders[1])
    small_all = small_all.reshape(rows, cols, -1)
    cut = seq_rows * col_width
    cond_all = (
        small_all[:, :, :cut]
        .reshape(rows, cols, seq_rows, col_width)
        .transpose(0, 2, 1, 3)
        .reshape(seqs, D)
    )
    biases = small_all[0, :, cut:]
    fc1_bias_all = biases[:, :local_units]
    qv_bias_all = biases[:, local_units : local_units + local_heads * PAIR]
    out_bias_all = biases[:, -2 * col_width : -col_width].reshape(1, D).astype(F32)
    fc2_bias_all = biases[:, -col_width:].reshape(1, D).astype(F32)

    cond_act = silu_fn(cond_all.astype(F32)).astype(BF16)
    cond_act = lax.dynamic_slice_in_dim(cond_act, grid.row * row_width, row_width, 1)
    mod_flat = mod_weight.reshape(row_width, 6 * col_width)
    own_bias = jnp.where(grid.row == 0, mod_bias.astype(F32), 0.0)
    mod_part = dot(cond_act, mod_flat).reshape(seqs, 6, col_width) + own_bias
    mod_part = jnp.broadcast_to(
        mod_part[:, None], (seqs, span, 6, col_width)
    ).reshape(devices, 6, col_width)
    modulation = (
        all_exchange(mod_part)
        .reshape(rows, cols, 6, col_width)
        .sum(0)
        .transpose(1, 0, 2)
        .reshape(6, 1, D)
    )
    shift_attn, scale_attn, gate_attn, shift_feed, scale_feed, gate_feed = modulation
    token_rows = jnp.concatenate([modulation.reshape(6, D), out_bias_all, fc2_bias_all], 0)

    top = top + grid.gather_last(*top, grid.orders[0])
    low = low + grid.gather_last(*low, grid.orders[1])
    if local_heads % 2 == 0:
        qkv_w, out_w = assemble(top, low, qkv_width, out_width)
    else:
        attn_top = {**split_columns(top[0], top[1]), **split_columns(top[2], top[3])}
        attn_low = {**split_columns(low[0], low[1]), **split_columns(low[2], low[3])}
        attn_blocks = [jnp.concatenate([attn_top[i], attn_low[i]], 0) for i in range(chips)]
        qkv_w = (
            jnp.stack([b[:, :qkv_width] for b in attn_blocks], 1)
            .reshape(D, pairs, 2, 3, HD)
            .transpose(0, 1, 3, 2, 4)
            .reshape(D, pairs * 3 * PAIR)
        )
        out_w = jnp.concatenate([b[:, qkv_width:] for b in attn_blocks], 1)

    fc1_bias_rel = grid.to_relative(fc1_bias_all).reshape(1, chips * local_units)
    qv_rel = grid.to_relative(qv_bias_all).reshape(pairs, 2, 2, HD).transpose(0, 2, 1, 3)
    qkv_bias_rel = jnp.concatenate(
        [qv_rel[:, :1], jnp.zeros_like(qv_rel[:, :1]), qv_rel[:, 1:]], 1
    ).reshape(1, pairs * 3 * PAIR)

    def both(mine):
        return (mine, grid.swap_core(mine))

    def own_total(lefts, weights):
        mine, theirs = rows_total(lefts, weights)
        return mine, grid.swap_core(theirs)

    def sum_rows(parts):
        return lax.psum_scatter(parts, "row", scatter_dimension=0, tiled=True)

    resid = tokens.astype(F32)
    normed_attn, _ = normalize(resid)
    hidden_attn = both((normed_attn * (1.0 + scale_attn) + shift_attn).astype(BF16))
    grad_feed_low = both((cotangent.astype(F32) * gate_feed).astype(BF16))

    (projected,) = rows_product(hidden_attn, [(qkv_w, 0, qkv_w.shape[1])], qkv_bias_rel, "bias")
    order1, order2 = grid.orders
    fc1_a, ids1_a = grid.gather_early(after(fc1_rows, top[2], low[2]), order1, (projected,))
    fc1_b, ids1_b = grid.gather_last(fc1_a, ids1_a, order1)
    unit_ids = range(chips)
    fc1_pieces = {
        **pieces_of(fc1_a, ids1_a, local_units), **pieces_of(fc1_b, ids1_b, local_units)
    }
    fc1_all = [fc1_pieces[i] for i in unit_ids]
    mixed, log_totals = attend(after(projected, fc1_a), latents, pairs, 0, pairs)
    fc2_a, ids2_a = grid.gather_early(after(fc2_rows, projected), order2, (mixed,))
    fc2_b, ids2_b = grid.gather_last(fc2_a, ids2_a, order2)
    fc2_pieces = {
        **pieces_of(fc2_a, ids2_a, local_units), **pieces_of(fc2_b, ids2_b, local_units)
    }
    fc2_all = [fc2_pieces[i] for i in unit_ids]
    mixed = after(mixed, fc2_a)
    out_all = [(out_w, 0, out_w.shape[1])]
    totals = own_total([mixed], out_all)
    attention_out, hidden_feed = token_kernel(
        middle_body,
        [after(totals[0], fc1_b), totals[1], tokens],
        token_rows,
        [F32, BF16],
        0,
        "middle",
    )
    hidden_feed = both(hidden_feed)
    acts, slopes = rows_product(hidden_feed, fc1_all, fc1_bias_rel, "gelu")

    def send_units(left, right, orders):
        count = len(orders)
        outs = [
            [count * (order[-1] ^ i) + part for i in grid.early_ids(order)]
            for part, order in enumerate(orders)
        ]
        sent = columns_product(left, right, [], outs, local_units // count)
        return [grid.swap_chip(a, order[-1]) for a, order in zip(sent, orders)], sent[0]

    def keep_units(left, right, got, orders):
        count = len(orders)
        outs = []
        for part, order in enumerate(orders):
            places = [count * i + part for i in grid.early_ids(order)]
            outs += [places[: len(places) // 2], places[len(places) // 2 :]]
        return columns_product(left, right, got, outs, local_units // count)

    def sum_chips(kept, orders, late):
        sums = [
            grid.scatter_chips(kept[2 * part], kept[2 * part + 1], order, late)
            for part, order in enumerate(orders)
        ]
        return jnp.concatenate(sums, 1).astype(BF16)

    fc2_got, fc2_sent = send_units(grad_feed_low, acts, grid.orders)
    grad_pre, bias_fc1 = rows_product(
        (after(grad_feed_low[0], fc2_sent), grad_feed_low[1]), fc2_all, slopes, "slope"
    )
    fc1_got, sent = send_units(hidden_feed, grad_pre, [order1])
    totals = own_total([after(grad_pre, sent, *fc2_got)], fc1_all)
    fc2_kept = keep_units(grad_feed_low, after(acts, totals[0]), fc2_got, grid.orders)
    grad_resid_mid, grad_attention_low, middle_sums = token_kernel(
        middle_back_body,
        [after(totals[0], fc2_kept[0]), totals[1], cotangent, tokens, attention_out],
        token_rows,
        [F32, BF16],
        4,
        "middle_back",
    )
    grad_attention_low = both(grad_attention_low)

    (grad_mixed,) = rows_product(
        grad_attention_low, out_all, jnp.zeros((1, out_w.shape[1]), F32), "bias"
    )
    (grad_out,) = columns_product(
        grad_attention_low, after(mixed, grad_mixed), [], [[0]], mixed.shape[1]
    )
    grad_mixed = after(grad_mixed, grad_out)
    grad_late, bias_late = attend_back(
        projected, mixed, grad_mixed, log_totals, latents, 1, pairs - 1
    )
    fc2_sums = sum_chips(fc2_kept, grid.orders, (grad_late,))
    fc1_kept = keep_units(hidden_feed, after(grad_pre, grad_late), fc1_got, [order1])
    late_chips = chips * (pairs - 1) // pairs
    qkv_late = columns_product(
        hidden_attn, grad_late, [], [[i] for i in range(late_chips)], qkv_width
    ) if (
        local_heads % 2 == 0
    ) else None
    early_input = after(grad_mixed, grad_late, fc2_sums, fc1_kept[0])
    grad_early, bias_early = attend_back(
        projected, mixed, early_input, log_totals, latents, 0, 1
    )
    fc1_sums = sum_chips(fc1_kept, [order1], (grad_early,))
    fc2_part = sum_rows(fc2_sums)
    fc1_part = sum_rows(fc1_sums)
    bias_qkv = jnp.concatenate([bias_early, bias_late], 1).sum((0, 2))
    if local_heads % 2 == 0:
        qkv_early = columns_product(hidden_attn, grad_early, [], [[0]], qkv_width)
        grad_qkv = [*qkv_early, *qkv_late]
    else:
        grad_projected = jnp.concatenate([grad_early, grad_late], 1)
        (grad_qkv,) = columns_product(
            hidden_attn, grad_projected, [], [[0]], 3 * PAIR * pairs
        )
        grad_qkv = (
            grad_qkv.reshape(D, pairs, 3, 2, HD).transpose(0, 1, 3, 2, 4).reshape(D, chips, qkv_width)
        )
        grad_qkv = [grad_qkv[:, i] for i in range(chips)]

    def pick(part, ids):
        lines = slice(0, half) if part == 0 else slice(half, D)
        return jnp.concatenate(
            [
                array
                for i in ids
                for array in (
                    grad_qkv[i][lines],
                    grad_out[lines, i * out_width : (i + 1) * out_width],
                )
            ],
            1,
        )

    attn_got = [
        grid.swap_chip(pick(number, gathered[3]), grid.orders[number][-1])
        for number, gathered in enumerate((top, low))
    ]
    attn_sums = []
    for number, gathered in enumerate((top, low)):
        order = grid.orders[number]
        kept = pick(number, gathered[1]).astype(F32) + attn_got[number].astype(F32)
        middle = kept.shape[1] // 2
        attn_sums.append(
            grid.scatter_chips(kept[:, :middle], kept[:, middle:].astype(BF16), order)
        )
    attn_part = grid.scatter_rows(jnp.concatenate(attn_sums, 0).astype(BF16))
    qkv_part = attn_part[:, :qkv_width]
    if local_heads % 2 == 0:
        qkv_part = qkv_part.reshape(row_width, local_heads // 2, 3, 2, HD).transpose(0, 1, 3, 2, 4)
    qkv_part = qkv_part.reshape(row_width, local_heads, 3 * HD)
    out_part = attn_part[:, qkv_width:].T.reshape(local_heads, HD, row_width)

    totals = own_total([after(grad_early, *attn_got), grad_late], [(qkv_w, 0, qkv_w.shape[1])])
    tokens_grad, first_sums = token_kernel(
        first_back_body, [*totals, tokens, grad_resid_mid], token_rows, [F32], 2, "first_back"
    )
    totals = own_total([after(acts, totals[0], fc2_part, *attn_sums)], fc2_all)
    layer_out, last_sums = token_kernel(
        last_body, [after(totals[0], fc1_part), totals[1], tokens, attention_out, cotangent], token_rows, [BF16], 2, "last"
    )

    first_sums, middle_sums, last_sums = (
        sums.sum(1) for sums in (first_sums, middle_sums, last_sums)
    )
    mod_rows = jnp.concatenate(
        [first_sums, middle_sums[2:3], middle_sums[:2], last_sums[:1], middle_sums[3:], last_sums[1:]]
    )
    mod_rows = mod_rows.reshape(8, cols, col_width).transpose(1, 0, 2)
    fc1_rel = bias_fc1.sum(0).reshape(chips, local_units)
    qkv_rel = bias_qkv.reshape(pairs, 3, 2, HD)
    qv_rel = jnp.stack([qkv_rel[:, 0], qkv_rel[:, 2]], 2).reshape(chips, local_heads * PAIR)
    hidden_rows = grid.to_absolute(jnp.concatenate([fc1_rel, qv_rel], 1)).reshape(
        cols, -1, col_width
    )
    pieces = jnp.concatenate([mod_rows, hidden_rows], 1)
    pieces = jnp.broadcast_to(pieces[None], (rows,) + pieces.shape).reshape(
        devices, -1, col_width
    )
    arrived = all_exchange(pieces)
    grad_modulation = arrived[:, :6].reshape(seqs, span, 6, col_width).sum(1)
    sums = arrived[:, 6:].sum(0)
    out_bias_grad = sums[0]
    fc2_bias_grad = sums[1]
    hidden_sums = sums[2:].reshape(-1)
    fc1_bias_grad = hidden_sums[:local_units]
    qv_bias_grad = hidden_sums[local_units:].reshape(local_heads, PAIR)
    mod_bias_grad = jnp.sum(grad_modulation, 0)
    grad_mod_flat = grad_modulation.reshape(seqs, 6 * col_width)
    mod_part_grad = lax.dot_general(
        cond_act.astype(F32), grad_mod_flat, TN, precision=PRECISE, preferred_element_type=F32
    ).reshape(row_width, 6, col_width)
    cond_part = lax.dot_general(
        grad_mod_flat,
        mod_flat.astype(F32),
        NT,
        precision=PRECISE,
        preferred_element_type=F32,
    )
    cond_pieces = lax.dynamic_update_slice_in_dim(
        jnp.zeros((seqs, D), F32), cond_part, grid.row * row_width, 1
    )
    cond_pieces = (
        cond_pieces.reshape(rows, seq_rows, cols, col_width)
        .transpose(0, 2, 1, 3)
        .reshape(devices, seq_rows, col_width)
    )
    grad_cond_act = all_exchange(cond_pieces).sum(0)
    _, silu_pull = jax.vjp(silu_fn, condition.astype(F32))
    condition_grad = silu_pull(grad_cond_act)[0]
    return (
        layer_out,
        tokens_grad,
        condition_grad,
        mod_part_grad,
        mod_bias_grad,
        qkv_part,
        qv_bias_grad,
        out_part,
        out_bias_grad,
        fc1_part.astype(F32),
        fc1_bias_grad,
        fc2_part.astype(F32).T,
        fc2_bias_grad,
    )


def solution(mesh):
    return jax.shard_map(
        per_device,
        mesh=mesh,
        in_specs=(
            P(("row", "col"), None),
            P("row", "col"),
            P("row", None, "col"),
            P(None, "col"),
            P("row", "col", None),
            P("col", None),
            P("col", None, "row"),
            P("col"),
            P("row", "col"),
            P("col"),
            P("col", "row"),
            P("col"),
            P(("row", "col"), None),
        ),
        out_specs=(
            P(("row", "col"), None),
            P(("row", "col"), None),
            P("row", "col"),
            P("row", None, "col"),
            P(None, "col"),
            P("row", "col", None),
            P("col", None),
            P("col", None, "row"),
            P("col"),
            P("row", "col"),
            P("col"),
            P("col", "row"),
            P("col"),
        ),
        check_vma=False,
    )
```

```python
import functools
import math

import jax
import jax.numpy as jnp
from jax import lax
from jax.experimental import pallas as pl
from jax.experimental.pallas import tpu as pltpu
from jax.sharding import PartitionSpec as P

D = 1024
HD = 64
LEN = 1024
PAIR = 2 * HD

EPSILON = 1e-06
PRECISE = lax.Precision.HIGHEST
NN = (((1,), (0,)), ((), ()))
NT = (((1,), (1,)), ((), ()))
TN = (((0,), (0,)), ((), ()))
F32 = jnp.float32
BF16 = jnp.bfloat16
QUERY_ROWS = 512
TOKEN_ROWS = 32
VMEM_BYTES = 40 * 1024 * 1024
SMALL_COST = pl.CostEstimate(flops=1000, bytes_accessed=1000, transcendentals=0)


def dot(left, right, dims=NN):
    return lax.dot_general(left, right, dims, preferred_element_type=F32)


def silu_fn(values):
    return values * jax.nn.sigmoid(values)


def gelu_both(values):
    c = math.sqrt(2.0 / math.pi)
    square = values * values
    half = 0.5 + 0.5 * jnp.tanh(values * (c + (c * 0.044715) * square))
    gelu = values * half
    slope = half + gelu * (1.0 - half) * (2.0 * c + (6.0 * c * 0.044715) * square)
    return gelu, slope


def normalize(resid):
    average = jnp.mean(resid, 1, keepdims=True)
    spread = jnp.mean(resid * resid, 1, keepdims=True) - average * average
    inv_std = lax.rsqrt(spread + EPSILON)
    return ((resid - average) * inv_std, inv_std)


def normalize_back(grad_norm, normed, inv_std):
    average = jnp.mean(grad_norm, 1, keepdims=True)
    crossed = jnp.mean(grad_norm * normed, 1, keepdims=True)
    return inv_std * (grad_norm - average - normed * crossed)


def after(array, *earlier):
    return lax.optimization_barrier((array, *earlier))[0]


def head_lanes(shape, head):
    lane = lax.broadcasted_iota(jnp.int32, shape, 1)
    return lane < HD if head == 0 else lane >= HD


def attend_kernel(q_ref, k_ref, v_ref, *refs):
    mixed_ref, log_ref = refs[-2:]
    queries = q_ref[...] * jnp.asarray(HD**-0.5, BF16)
    key_rows = k_ref[...]
    values_across = v_ref[...].T
    mask = head_lanes(key_rows.shape, 0)
    zero = jnp.zeros_like(key_rows)
    keys = (jnp.where(mask, key_rows, zero), jnp.where(mask, zero, key_rows))
    length = queries.shape[0]
    for start in range(0, length, QUERY_ROWS):
        stop = start + QUERY_ROWS
        q_part = queries[start:stop]
        outs = []
        for head in range(2):
            scores = dot(keys[head], q_part, NT)
            top = jnp.max(scores, 0, keepdims=True)
            expon = jnp.exp(scores - top)
            total = jnp.sum(expon, 0, keepdims=True)
            out = dot(values_across[head * HD : (head + 1) * HD], expon.astype(BF16))
            outs.append(out / total)
            log_ref[0, 0, head : head + 1, start:stop] = top + jnp.log(total)
        mixed_ref[start:stop, :] = jnp.concatenate(outs, 0).T.astype(BF16)


def attend_back_kernel(q_ref, k_ref, v_ref, mixed_ref, grad_ref, log_ref, out_ref, sums_ref):
    scale = jnp.asarray(HD**-0.5, BF16)
    queries = q_ref[...] * scale
    key_rows = k_ref[...]
    value_rows = v_ref[...]
    grad_rows = grad_ref[...]
    mask = head_lanes(value_rows.shape, 0)
    zero = jnp.zeros_like(value_rows)
    keys = (jnp.where(mask, key_rows, zero), jnp.where(mask, zero, key_rows))
    values = (jnp.where(mask, value_rows, zero), jnp.where(mask, zero, value_rows))
    keys_across = (key_rows * scale).T
    product = grad_rows.astype(F32) * mixed_ref[...].astype(F32)
    picks = (
        lax.broadcasted_iota(jnp.int32, (8, PAIR), 0)
        == lax.broadcasted_iota(jnp.int32, (8, PAIR), 1) // HD
    ).astype(F32)
    inner = lax.dot_general(picks, product, NT, precision=PRECISE, preferred_element_type=F32)
    length = queries.shape[0]
    grad_k = [None, None]
    grad_v = [None, None]
    for start in range(0, length, QUERY_ROWS):
        stop = start + QUERY_ROWS
        q_part = queries[start:stop]
        g_part = grad_rows[start:stop]
        outs = []
        for head in range(2):
            scores = dot(keys[head], q_part, NT)
            probs = jnp.exp(scores - log_ref[0, 0, head : head + 1, start:stop])
            grad_probs = dot(values[head], g_part, NT)
            grad_scores = (probs * (grad_probs - inner[head : head + 1, start:stop])).astype(BF16)
            part_v = dot(probs.astype(BF16), g_part)
            part_k = dot(grad_scores, q_part)
            grad_v[head] = part_v if grad_v[head] is None else grad_v[head] + part_v
            grad_k[head] = part_k if grad_k[head] is None else grad_k[head] + part_k
            outs.append(dot(keys_across[head * HD : (head + 1) * HD], grad_scores))
        out_ref[start:stop, 0:PAIR] = jnp.concatenate(outs, 0).T.astype(BF16)
    out_ref[:, PAIR : 2 * PAIR] = jnp.where(mask, grad_k[0], grad_k[1]).astype(BF16)
    out_ref[:, 2 * PAIR :] = jnp.where(mask, grad_v[0], grad_v[1]).astype(BF16)
    sums_ref[0, 0] = jnp.sum(out_ref[...].astype(F32).reshape(length // 8, 8, 3 * PAIR), 0)


def attention_specs(first):
    part = lambda offset: pl.BlockSpec((LEN, PAIR), lambda s, p: (s, 3 * (p + first) + offset))
    plain = pl.BlockSpec((LEN, PAIR), lambda s, p: (s, p + first))
    logs = pl.BlockSpec((1, 1, 2, LEN), lambda s, p: (s, p + first, 0, 0))
    return [part(0), part(1), part(2)], plain, logs


def attend(projected, latents, pairs, first, count, earlier=()):
    parts, plain, logs = attention_specs(first)
    rows = projected.shape[0]
    return pl.pallas_call(
        attend_kernel,
        grid=(latents, count),
        in_specs=parts + [pl.BlockSpec(memory_space=pl.ANY)] * len(earlier),
        out_specs=[plain, logs],
        out_shape=[
            jax.ShapeDtypeStruct((rows, pairs * PAIR), BF16),
            jax.ShapeDtypeStruct((latents, pairs, 2, LEN), F32),
        ],
        input_output_aliases={3 + i: i for i in range(len(earlier))},
        compiler_params=pltpu.CompilerParams(vmem_limit_bytes=VMEM_BYTES),
        cost_estimate=SMALL_COST,
        name="attend",
    )(projected, projected, projected, *earlier)


def attend_back(projected, mixed, grad_mixed, log_totals, latents, first, count):
    parts, plain, logs = attention_specs(first)
    rows = projected.shape[0]
    return pl.pallas_call(
        attend_back_kernel,
        grid=(latents, count),
        in_specs=[*parts, plain, plain, logs],
        out_specs=[
            pl.BlockSpec((LEN, 3 * PAIR), lambda s, p: (s, p)),
            pl.BlockSpec((1, 1, 8, 3 * PAIR), lambda s, p: (s, p, 0, 0)),
        ],
        out_shape=[
            jax.ShapeDtypeStruct((rows, count * 3 * PAIR), BF16),
            jax.ShapeDtypeStruct((latents, count, 8, 3 * PAIR), F32),
        ],
        compiler_params=pltpu.CompilerParams(vmem_limit_bytes=VMEM_BYTES),
        cost_estimate=SMALL_COST,
        name="attend_back",
    )(projected, projected, projected, mixed, grad_mixed, log_totals)


def kernel_call(body, grid, in_specs, out_specs, out_shape, name):
    return pl.pallas_call(
        body,
        grid=grid,
        in_specs=in_specs,
        out_specs=out_specs,
        out_shape=out_shape,
        compiler_params=pltpu.CompilerParams(vmem_limit_bytes=VMEM_BYTES),
        cost_estimate=SMALL_COST,
        name=name,
    )


def whole(array):
    return pl.BlockSpec(array.shape, lambda *step: (0,) * array.ndim)


def pieces_of(array, ids, width):
    return {i: (array, place, width) for place, i in enumerate(ids)}


def piece_spec(piece):
    array, block, width = piece
    return pl.BlockSpec((array.shape[0], width), lambda *step: (0, block))


def row_specs(local_rows, tile, width):
    count = local_rows // tile
    mine = pl.BlockSpec((tile, width), lambda i: (jnp.minimum(i, count - 1), 0))
    theirs = pl.BlockSpec((tile, width), lambda i: (jnp.maximum(i - count, 0), 0))
    return count, mine, theirs


def rows_product(pair, weights, extra, kind):
    local_rows, depth = pair[0].shape
    tile = min(512, local_rows)
    count, mine, theirs = row_specs(local_rows, tile, depth)
    widths = [piece[2] for piece in weights]
    width = sum(widths)
    total = 2 * local_rows

    def body(*refs):
        mine_ref, theirs_ref = refs[:2]
        weight_refs = refs[2 : 2 + len(weights)]
        extra_ref = refs[2 + len(weights)]
        out_refs = refs[3 + len(weights) :]
        step = pl.program_id(0)
        left = jnp.where(step < count, mine_ref[...], theirs_ref[...])
        if kind == "slope":

            @pl.when(step == 0)
            def _():
                out_refs[1][...] = jnp.zeros(out_refs[1].shape, F32)

        start = 0
        for ref, span in zip(weight_refs, widths):
            step_width = min(256, span)
            for low in range(0, span, step_width):
                cols = slice(start + low, start + low + step_width)
                product = dot(left, ref[:, low : low + step_width])
                if kind == "bias":
                    out_refs[0][:, cols] = (product + extra_ref[:, cols]).astype(BF16)
                elif kind == "gelu":
                    act, slope = gelu_both(product + extra_ref[:, cols])
                    out_refs[0][:, cols] = act.astype(BF16)
                    out_refs[1][:, cols] = slope.astype(BF16)
                else:
                    grad = (product * extra_ref[:, cols].astype(F32)).astype(BF16)
                    out_refs[0][:, cols] = grad
                    out_refs[1][:, cols] += jnp.sum(
                        grad.astype(F32).reshape(tile // 8, 8, step_width), 0
                    )
            start += span

    rows_out = pl.BlockSpec((tile, width), lambda i: (i, 0))
    low_shape = jax.ShapeDtypeStruct((total, width), BF16)
    if kind == "bias":
        out_specs, out_shape = [rows_out], [low_shape]
    elif kind == "gelu":
        out_specs, out_shape = [rows_out, rows_out], [low_shape, low_shape]
    else:
        out_specs = [rows_out, pl.BlockSpec((8, width), lambda i: (0, 0))]
        out_shape = [low_shape, jax.ShapeDtypeStruct((8, width), F32)]
    extra_spec = rows_out if kind == "slope" else whole(extra)
    return kernel_call(
        body,
        (2 * count,),
        [mine, theirs, *[piece_spec(w) for w in weights], extra_spec],
        out_specs,
        out_shape,
        "rows_" + kind,
    )(*pair, *[w[0] for w in weights], extra)


def columns_of(refs, start, stop):
    for ref in refs:
        if start < ref.shape[1]:
            return ref[:, start:stop]
        start, stop = start - ref.shape[1], stop - ref.shape[1]


def rows_total(lefts, weights):
    local_rows = lefts[0].shape[0] // 2
    tile = min(512, local_rows)
    count = local_rows // tile
    width = weights[0][0].shape[0]
    ends = set()
    for spans in ([a.shape[1] for a in lefts], [w[2] for w in weights]):
        end = 0
        for span in spans:
            end += span
            ends.add(end)
    ends = sorted(ends)

    def body(*refs):
        left_refs = refs[: len(lefts)]
        weight_refs = refs[len(lefts) : -2]
        mine_ref, theirs_ref = refs[-2:]
        total = None
        for start, stop in zip([0] + ends, ends):
            part = dot(columns_of(left_refs, start, stop), columns_of(weight_refs, start, stop), NT)
            total = part if total is None else total + part
        step = pl.program_id(0)

        @pl.when(step < count)
        def _():
            mine_ref[...] = total

        @pl.when(step >= count)
        def _():
            theirs_ref[...] = total.astype(BF16)

    return kernel_call(
        body,
        (2 * count,),
        [pl.BlockSpec((tile, a.shape[1]), lambda i: (i, 0)) for a in lefts]
        + [piece_spec(w) for w in weights],
        [
            pl.BlockSpec((tile, width), lambda i: (jnp.minimum(i, count - 1), 0)),
            pl.BlockSpec((tile, width), lambda i: (jnp.maximum(i - count, 0), 0)),
        ],
        [
            jax.ShapeDtypeStruct((local_rows, width), F32),
            jax.ShapeDtypeStruct((local_rows, width), BF16),
        ],
        "rows_total",
    )(*lefts, *[w[0] for w in weights])


def token_kernel(body, arrays, rows_of, out_types, sums, name):
    tokens = arrays[0].shape[0]
    tile = min(256, tokens)
    outs = len(out_types)

    def kernel(*refs):
        rows_ref = refs[len(arrays)]
        out_refs = refs[len(arrays) + 1 :]
        rows = [rows_ref[i : i + 1, :] for i in range(8)]
        if sums:
            sum_ref = out_refs[outs]

            @pl.when(pl.program_id(0) == 0)
            def _():
                sum_ref[...] = jnp.zeros(sum_ref.shape, F32)

        for start in range(0, tile, TOKEN_ROWS):
            lines = slice(start, start + TOKEN_ROWS)
            values = [ref[lines, :].astype(F32) for ref in refs[: len(arrays)]]
            results, columns = body(values, rows)
            for ref, result in zip(out_refs, results):
                ref[lines, :] = result.astype(ref.dtype)
            for i, column in enumerate(columns):
                sum_ref[i] += jnp.sum(column.reshape(TOKEN_ROWS // 8, 8, D), 0)

    tokens_spec = pl.BlockSpec((tile, D), lambda i: (i, 0))
    out_specs = [tokens_spec] * outs
    out_shape = [jax.ShapeDtypeStruct((tokens, D), t) for t in out_types]
    if sums:
        out_specs = out_specs + [pl.BlockSpec((sums, 8, D), lambda i: (0, 0, 0))]
        out_shape = out_shape + [jax.ShapeDtypeStruct((sums, 8, D), F32)]
    return kernel_call(
        kernel,
        (tokens // tile,),
        [tokens_spec] * len(arrays) + [whole(rows_of)],
        out_specs,
        out_shape,
        name,
    )(*arrays, rows_of)


def middle_body(values, rows):
    mine, theirs, tokens = values
    gate, shift, scale, bias = rows[2], rows[3], rows[4], rows[6]
    attention_out = mine + theirs + bias
    normed, _ = normalize(tokens + gate * attention_out)
    return [attention_out, normed * (1.0 + scale) + shift], []


def middle_back_body(values, rows):
    mine, theirs, upstream, tokens, attention_out = values
    gate, scale = rows[2], rows[4]
    grad_hidden = mine + theirs
    normed, inv_std = normalize(tokens + gate * attention_out)
    grad = upstream + normalize_back(grad_hidden * (1.0 + scale), normed, inv_std)
    grad_attention = grad * gate
    return [grad, grad_attention], [
        grad_hidden,
        grad_hidden * normed,
        grad * attention_out,
        grad_attention,
    ]


def first_back_body(values, rows):
    mine, theirs, tokens, grad_resid = values
    scale = rows[1]
    grad_hidden = mine + theirs
    normed, inv_std = normalize(tokens)
    grad = grad_resid + normalize_back(grad_hidden * (1.0 + scale), normed, inv_std)
    return [grad], [grad_hidden, grad_hidden * normed]


def last_body(values, rows):
    mine, theirs, tokens, attention_out, upstream = values
    gate_attn, gate_feed, bias = rows[2], rows[5], rows[7]
    feed_out = mine + theirs + bias
    resid_mid = tokens + gate_attn * attention_out
    return [resid_mid + gate_feed * feed_out], [upstream * feed_out, upstream * gate_feed]


def columns_product(pair, right, added, outs, width):
    local_rows, depth = pair[0].shape
    rows = right.shape[0]
    tile = 256
    blocks = [i for ids in outs for i in ids]
    extra = list(added)
    per_extra = len(blocks) // max(1, len(extra))

    def body(mine_ref, theirs_ref, *refs):
        right_refs = refs[: len(blocks)]
        add_refs = refs[len(blocks) : len(blocks) + len(extra)]
        out_refs = refs[len(blocks) + len(extra) :]
        mine, theirs = mine_ref[...].T, theirs_ref[...].T
        number = 0
        for ref, ids in zip(out_refs, outs):
            for place in range(len(ids)):
                total = dot(mine, right_refs[number][:local_rows])
                total = total + dot(theirs, right_refs[number][local_rows:])
                if extra:
                    start = number % per_extra * width
                    part = add_refs[number // per_extra][:, start : start + width]
                    total = total + part.astype(F32)
                ref[:, place * width : (place + 1) * width] = total.astype(BF16)
                number += 1

    token_spec = pl.BlockSpec((local_rows, tile), lambda i: (0, i))

    def out_spec(count):
        return pl.BlockSpec((tile, count * width), lambda i: (i, 0))

    return kernel_call(
        body,
        (depth // tile,),
        [token_spec, token_spec]
        + [pl.BlockSpec((rows, width), lambda i, b=b: (0, b)) for b in blocks]
        + [out_spec(per_extra) for _ in extra],
        [out_spec(len(ids)) for ids in outs],
        [jax.ShapeDtypeStruct((depth, len(ids) * width), BF16) for ids in outs],
        "columns_product",
    )(*pair, *[right] * len(blocks), *extra)


def assemble(top, low, qkv_width, out_width):
    parts = [top[0], top[2], low[0], low[2]]
    ids = [top[1], top[3], low[1], low[3]]
    half, width = parts[0].shape
    block = qkv_width + out_width
    blocks = 2 * width // block
    tile = 128

    def body(a_ref, b_ref, c_ref, d_ref, qkv_ref, out_ref):
        for number, ref in enumerate((a_ref, b_ref, c_ref, d_ref)):
            for place, i in enumerate(ids[number]):
                start = place * block
                qkv_ref[number // 2, :, i * qkv_width : (i + 1) * qkv_width] = ref[
                    :, start : start + qkv_width
                ]
                out_ref[number // 2, :, i * out_width : (i + 1) * out_width] = ref[
                    :, start + qkv_width : start + block
                ]

    qkv, out = kernel_call(
        body,
        (half // tile,),
        [pl.BlockSpec((tile, width), lambda i: (i, 0))] * 4,
        [
            pl.BlockSpec((2, tile, blocks * qkv_width), lambda i: (0, i, 0)),
            pl.BlockSpec((2, tile, blocks * out_width), lambda i: (0, i, 0)),
        ],
        [
            jax.ShapeDtypeStruct((2, half, blocks * qkv_width), BF16),
            jax.ShapeDtypeStruct((2, half, blocks * out_width), BF16),
        ],
        "assemble",
    )(*parts)
    return qkv.reshape(2 * half, -1), out.reshape(2 * half, -1)


class Grid:
    def __init__(self):
        self.rows = lax.axis_size("row")
        self.cols = lax.axis_size("col")
        self.chips = self.cols // 2
        self.bits = [1 << b for b in range(self.chips.bit_length() - 1)]
        self.orders = (self.bits, self.bits[::-1])
        self.row = lax.axis_index("row")
        self.col = lax.axis_index("col")
        self.core = self.col % 2
        source = lax.iota(jnp.int32, self.chips) ^ (self.col // 2)
        self.choose = (
            (2 * source + self.core)[:, None] == lax.iota(jnp.int32, self.cols)[None, :]
        ).astype(F32)

    def swap(self, array, flip):
        pairs = [(i, i ^ flip) for i in range(self.cols)]
        return lax.ppermute(array, "col", pairs)

    def swap_core(self, array):
        return self.swap(array, 1)

    def swap_chip(self, array, bit):
        return self.swap(array, 2 * bit)

    def to_relative(self, blocks):
        flat = blocks.reshape(self.cols, -1).astype(F32)
        picked = lax.dot_general(
            self.choose, flat, NN, precision=PRECISE, preferred_element_type=F32
        )
        return picked.reshape((self.chips,) + blocks.shape[1:])

    def to_absolute(self, blocks):
        flat = blocks.reshape(self.chips, -1)
        placed = lax.dot_general(
            self.choose, flat, TN, precision=PRECISE, preferred_element_type=F32
        )
        return placed.reshape((self.cols,) + blocks.shape[1:])

    def gather_rows(self, block):
        count = self.rows
        got = [block]
        for step in range(1, count):
            got.append(
                lax.ppermute(block, "row", [(i, (i + step) % count) for i in range(count)])
            )
        stacked = jnp.stack(got)
        ordered = [
            lax.dynamic_index_in_dim(stacked, (self.row - i) % count, 0, keepdims=False)
            for i in range(count)
        ]
        return jnp.concatenate(ordered, 0), got[-1]

    def scatter_rows(self, whole):
        count = self.rows
        blocks = whole.reshape(count, whole.shape[0] // count, whole.shape[1])
        total = lax.dynamic_index_in_dim(blocks, self.row, 0, keepdims=False).astype(F32)
        for step in range(1, count):
            sent = lax.dynamic_index_in_dim(blocks, (self.row + step) % count, 0, keepdims=False)
            total = total + lax.ppermute(
                sent, "row", [(i, (i + step) % count) for i in range(count)]
            ).astype(F32)
        return total

    def gather_early(self, block, order, late=()):
        held, ids = block, [0]
        for bit in order[:-1]:
            got = self.swap_chip(held, bit)
            if bit == order[-2]:
                got = after(got, *late)
            held = jnp.concatenate([held, got], 1)
            ids = ids + [bit ^ i for i in ids]
        return held, ids

    def early_ids(self, order):
        ids = [0]
        for bit in order[:-1]:
            ids = ids + [bit ^ i for i in ids]
        return ids

    def gather_last(self, held, ids, order):
        return self.swap_chip(held, order[-1]), [order[-1] ^ i for i in ids]

    def scatter_chips(self, keep, send, order, late=()):
        for bit in order[-2::-1]:
            got = self.swap_chip(send, bit)
            if bit == order[-2]:
                got = after(got, *late)
            total = keep.astype(F32) + got.astype(F32)
            if bit == order[0]:
                return total
            half = total.shape[1] // 2
            keep, send = total[:, :half], total[:, half:].astype(BF16)


def split_columns(array, ids):
    width = array.shape[1] // len(ids)
    return {i: array[:, n * width : (n + 1) * width] for n, i in enumerate(ids)}


def all_exchange(pieces):
    return lax.all_to_all(pieces, ("row", "col"), 0, 0, tiled=True)


def per_device(
    tokens,
    condition,
    mod_weight,
    mod_bias,
    qkv_weight,
    qv_bias,
    out_weight,
    out_bias,
    fc1_weight,
    fc1_bias,
    fc2_weight,
    fc2_bias,
    cotangent,
):
    grid = Grid()
    rows, cols, chips = grid.rows, grid.cols, grid.chips
    devices = rows * cols
    local_rows = tokens.shape[0]
    both_rows = 2 * local_rows
    latents = both_rows // LEN
    span = LEN // local_rows
    seq_rows = condition.shape[0]
    seqs = seq_rows * rows
    row_width = D // rows
    col_width = D // cols
    local_heads = qkv_weight.shape[1]
    local_units = fc1_weight.shape[1]
    plane_heads = local_heads * chips
    pairs = plane_heads // 2
    qkv_width = local_heads * 3 * HD
    out_width = local_heads * HD

    if local_heads % 2 == 0:
        qkv_local = (
            qkv_weight.reshape(row_width, local_heads // 2, 2, 3, HD)
            .transpose(0, 1, 3, 2, 4)
            .reshape(row_width, qkv_width)
        )
    else:
        qkv_local = qkv_weight.reshape(row_width, qkv_width)
    attn_local = jnp.concatenate(
        [qkv_local, out_weight.reshape(out_width, row_width).T], 1
    )
    attn_width = qkv_width + out_width
    fc1_local = fc1_weight
    fc2_local = fc2_weight.T

    small = jnp.concatenate(
        [
            condition.reshape(-1),
            fc1_bias,
            qv_bias.reshape(-1),
            out_bias,
            fc2_bias,
        ]
    )
    small_all = all_exchange(
        jnp.broadcast_to(small.reshape(1, -1, 128), (devices, small.size // 128, 128))
    )

    attn_rows, mark = grid.gather_rows(attn_local)
    fc1_rows = lax.all_gather(after(fc1_local, mark), "row", axis=0, tiled=True)
    fc2_rows = lax.all_gather(after(fc2_local, fc1_rows), "row", axis=0, tiled=True)
    attn_rows = after(attn_rows, small_all)
    half = D // 2
    top = grid.gather_early(attn_rows[:half], grid.orders[0])
    low = grid.gather_early(attn_rows[half:], grid.orders[1])
    small_all = after(small_all, top[0], low[0]).reshape(rows, cols, -1)
    cut = seq_rows * col_width
    cond_all = (
        small_all[:, :, :cut]
        .reshape(rows, cols, seq_rows, col_width)
        .transpose(0, 2, 1, 3)
        .reshape(seqs, D)
    )
    biases = small_all[0, :, cut:]
    fc1_bias_all = biases[:, :local_units]
    qv_bias_all = biases[:, local_units : local_units + local_heads * PAIR]
    out_bias_all = biases[:, -2 * col_width : -col_width].reshape(1, D).astype(F32)
    fc2_bias_all = biases[:, -col_width:].reshape(1, D).astype(F32)

    cond_act = silu_fn(cond_all.astype(F32)).astype(BF16)
    cond_act = lax.dynamic_slice_in_dim(cond_act, grid.row * row_width, row_width, 1)
    mod_flat = mod_weight.reshape(row_width, 6 * col_width)
    own_bias = jnp.where(grid.row == 0, mod_bias.astype(F32), 0.0)
    mod_part = dot(cond_act, mod_flat).reshape(seqs, 6, col_width) + own_bias
    mod_part = jnp.broadcast_to(
        mod_part[:, None], (seqs, span, 6, col_width)
    ).reshape(devices, 6, col_width)
    modulation = (
        all_exchange(mod_part)
        .reshape(rows, cols, 6, col_width)
        .sum(0)
        .transpose(1, 0, 2)
        .reshape(6, 1, D)
    )
    shift_attn, scale_attn, gate_attn, shift_feed, scale_feed, gate_feed = modulation
    token_rows = jnp.concatenate([modulation.reshape(6, D), out_bias_all, fc2_bias_all], 0)

    top = top + grid.gather_last(*top, grid.orders[0])
    low = low + grid.gather_last(*low, grid.orders[1])
    if local_heads % 2 == 0:
        qkv_w, out_w = assemble(top, low, qkv_width, out_width)
    else:
        attn_top = {**split_columns(top[0], top[1]), **split_columns(top[2], top[3])}
        attn_low = {**split_columns(low[0], low[1]), **split_columns(low[2], low[3])}
        attn_blocks = [jnp.concatenate([attn_top[i], attn_low[i]], 0) for i in range(chips)]
        qkv_w = (
            jnp.stack([b[:, :qkv_width] for b in attn_blocks], 1)
            .reshape(D, pairs, 2, 3, HD)
            .transpose(0, 1, 3, 2, 4)
            .reshape(D, pairs * 3 * PAIR)
        )
        out_w = jnp.concatenate([b[:, qkv_width:] for b in attn_blocks], 1)

    fc1_bias_rel = grid.to_relative(fc1_bias_all).reshape(1, chips * local_units)
    qv_rel = grid.to_relative(qv_bias_all).reshape(pairs, 2, 2, HD).transpose(0, 2, 1, 3)
    qkv_bias_rel = jnp.concatenate(
        [qv_rel[:, :1], jnp.zeros_like(qv_rel[:, :1]), qv_rel[:, 1:]], 1
    ).reshape(1, pairs * 3 * PAIR)

    def both(mine):
        return (mine, grid.swap_core(mine))

    def own_total(lefts, weights):
        mine, theirs = rows_total(lefts, weights)
        return mine, grid.swap_core(theirs)

    def sum_rows(parts):
        return lax.psum_scatter(parts, "row", scatter_dimension=0, tiled=True)

    resid = tokens.astype(F32)
    normed_attn, _ = normalize(resid)
    hidden_attn = both((normed_attn * (1.0 + scale_attn) + shift_attn).astype(BF16))
    grad_feed_low = both((cotangent.astype(F32) * gate_feed).astype(BF16))

    (projected,) = rows_product(hidden_attn, [(qkv_w, 0, qkv_w.shape[1])], qkv_bias_rel, "bias")
    unit_half = local_units // 2

    def units_early(held, earlier, late):
        held = after(held, *earlier)
        parts = (held[:, :unit_half], held[:, unit_half:])
        return [grid.gather_early(part, order, late) for part, order in zip(parts, grid.orders)]

    def units_last(early, *earlier):
        return [
            grid.gather_last(after(held, *earlier), ids, order)
            for (held, ids), order in zip(early, grid.orders)
        ]

    def unit_pieces(early, last):
        found = [{**pieces_of(*e, unit_half), **pieces_of(*l, unit_half)} for e, l in zip(early, last)]
        return [found[part][i] for i in range(chips) for part in range(2)]

    fc1_early = units_early(fc1_rows, (top[2], low[2]), (projected,))
    fc1_last = units_last(fc1_early)
    fc1_got_last = [got for got, _ in fc1_last]
    projected = after(projected, *[held for held, _ in fc1_early])
    middle_pair = pairs // 2
    first_half = attend(projected, latents, pairs, 0, middle_pair)
    fc2_early = units_early(fc2_rows, (first_half[0], *fc1_got_last), ())
    mixed, log_totals = attend(
        after(projected, first_half[0], *fc1_got_last),
        latents,
        pairs,
        middle_pair,
        pairs - middle_pair,
        first_half,
    )
    fc2_last = units_last(fc2_early, mixed)
    mixed = after(mixed, *[held for held, _ in fc2_early])
    fc1_all = unit_pieces(fc1_early, fc1_last)
    fc2_all = unit_pieces(fc2_early, fc2_last)
    order1 = grid.orders[0]
    out_all = [(out_w, 0, out_w.shape[1])]
    totals = own_total([mixed], out_all)
    attention_out, hidden_feed = token_kernel(
        middle_body,
        [*totals, tokens],
        token_rows,
        [F32, BF16],
        0,
        "middle",
    )
    hidden_feed = both(hidden_feed)
    acts, slopes = rows_product(hidden_feed, fc1_all, fc1_bias_rel, "gelu")
    acts = after(acts, *[got for got, _ in fc2_last])

    def send_units(left, right, orders):
        count = len(orders)
        outs = [
            [count * (order[-1] ^ i) + part for i in grid.early_ids(order)]
            for part, order in enumerate(orders)
        ]
        sent = columns_product(left, right, [], outs, local_units // count)
        return [grid.swap_chip(a, order[-1]) for a, order in zip(sent, orders)], sent[0]

    def keep_units(left, right, got, orders):
        count = len(orders)
        outs = []
        for part, order in enumerate(orders):
            places = [count * i + part for i in grid.early_ids(order)]
            outs += [places[: len(places) // 2], places[len(places) // 2 :]]
        return columns_product(left, right, got, outs, local_units // count)

    def sum_chips(kept, orders, late):
        sums = [
            grid.scatter_chips(kept[2 * part], kept[2 * part + 1], order, late)
            for part, order in enumerate(orders)
        ]
        return jnp.concatenate(sums, 1).astype(BF16)

    fc2_got, fc2_sent = send_units(grad_feed_low, acts, grid.orders)
    grad_pre, bias_fc1 = rows_product(
        (after(grad_feed_low[0], fc2_sent), grad_feed_low[1]), fc2_all, slopes, "slope"
    )
    fc1_got, sent = send_units(hidden_feed, grad_pre, [order1])
    totals = own_total([after(grad_pre, sent, *fc2_got)], fc1_all)
    fc2_kept = keep_units(grad_feed_low, after(acts, totals[0]), fc2_got, grid.orders)
    grad_resid_mid, grad_attention_low, middle_sums = token_kernel(
        middle_back_body,
        [after(totals[0], fc2_kept[0]), totals[1], cotangent, tokens, attention_out],
        token_rows,
        [F32, BF16],
        4,
        "middle_back",
    )
    grad_attention_low = both(grad_attention_low)

    (grad_mixed,) = rows_product(
        grad_attention_low, out_all, jnp.zeros((1, out_w.shape[1]), F32), "bias"
    )
    (grad_out,) = columns_product(
        grad_attention_low, after(mixed, grad_mixed), [], [[0]], mixed.shape[1]
    )
    grad_mixed = after(grad_mixed, grad_out)
    grad_late, bias_late = attend_back(
        projected, mixed, grad_mixed, log_totals, latents, 1, pairs - 1
    )
    fc2_sums = sum_chips(fc2_kept, grid.orders, (grad_late,))
    fc1_kept = keep_units(hidden_feed, after(grad_pre, grad_late), fc1_got, [order1])
    late_chips = chips * (pairs - 1) // pairs
    qkv_late = columns_product(
        hidden_attn, grad_late, [], [[i] for i in range(late_chips)], qkv_width
    ) if (
        local_heads % 2 == 0
    ) else None
    early_input = after(grad_mixed, grad_late, fc2_sums, fc1_kept[0])
    grad_early, bias_early = attend_back(
        projected, mixed, early_input, log_totals, latents, 0, 1
    )
    fc1_sums = sum_chips(fc1_kept, [order1], (grad_early,))
    fc2_part = sum_rows(fc2_sums)
    fc1_part = sum_rows(fc1_sums)
    bias_qkv = jnp.concatenate([bias_early, bias_late], 1).sum((0, 2))
    if local_heads % 2 == 0:
        qkv_early = columns_product(hidden_attn, grad_early, [], [[0]], qkv_width)
        grad_qkv = [*qkv_early, *qkv_late]
    else:
        grad_projected = jnp.concatenate([grad_early, grad_late], 1)
        (grad_qkv,) = columns_product(
            hidden_attn, grad_projected, [], [[0]], 3 * PAIR * pairs
        )
        grad_qkv = (
            grad_qkv.reshape(D, pairs, 3, 2, HD).transpose(0, 1, 3, 2, 4).reshape(D, chips, qkv_width)
        )
        grad_qkv = [grad_qkv[:, i] for i in range(chips)]

    def pick(part, ids):
        lines = slice(0, half) if part == 0 else slice(half, D)
        return jnp.concatenate(
            [
                array
                for i in ids
                for array in (
                    grad_qkv[i][lines],
                    grad_out[lines, i * out_width : (i + 1) * out_width],
                )
            ],
            1,
        )

    attn_got = [
        grid.swap_chip(pick(number, gathered[3]), grid.orders[number][-1])
        for number, gathered in enumerate((top, low))
    ]
    attn_sums = []
    for number, gathered in enumerate((top, low)):
        order = grid.orders[number]
        kept = pick(number, gathered[1]).astype(F32) + attn_got[number].astype(F32)
        middle = kept.shape[1] // 2
        attn_sums.append(
            grid.scatter_chips(kept[:, :middle], kept[:, middle:].astype(BF16), order)
        )
    attn_part = grid.scatter_rows(jnp.concatenate(attn_sums, 0).astype(BF16))
    qkv_part = attn_part[:, :qkv_width]
    if local_heads % 2 == 0:
        qkv_part = qkv_part.reshape(row_width, local_heads // 2, 3, 2, HD).transpose(0, 1, 3, 2, 4)
    qkv_part = qkv_part.reshape(row_width, local_heads, 3 * HD)
    out_part = attn_part[:, qkv_width:].T.reshape(local_heads, HD, row_width)

    totals = own_total([after(grad_early, *attn_got), grad_late], [(qkv_w, 0, qkv_w.shape[1])])
    tokens_grad, first_sums = token_kernel(
        first_back_body, [*totals, tokens, grad_resid_mid], token_rows, [F32], 2, "first_back"
    )
    totals = own_total([after(acts, totals[0], fc2_part, *attn_sums)], fc2_all)
    layer_out, last_sums = token_kernel(
        last_body, [after(totals[0], fc1_part), totals[1], tokens, attention_out, cotangent], token_rows, [BF16], 2, "last"
    )

    first_sums, middle_sums, last_sums = (
        sums.sum(1) for sums in (first_sums, middle_sums, last_sums)
    )
    mod_rows = jnp.concatenate(
        [first_sums, middle_sums[2:3], middle_sums[:2], last_sums[:1], middle_sums[3:], last_sums[1:]]
    )
    mod_rows = mod_rows.reshape(8, cols, col_width).transpose(1, 0, 2)
    fc1_rel = bias_fc1.sum(0).reshape(chips, local_units)
    qkv_rel = bias_qkv.reshape(pairs, 3, 2, HD)
    qv_rel = jnp.stack([qkv_rel[:, 0], qkv_rel[:, 2]], 2).reshape(chips, local_heads * PAIR)
    hidden_rows = grid.to_absolute(jnp.concatenate([fc1_rel, qv_rel], 1)).reshape(
        cols, -1, col_width
    )
    pieces = jnp.concatenate([mod_rows, hidden_rows], 1)
    pieces = jnp.broadcast_to(pieces[None], (rows,) + pieces.shape).reshape(
        devices, -1, col_width
    )
    arrived = all_exchange(pieces)
    grad_modulation = arrived[:, :6].reshape(seqs, span, 6, col_width).sum(1)
    sums = arrived[:, 6:].sum(0)
    out_bias_grad = sums[0]
    fc2_bias_grad = sums[1]
    hidden_sums = sums[2:].reshape(-1)
    fc1_bias_grad = hidden_sums[:local_units]
    qv_bias_grad = hidden_sums[local_units:].reshape(local_heads, PAIR)
    mod_bias_grad = jnp.sum(grad_modulation, 0)
    grad_mod_flat = grad_modulation.reshape(seqs, 6 * col_width)
    mod_part_grad = lax.dot_general(
        cond_act.astype(F32), grad_mod_flat, TN, precision=PRECISE, preferred_element_type=F32
    ).reshape(row_width, 6, col_width)
    cond_part = lax.dot_general(
        grad_mod_flat,
        mod_flat.astype(F32),
        NT,
        precision=PRECISE,
        preferred_element_type=F32,
    )
    cond_pieces = lax.dynamic_update_slice_in_dim(
        jnp.zeros((seqs, D), F32), cond_part, grid.row * row_width, 1
    )
    cond_pieces = (
        cond_pieces.reshape(rows, seq_rows, cols, col_width)
        .transpose(0, 2, 1, 3)
        .reshape(devices, seq_rows, col_width)
    )
    grad_cond_act = all_exchange(cond_pieces).sum(0)
    _, silu_pull = jax.vjp(silu_fn, condition.astype(F32))
    condition_grad = silu_pull(grad_cond_act)[0]
    return (
        layer_out,
        tokens_grad,
        condition_grad,
        mod_part_grad,
        mod_bias_grad,
        qkv_part,
        qv_bias_grad,
        out_part,
        out_bias_grad,
        fc1_part.astype(F32),
        fc1_bias_grad,
        fc2_part.astype(F32).T,
        fc2_bias_grad,
    )


def solution(mesh):
    return jax.shard_map(
        per_device,
        mesh=mesh,
        in_specs=(
            P(("row", "col"), None),
            P("row", "col"),
            P("row", None, "col"),
            P(None, "col"),
            P("row", "col", None),
            P("col", None),
            P("col", None, "row"),
            P("col"),
            P("row", "col"),
            P("col"),
            P("col", "row"),
            P("col"),
            P(("row", "col"), None),
        ),
        out_specs=(
            P(("row", "col"), None),
            P(("row", "col"), None),
            P("row", "col"),
            P("row", None, "col"),
            P(None, "col"),
            P("row", "col", None),
            P("col", None),
            P("col", None, "row"),
            P("col"),
            P("row", "col"),
            P("col"),
            P("col", "row"),
            P("col"),
        ),
        check_vma=False,
    )
```

```python
import functools
import math

import jax
import jax.numpy as jnp
from jax import lax
from jax.experimental import pallas as pl
from jax.experimental.pallas import tpu as pltpu
from jax.sharding import PartitionSpec as P

D = 1024
HD = 64
LEN = 1024
PAIR = 2 * HD

EPSILON = 1e-06
PRECISE = lax.Precision.HIGHEST
NN = (((1,), (0,)), ((), ()))
NT = (((1,), (1,)), ((), ()))
TN = (((0,), (0,)), ((), ()))
F32 = jnp.float32
BF16 = jnp.bfloat16
QUERY_ROWS = 512
TOKEN_ROWS = 32
VMEM_NEEDS = {
    "attend": 14,
    "attend_back": 20,
    "tokens": 14,
    "rows": 26,
    "rows_total": 20,
    "columns_product": 26,
    "assemble": 12,
}
SMALL_COST = pl.CostEstimate(flops=1000, bytes_accessed=1000, transcendentals=0)


def vmem_of(need):
    return VMEM_NEEDS[need] * 1024 * 1024


def dot(left, right, dims=NN):
    return lax.dot_general(left, right, dims, preferred_element_type=F32)


def silu_fn(values):
    return values * jax.nn.sigmoid(values)


def gelu_both(values):
    c = math.sqrt(2.0 / math.pi)
    square = values * values
    half = 0.5 + 0.5 * jnp.tanh(values * (c + (c * 0.044715) * square))
    gelu = values * half
    slope = half + gelu * (1.0 - half) * (2.0 * c + (6.0 * c * 0.044715) * square)
    return gelu, slope


def normalize(resid):
    average = jnp.mean(resid, 1, keepdims=True)
    spread = jnp.mean(resid * resid, 1, keepdims=True) - average * average
    inv_std = lax.rsqrt(spread + EPSILON)
    return ((resid - average) * inv_std, inv_std)


def normalize_back(grad_norm, normed, inv_std):
    average = jnp.mean(grad_norm, 1, keepdims=True)
    crossed = jnp.mean(grad_norm * normed, 1, keepdims=True)
    return inv_std * (grad_norm - average - normed * crossed)


def after(array, *earlier):
    return lax.optimization_barrier((array, *earlier))[0]


def head_lanes(shape, head):
    lane = lax.broadcasted_iota(jnp.int32, shape, 1)
    return lane < HD if head == 0 else lane >= HD


def attend_kernel(q_ref, k_ref, v_ref, *refs):
    mixed_ref, log_ref = refs[-2:]
    queries = q_ref[...] * jnp.asarray(HD**-0.5, BF16)
    key_rows = k_ref[...]
    values_across = v_ref[...].T
    mask = head_lanes(key_rows.shape, 0)
    zero = jnp.zeros_like(key_rows)
    keys = (jnp.where(mask, key_rows, zero), jnp.where(mask, zero, key_rows))
    length = queries.shape[0]
    for start in range(0, length, QUERY_ROWS):
        stop = start + QUERY_ROWS
        q_part = queries[start:stop]
        outs = []
        for head in range(2):
            scores = dot(keys[head], q_part, NT)
            top = jnp.max(scores, 0, keepdims=True)
            expon = jnp.exp(scores - top)
            total = jnp.sum(expon, 0, keepdims=True)
            out = dot(values_across[head * HD : (head + 1) * HD], expon.astype(BF16))
            outs.append(out / total)
            log_ref[0, 0, head : head + 1, start:stop] = top + jnp.log(total)
        mixed_ref[start:stop, :] = jnp.concatenate(outs, 0).T.astype(BF16)


def attend_back_kernel(q_ref, k_ref, v_ref, mixed_ref, grad_ref, log_ref, out_ref, sums_ref):
    scale = jnp.asarray(HD**-0.5, BF16)
    queries = q_ref[...] * scale
    key_rows = k_ref[...]
    value_rows = v_ref[...]
    grad_rows = grad_ref[...]
    mask = head_lanes(value_rows.shape, 0)
    zero = jnp.zeros_like(value_rows)
    keys = (jnp.where(mask, key_rows, zero), jnp.where(mask, zero, key_rows))
    values = (jnp.where(mask, value_rows, zero), jnp.where(mask, zero, value_rows))
    keys_across = (key_rows * scale).T
    product = grad_rows.astype(F32) * mixed_ref[...].astype(F32)
    picks = (
        lax.broadcasted_iota(jnp.int32, (8, PAIR), 0)
        == lax.broadcasted_iota(jnp.int32, (8, PAIR), 1) // HD
    ).astype(F32)
    inner = lax.dot_general(picks, product, NT, precision=PRECISE, preferred_element_type=F32)
    length = queries.shape[0]
    grad_k = [None, None]
    grad_v = [None, None]
    for start in range(0, length, QUERY_ROWS):
        stop = start + QUERY_ROWS
        q_part = queries[start:stop]
        g_part = grad_rows[start:stop]
        outs = []
        for head in range(2):
            scores = dot(keys[head], q_part, NT)
            probs = jnp.exp(scores - log_ref[0, 0, head : head + 1, start:stop])
            grad_probs = dot(values[head], g_part, NT)
            grad_scores = (probs * (grad_probs - inner[head : head + 1, start:stop])).astype(BF16)
            part_v = dot(probs.astype(BF16), g_part)
            part_k = dot(grad_scores, q_part)
            grad_v[head] = part_v if grad_v[head] is None else grad_v[head] + part_v
            grad_k[head] = part_k if grad_k[head] is None else grad_k[head] + part_k
            outs.append(dot(keys_across[head * HD : (head + 1) * HD], grad_scores))
        out_ref[start:stop, 0:PAIR] = jnp.concatenate(outs, 0).T.astype(BF16)
    out_ref[:, PAIR : 2 * PAIR] = jnp.where(mask, grad_k[0], grad_k[1]).astype(BF16)
    out_ref[:, 2 * PAIR :] = jnp.where(mask, grad_v[0], grad_v[1]).astype(BF16)
    sums_ref[0, 0] = jnp.sum(out_ref[...].astype(F32).reshape(length // 8, 8, 3 * PAIR), 0)


def attention_specs(first):
    part = lambda offset: pl.BlockSpec((LEN, PAIR), lambda s, p: (s, 3 * (p + first) + offset))
    plain = pl.BlockSpec((LEN, PAIR), lambda s, p: (s, p + first))
    logs = pl.BlockSpec((1, 1, 2, LEN), lambda s, p: (s, p + first, 0, 0))
    return [part(0), part(1), part(2)], plain, logs


def attend(projected, latents, pairs, first, count, earlier=()):
    parts, plain, logs = attention_specs(first)
    rows = projected.shape[0]
    return pl.pallas_call(
        attend_kernel,
        grid=(latents, count),
        in_specs=parts + [pl.BlockSpec(memory_space=pl.ANY)] * len(earlier),
        out_specs=[plain, logs],
        out_shape=[
            jax.ShapeDtypeStruct((rows, pairs * PAIR), BF16),
            jax.ShapeDtypeStruct((latents, pairs, 2, LEN), F32),
        ],
        input_output_aliases={3 + i: i for i in range(len(earlier))},
        compiler_params=pltpu.CompilerParams(vmem_limit_bytes=vmem_of("attend")),
        cost_estimate=SMALL_COST,
        name="attend",
    )(projected, projected, projected, *earlier)


def attend_back(projected, mixed, grad_mixed, log_totals, latents, first, count):
    parts, plain, logs = attention_specs(first)
    rows = projected.shape[0]
    return pl.pallas_call(
        attend_back_kernel,
        grid=(latents, count),
        in_specs=[*parts, plain, plain, logs],
        out_specs=[
            pl.BlockSpec((LEN, 3 * PAIR), lambda s, p: (s, p)),
            pl.BlockSpec((1, 1, 8, 3 * PAIR), lambda s, p: (s, p, 0, 0)),
        ],
        out_shape=[
            jax.ShapeDtypeStruct((rows, count * 3 * PAIR), BF16),
            jax.ShapeDtypeStruct((latents, count, 8, 3 * PAIR), F32),
        ],
        compiler_params=pltpu.CompilerParams(vmem_limit_bytes=vmem_of("attend_back")),
        cost_estimate=SMALL_COST,
        name="attend_back",
    )(projected, projected, projected, mixed, grad_mixed, log_totals)


def kernel_call(body, grid, in_specs, out_specs, out_shape, name, need):
    return pl.pallas_call(
        body,
        grid=grid,
        in_specs=in_specs,
        out_specs=out_specs,
        out_shape=out_shape,
        compiler_params=pltpu.CompilerParams(vmem_limit_bytes=vmem_of(need)),
        cost_estimate=SMALL_COST,
        name=name,
    )


def whole(array):
    return pl.BlockSpec(array.shape, lambda *step: (0,) * array.ndim)


def pieces_of(array, ids, width):
    return {i: (array, place, width) for place, i in enumerate(ids)}


def piece_spec(piece):
    array, block, width = piece
    return pl.BlockSpec((array.shape[0], width), lambda *step: (0, block))


def row_specs(local_rows, tile, width):
    count = local_rows // tile
    mine = pl.BlockSpec((tile, width), lambda i: (jnp.minimum(i, count - 1), 0))
    theirs = pl.BlockSpec((tile, width), lambda i: (jnp.maximum(i - count, 0), 0))
    return count, mine, theirs


def rows_product(pair, weights, extra, kind):
    local_rows, depth = pair[0].shape
    tile = min(512, local_rows)
    count, mine, theirs = row_specs(local_rows, tile, depth)
    widths = [piece[2] for piece in weights]
    width = sum(widths)
    total = 2 * local_rows

    def body(*refs):
        mine_ref, theirs_ref = refs[:2]
        weight_refs = refs[2 : 2 + len(weights)]
        extra_ref = refs[2 + len(weights)]
        out_refs = refs[3 + len(weights) :]
        step = pl.program_id(0)
        left = jnp.where(step < count, mine_ref[...], theirs_ref[...])
        if kind == "slope":

            @pl.when(step == 0)
            def _():
                out_refs[1][...] = jnp.zeros(out_refs[1].shape, F32)

        start = 0
        for ref, span in zip(weight_refs, widths):
            step_width = min(256, span)
            for low in range(0, span, step_width):
                cols = slice(start + low, start + low + step_width)
                product = dot(left, ref[:, low : low + step_width])
                if kind == "bias":
                    out_refs[0][:, cols] = (product + extra_ref[:, cols]).astype(BF16)
                elif kind == "gelu":
                    act, slope = gelu_both(product + extra_ref[:, cols])
                    out_refs[0][:, cols] = act.astype(BF16)
                    out_refs[1][:, cols] = slope.astype(BF16)
                else:
                    grad = (product * extra_ref[:, cols].astype(F32)).astype(BF16)
                    out_refs[0][:, cols] = grad
                    out_refs[1][:, cols] += jnp.sum(
                        grad.astype(F32).reshape(tile // 8, 8, step_width), 0
                    )
            start += span

    rows_out = pl.BlockSpec((tile, width), lambda i: (i, 0))
    low_shape = jax.ShapeDtypeStruct((total, width), BF16)
    if kind == "bias":
        out_specs, out_shape = [rows_out], [low_shape]
    elif kind == "gelu":
        out_specs, out_shape = [rows_out, rows_out], [low_shape, low_shape]
    else:
        out_specs = [rows_out, pl.BlockSpec((8, width), lambda i: (0, 0))]
        out_shape = [low_shape, jax.ShapeDtypeStruct((8, width), F32)]
    extra_spec = rows_out if kind == "slope" else whole(extra)
    return kernel_call(
        body,
        (2 * count,),
        [mine, theirs, *[piece_spec(w) for w in weights], extra_spec],
        out_specs,
        out_shape,
        "rows_" + kind,
        "rows",
    )(*pair, *[w[0] for w in weights], extra)


def columns_of(refs, start, stop):
    for ref in refs:
        if start < ref.shape[1]:
            return ref[:, start:stop]
        start, stop = start - ref.shape[1], stop - ref.shape[1]


def rows_total(lefts, weights):
    local_rows = lefts[0].shape[0] // 2
    tile = min(512, local_rows)
    count = local_rows // tile
    width = weights[0][0].shape[0]
    ends = set()
    for spans in ([a.shape[1] for a in lefts], [w[2] for w in weights]):
        end = 0
        for span in spans:
            end += span
            ends.add(end)
    ends = sorted(ends)

    def body(*refs):
        left_refs = refs[: len(lefts)]
        weight_refs = refs[len(lefts) : -2]
        mine_ref, theirs_ref = refs[-2:]
        total = None
        for start, stop in zip([0] + ends, ends):
            part = dot(columns_of(left_refs, start, stop), columns_of(weight_refs, start, stop), NT)
            total = part if total is None else total + part
        step = pl.program_id(0)

        @pl.when(step < count)
        def _():
            mine_ref[...] = total

        @pl.when(step >= count)
        def _():
            theirs_ref[...] = total.astype(BF16)

    return kernel_call(
        body,
        (2 * count,),
        [pl.BlockSpec((tile, a.shape[1]), lambda i: (i, 0)) for a in lefts]
        + [piece_spec(w) for w in weights],
        [
            pl.BlockSpec((tile, width), lambda i: (jnp.minimum(i, count - 1), 0)),
            pl.BlockSpec((tile, width), lambda i: (jnp.maximum(i - count, 0), 0)),
        ],
        [
            jax.ShapeDtypeStruct((local_rows, width), F32),
            jax.ShapeDtypeStruct((local_rows, width), BF16),
        ],
        "rows_total",
        "rows_total",
    )(*lefts, *[w[0] for w in weights])


def token_kernel(body, arrays, rows_of, out_types, sums, name):
    tokens = arrays[0].shape[0]
    tile = min(256, tokens)
    outs = len(out_types)

    def kernel(*refs):
        rows_ref = refs[len(arrays)]
        out_refs = refs[len(arrays) + 1 :]
        rows = [rows_ref[i : i + 1, :] for i in range(8)]
        if sums:
            sum_ref = out_refs[outs]

            @pl.when(pl.program_id(0) == 0)
            def _():
                sum_ref[...] = jnp.zeros(sum_ref.shape, F32)

        for start in range(0, tile, TOKEN_ROWS):
            lines = slice(start, start + TOKEN_ROWS)
            values = [ref[lines, :].astype(F32) for ref in refs[: len(arrays)]]
            results, columns = body(values, rows)
            for ref, result in zip(out_refs, results):
                ref[lines, :] = result.astype(ref.dtype)
            for i, column in enumerate(columns):
                sum_ref[i] += jnp.sum(column.reshape(TOKEN_ROWS // 8, 8, D), 0)

    tokens_spec = pl.BlockSpec((tile, D), lambda i: (i, 0))
    out_specs = [tokens_spec] * outs
    out_shape = [jax.ShapeDtypeStruct((tokens, D), t) for t in out_types]
    if sums:
        out_specs = out_specs + [pl.BlockSpec((sums, 8, D), lambda i: (0, 0, 0))]
        out_shape = out_shape + [jax.ShapeDtypeStruct((sums, 8, D), F32)]
    return kernel_call(
        kernel,
        (tokens // tile,),
        [tokens_spec] * len(arrays) + [whole(rows_of)],
        out_specs,
        out_shape,
        name,
        "tokens",
    )(*arrays, rows_of)


def middle_body(values, rows):
    mine, theirs, tokens = values
    gate, shift, scale, bias = rows[2], rows[3], rows[4], rows[6]
    attention_out = mine + theirs + bias
    normed, _ = normalize(tokens + gate * attention_out)
    return [attention_out, normed * (1.0 + scale) + shift], []


def middle_back_body(values, rows):
    mine, theirs, upstream, tokens, attention_out = values
    gate, scale = rows[2], rows[4]
    grad_hidden = mine + theirs
    normed, inv_std = normalize(tokens + gate * attention_out)
    grad = upstream + normalize_back(grad_hidden * (1.0 + scale), normed, inv_std)
    grad_attention = grad * gate
    return [grad, grad_attention], [
        grad_hidden,
        grad_hidden * normed,
        grad * attention_out,
        grad_attention,
    ]


def first_back_body(values, rows):
    mine, theirs, tokens, grad_resid = values
    scale = rows[1]
    grad_hidden = mine + theirs
    normed, inv_std = normalize(tokens)
    grad = grad_resid + normalize_back(grad_hidden * (1.0 + scale), normed, inv_std)
    return [grad], [grad_hidden, grad_hidden * normed]


def last_body(values, rows):
    mine, theirs, tokens, attention_out, upstream = values
    gate_attn, gate_feed, bias = rows[2], rows[5], rows[7]
    feed_out = mine + theirs + bias
    resid_mid = tokens + gate_attn * attention_out
    return [resid_mid + gate_feed * feed_out], [upstream * feed_out, upstream * gate_feed]


def columns_product(pair, right, added, outs, width):
    local_rows, depth = pair[0].shape
    rows = right.shape[0]
    tile = 256
    blocks = [i for ids in outs for i in ids]
    extra = list(added)
    per_extra = len(blocks) // max(1, len(extra))

    def body(mine_ref, theirs_ref, *refs):
        right_refs = refs[: len(blocks)]
        add_refs = refs[len(blocks) : len(blocks) + len(extra)]
        out_refs = refs[len(blocks) + len(extra) :]
        mine, theirs = mine_ref[...].T, theirs_ref[...].T
        number = 0
        for ref, ids in zip(out_refs, outs):
            for place in range(len(ids)):
                total = dot(mine, right_refs[number][:local_rows])
                total = total + dot(theirs, right_refs[number][local_rows:])
                if extra:
                    start = number % per_extra * width
                    part = add_refs[number // per_extra][:, start : start + width]
                    total = total + part.astype(F32)
                ref[:, place * width : (place + 1) * width] = total.astype(BF16)
                number += 1

    token_spec = pl.BlockSpec((local_rows, tile), lambda i: (0, i))

    def out_spec(count):
        return pl.BlockSpec((tile, count * width), lambda i: (i, 0))

    return kernel_call(
        body,
        (depth // tile,),
        [token_spec, token_spec]
        + [pl.BlockSpec((rows, width), lambda i, b=b: (0, b)) for b in blocks]
        + [out_spec(per_extra) for _ in extra],
        [out_spec(len(ids)) for ids in outs],
        [jax.ShapeDtypeStruct((depth, len(ids) * width), BF16) for ids in outs],
        "columns_product",
        "columns_product",
    )(*pair, *[right] * len(blocks), *extra)


def assemble(top, low, qkv_width, out_width):
    parts = [top[0], top[2], low[0], low[2]]
    ids = [top[1], top[3], low[1], low[3]]
    half, width = parts[0].shape
    block = qkv_width + out_width
    blocks = 2 * width // block
    tile = 128

    def body(a_ref, b_ref, c_ref, d_ref, qkv_ref, out_ref):
        for number, ref in enumerate((a_ref, b_ref, c_ref, d_ref)):
            for place, i in enumerate(ids[number]):
                start = place * block
                qkv_ref[number // 2, :, i * qkv_width : (i + 1) * qkv_width] = ref[
                    :, start : start + qkv_width
                ]
                out_ref[number // 2, :, i * out_width : (i + 1) * out_width] = ref[
                    :, start + qkv_width : start + block
                ]

    qkv, out = kernel_call(
        body,
        (half // tile,),
        [pl.BlockSpec((tile, width), lambda i: (i, 0))] * 4,
        [
            pl.BlockSpec((2, tile, blocks * qkv_width), lambda i: (0, i, 0)),
            pl.BlockSpec((2, tile, blocks * out_width), lambda i: (0, i, 0)),
        ],
        [
            jax.ShapeDtypeStruct((2, half, blocks * qkv_width), BF16),
            jax.ShapeDtypeStruct((2, half, blocks * out_width), BF16),
        ],
        "assemble",
        "assemble",
    )(*parts)
    return qkv.reshape(2 * half, -1), out.reshape(2 * half, -1)


class Grid:
    def __init__(self):
        self.rows = lax.axis_size("row")
        self.cols = lax.axis_size("col")
        self.chips = self.cols // 2
        self.bits = [1 << b for b in range(self.chips.bit_length() - 1)]
        self.orders = (self.bits, self.bits[::-1])
        self.row = lax.axis_index("row")
        self.col = lax.axis_index("col")
        self.core = self.col % 2
        source = lax.iota(jnp.int32, self.chips) ^ (self.col // 2)
        self.choose = (
            (2 * source + self.core)[:, None] == lax.iota(jnp.int32, self.cols)[None, :]
        ).astype(F32)

    def swap(self, array, flip):
        pairs = [(i, i ^ flip) for i in range(self.cols)]
        return lax.ppermute(array, "col", pairs)

    def swap_core(self, array):
        return self.swap(array, 1)

    def swap_chip(self, array, bit):
        return self.swap(array, 2 * bit)

    def to_relative(self, blocks):
        flat = blocks.reshape(self.cols, -1).astype(F32)
        picked = lax.dot_general(
            self.choose, flat, NN, precision=PRECISE, preferred_element_type=F32
        )
        return picked.reshape((self.chips,) + blocks.shape[1:])

    def to_absolute(self, blocks):
        flat = blocks.reshape(self.chips, -1)
        placed = lax.dot_general(
            self.choose, flat, TN, precision=PRECISE, preferred_element_type=F32
        )
        return placed.reshape((self.cols,) + blocks.shape[1:])

    def gather_rows(self, block):
        count = self.rows
        got = [block]
        for step in range(1, count):
            got.append(
                lax.ppermute(block, "row", [(i, (i + step) % count) for i in range(count)])
            )
        stacked = jnp.stack(got)
        ordered = [
            lax.dynamic_index_in_dim(stacked, (self.row - i) % count, 0, keepdims=False)
            for i in range(count)
        ]
        return jnp.concatenate(ordered, 0), got[-1]

    def scatter_rows(self, whole):
        count = self.rows
        blocks = whole.reshape(count, whole.shape[0] // count, whole.shape[1])
        total = lax.dynamic_index_in_dim(blocks, self.row, 0, keepdims=False).astype(F32)
        for step in range(1, count):
            sent = lax.dynamic_index_in_dim(blocks, (self.row + step) % count, 0, keepdims=False)
            total = total + lax.ppermute(
                sent, "row", [(i, (i + step) % count) for i in range(count)]
            ).astype(F32)
        return total

    def gather_early(self, block, order, late=()):
        held, ids = block, [0]
        for bit in order[:-1]:
            got = self.swap_chip(held, bit)
            if bit == order[-2]:
                got = after(got, *late)
            held = jnp.concatenate([held, got], 1)
            ids = ids + [bit ^ i for i in ids]
        return held, ids

    def early_ids(self, order):
        ids = [0]
        for bit in order[:-1]:
            ids = ids + [bit ^ i for i in ids]
        return ids

    def gather_last(self, held, ids, order):
        return self.swap_chip(held, order[-1]), [order[-1] ^ i for i in ids]

    def scatter_chips(self, keep, send, order, late=()):
        for bit in order[-2::-1]:
            got = self.swap_chip(send, bit)
            if bit == order[-2]:
                got = after(got, *late)
            total = keep.astype(F32) + got.astype(F32)
            if bit == order[0]:
                return total
            half = total.shape[1] // 2
            keep, send = total[:, :half], total[:, half:].astype(BF16)


def split_columns(array, ids):
    width = array.shape[1] // len(ids)
    return {i: array[:, n * width : (n + 1) * width] for n, i in enumerate(ids)}


def all_exchange(pieces):
    return lax.all_to_all(pieces, ("row", "col"), 0, 0, tiled=True)


def per_device(
    tokens,
    condition,
    mod_weight,
    mod_bias,
    qkv_weight,
    qv_bias,
    out_weight,
    out_bias,
    fc1_weight,
    fc1_bias,
    fc2_weight,
    fc2_bias,
    cotangent,
):
    grid = Grid()
    rows, cols, chips = grid.rows, grid.cols, grid.chips
    devices = rows * cols
    local_rows = tokens.shape[0]
    both_rows = 2 * local_rows
    latents = both_rows // LEN
    span = LEN // local_rows
    seq_rows = condition.shape[0]
    seqs = seq_rows * rows
    row_width = D // rows
    col_width = D // cols
    local_heads = qkv_weight.shape[1]
    local_units = fc1_weight.shape[1]
    plane_heads = local_heads * chips
    pairs = plane_heads // 2
    qkv_width = local_heads * 3 * HD
    out_width = local_heads * HD

    if local_heads % 2 == 0:
        qkv_local = (
            qkv_weight.reshape(row_width, local_heads // 2, 2, 3, HD)
            .transpose(0, 1, 3, 2, 4)
            .reshape(row_width, qkv_width)
        )
    else:
        qkv_local = qkv_weight.reshape(row_width, qkv_width)
    attn_local = jnp.concatenate(
        [qkv_local, out_weight.reshape(out_width, row_width).T], 1
    )
    attn_width = qkv_width + out_width
    fc1_local = fc1_weight
    fc2_local = fc2_weight.T

    small = jnp.concatenate(
        [
            condition.reshape(-1),
            fc1_bias,
            qv_bias.reshape(-1),
            out_bias,
            fc2_bias,
        ]
    )
    small_all = all_exchange(
        jnp.broadcast_to(small.reshape(1, -1, 128), (devices, small.size // 128, 128))
    )

    attn_rows, mark = grid.gather_rows(attn_local)
    fc1_rows = lax.all_gather(after(fc1_local, mark), "row", axis=0, tiled=True)
    fc2_rows = lax.all_gather(after(fc2_local, fc1_rows), "row", axis=0, tiled=True)
    half = D // 2
    top = grid.gather_early(attn_rows[:half], grid.orders[0])
    low = grid.gather_early(attn_rows[half:], grid.orders[1])
    small_all = small_all.reshape(rows, cols, -1)
    cut = seq_rows * col_width
    cond_all = (
        small_all[:, :, :cut]
        .reshape(rows, cols, seq_rows, col_width)
        .transpose(0, 2, 1, 3)
        .reshape(seqs, D)
    )
    biases = small_all[0, :, cut:]
    fc1_bias_all = biases[:, :local_units]
    qv_bias_all = biases[:, local_units : local_units + local_heads * PAIR]
    out_bias_all = biases[:, -2 * col_width : -col_width].reshape(1, D).astype(F32)
    fc2_bias_all = biases[:, -col_width:].reshape(1, D).astype(F32)

    cond_act = silu_fn(cond_all.astype(F32)).astype(BF16)
    cond_act = lax.dynamic_slice_in_dim(cond_act, grid.row * row_width, row_width, 1)
    mod_flat = mod_weight.reshape(row_width, 6 * col_width)
    own_bias = jnp.where(grid.row == 0, mod_bias.astype(F32), 0.0)
    mod_part = dot(cond_act, mod_flat).reshape(seqs, 6, col_width) + own_bias
    mod_part = jnp.broadcast_to(
        mod_part[:, None], (seqs, span, 6, col_width)
    ).reshape(devices, 6, col_width)
    modulation = (
        all_exchange(mod_part)
        .reshape(rows, cols, 6, col_width)
        .sum(0)
        .transpose(1, 0, 2)
        .reshape(6, 1, D)
    )
    shift_attn, scale_attn, gate_attn, shift_feed, scale_feed, gate_feed = modulation
    token_rows = jnp.concatenate([modulation.reshape(6, D), out_bias_all, fc2_bias_all], 0)

    top = top + grid.gather_last(*top, grid.orders[0])
    low = low + grid.gather_last(*low, grid.orders[1])
    if local_heads % 2 == 0:
        qkv_w, out_w = assemble(top, low, qkv_width, out_width)
    else:
        attn_top = {**split_columns(top[0], top[1]), **split_columns(top[2], top[3])}
        attn_low = {**split_columns(low[0], low[1]), **split_columns(low[2], low[3])}
        attn_blocks = [jnp.concatenate([attn_top[i], attn_low[i]], 0) for i in range(chips)]
        qkv_w = (
            jnp.stack([b[:, :qkv_width] for b in attn_blocks], 1)
            .reshape(D, pairs, 2, 3, HD)
            .transpose(0, 1, 3, 2, 4)
            .reshape(D, pairs * 3 * PAIR)
        )
        out_w = jnp.concatenate([b[:, qkv_width:] for b in attn_blocks], 1)

    fc1_bias_rel = grid.to_relative(fc1_bias_all).reshape(1, chips * local_units)
    qv_rel = grid.to_relative(qv_bias_all).reshape(pairs, 2, 2, HD).transpose(0, 2, 1, 3)
    qkv_bias_rel = jnp.concatenate(
        [qv_rel[:, :1], jnp.zeros_like(qv_rel[:, :1]), qv_rel[:, 1:]], 1
    ).reshape(1, pairs * 3 * PAIR)

    def both(mine):
        return (mine, grid.swap_core(mine))

    def own_total(lefts, weights):
        mine, theirs = rows_total(lefts, weights)
        return mine, grid.swap_core(theirs)

    def sum_rows(parts):
        return lax.psum_scatter(parts, "row", scatter_dimension=0, tiled=True)

    resid = tokens.astype(F32)
    normed_attn, _ = normalize(resid)
    hidden_attn = both((normed_attn * (1.0 + scale_attn) + shift_attn).astype(BF16))
    grad_feed_low = both((cotangent.astype(F32) * gate_feed).astype(BF16))

    (projected,) = rows_product(hidden_attn, [(qkv_w, 0, qkv_w.shape[1])], qkv_bias_rel, "bias")
    unit_half = local_units // 2

    def units_early(held, earlier, late):
        held = after(held, *earlier)
        parts = (held[:, :unit_half], held[:, unit_half:])
        return [grid.gather_early(part, order, late) for part, order in zip(parts, grid.orders)]

    def units_last(early, *earlier):
        return [
            grid.gather_last(after(held, *earlier), ids, order)
            for (held, ids), order in zip(early, grid.orders)
        ]

    def unit_pieces(early, last):
        found = [{**pieces_of(*e, unit_half), **pieces_of(*l, unit_half)} for e, l in zip(early, last)]
        return [found[part][i] for i in range(chips) for part in range(2)]

    fc1_early = units_early(fc1_rows, (top[2], low[2]), (projected,))
    fc1_last = units_last(fc1_early)
    fc1_got_last = [got for got, _ in fc1_last]
    projected = after(projected, *[held for held, _ in fc1_early])
    middle_pair = pairs // 2
    first_half = attend(projected, latents, pairs, 0, middle_pair)
    fc2_early = units_early(fc2_rows, (first_half[0], *fc1_got_last), ())
    mixed, log_totals = attend(
        after(projected, first_half[0], *fc1_got_last),
        latents,
        pairs,
        middle_pair,
        pairs - middle_pair,
        first_half,
    )
    fc2_last = units_last(fc2_early, mixed)
    mixed = after(mixed, *[held for held, _ in fc2_early])
    fc1_all = unit_pieces(fc1_early, fc1_last)
    fc2_all = unit_pieces(fc2_early, fc2_last)
    order1 = grid.orders[0]
    out_all = [(out_w, 0, out_w.shape[1])]
    totals = own_total([mixed], out_all)
    attention_out, hidden_feed = token_kernel(
        middle_body,
        [*totals, tokens],
        token_rows,
        [F32, BF16],
        0,
        "middle",
    )
    hidden_feed = both(hidden_feed)
    acts, slopes = rows_product(hidden_feed, fc1_all, fc1_bias_rel, "gelu")
    acts = after(acts, *[got for got, _ in fc2_last])

    def send_units(left, right, orders):
        count = len(orders)
        outs = [
            [count * (order[-1] ^ i) + part for i in grid.early_ids(order)]
            for part, order in enumerate(orders)
        ]
        sent = columns_product(left, right, [], outs, local_units // count)
        return [grid.swap_chip(a, order[-1]) for a, order in zip(sent, orders)], sent[0]

    def keep_units(left, right, got, orders):
        count = len(orders)
        outs = []
        for part, order in enumerate(orders):
            places = [count * i + part for i in grid.early_ids(order)]
            outs += [places[: len(places) // 2], places[len(places) // 2 :]]
        return columns_product(left, right, got, outs, local_units // count)

    def sum_chips(kept, orders, late):
        sums = [
            grid.scatter_chips(kept[2 * part], kept[2 * part + 1], order, late)
            for part, order in enumerate(orders)
        ]
        return jnp.concatenate(sums, 1).astype(BF16)

    fc2_got, fc2_sent = send_units(grad_feed_low, acts, grid.orders)
    grad_pre, bias_fc1 = rows_product(
        (after(grad_feed_low[0], fc2_sent), grad_feed_low[1]), fc2_all, slopes, "slope"
    )
    fc1_got, sent = send_units(hidden_feed, grad_pre, [order1])
    totals = own_total([after(grad_pre, sent, *fc2_got)], fc1_all)
    fc2_kept = keep_units(grad_feed_low, after(acts, totals[0]), fc2_got, grid.orders)
    grad_resid_mid, grad_attention_low, middle_sums = token_kernel(
        middle_back_body,
        [after(totals[0], fc2_kept[0]), totals[1], cotangent, tokens, attention_out],
        token_rows,
        [F32, BF16],
        4,
        "middle_back",
    )
    grad_attention_low = both(grad_attention_low)

    (grad_mixed,) = rows_product(
        grad_attention_low, out_all, jnp.zeros((1, out_w.shape[1]), F32), "bias"
    )
    (grad_out,) = columns_product(
        grad_attention_low, after(mixed, grad_mixed), [], [[0]], mixed.shape[1]
    )
    grad_mixed = after(grad_mixed, grad_out)
    grad_late, bias_late = attend_back(
        projected, mixed, grad_mixed, log_totals, latents, 1, pairs - 1
    )
    fc2_sums = sum_chips(fc2_kept, grid.orders, (grad_late,))
    fc1_kept = keep_units(hidden_feed, after(grad_pre, grad_late), fc1_got, [order1])
    late_chips = chips * (pairs - 1) // pairs
    qkv_late = columns_product(
        hidden_attn, grad_late, [], [[i] for i in range(late_chips)], qkv_width
    ) if (
        local_heads % 2 == 0
    ) else None
    early_input = after(grad_mixed, grad_late, fc2_sums, fc1_kept[0])
    grad_early, bias_early = attend_back(
        projected, mixed, early_input, log_totals, latents, 0, 1
    )
    fc1_sums = sum_chips(fc1_kept, [order1], (grad_early,))
    fc2_part = sum_rows(fc2_sums)
    fc1_part = sum_rows(fc1_sums)
    bias_qkv = jnp.concatenate([bias_early, bias_late], 1).sum((0, 2))
    if local_heads % 2 == 0:
        qkv_early = columns_product(hidden_attn, grad_early, [], [[0]], qkv_width)
        grad_qkv = [*qkv_early, *qkv_late]
    else:
        grad_projected = jnp.concatenate([grad_early, grad_late], 1)
        (grad_qkv,) = columns_product(
            hidden_attn, grad_projected, [], [[0]], 3 * PAIR * pairs
        )
        grad_qkv = (
            grad_qkv.reshape(D, pairs, 3, 2, HD).transpose(0, 1, 3, 2, 4).reshape(D, chips, qkv_width)
        )
        grad_qkv = [grad_qkv[:, i] for i in range(chips)]

    def pick(part, ids):
        lines = slice(0, half) if part == 0 else slice(half, D)
        return jnp.concatenate(
            [
                array
                for i in ids
                for array in (
                    grad_qkv[i][lines],
                    grad_out[lines, i * out_width : (i + 1) * out_width],
                )
            ],
            1,
        )

    attn_got = [
        grid.swap_chip(pick(number, gathered[3]), grid.orders[number][-1])
        for number, gathered in enumerate((top, low))
    ]
    attn_sums = []
    for number, gathered in enumerate((top, low)):
        order = grid.orders[number]
        kept = pick(number, gathered[1]).astype(F32) + attn_got[number].astype(F32)
        middle = kept.shape[1] // 2
        attn_sums.append(
            grid.scatter_chips(kept[:, :middle], kept[:, middle:].astype(BF16), order)
        )
    attn_part = grid.scatter_rows(jnp.concatenate(attn_sums, 0).astype(BF16))
    qkv_part = attn_part[:, :qkv_width]
    if local_heads % 2 == 0:
        qkv_part = qkv_part.reshape(row_width, local_heads // 2, 3, 2, HD).transpose(0, 1, 3, 2, 4)
    qkv_part = qkv_part.reshape(row_width, local_heads, 3 * HD)
    out_part = attn_part[:, qkv_width:].T.reshape(local_heads, HD, row_width)

    totals = own_total([after(grad_early, *attn_got), grad_late], [(qkv_w, 0, qkv_w.shape[1])])
    tokens_grad, first_sums = token_kernel(
        first_back_body, [*totals, tokens, grad_resid_mid], token_rows, [F32], 2, "first_back"
    )
    totals = own_total([after(acts, totals[0], fc2_part, *attn_sums)], fc2_all)
    layer_out, last_sums = token_kernel(
        last_body, [after(totals[0], fc1_part), totals[1], tokens, attention_out, cotangent], token_rows, [BF16], 2, "last"
    )

    first_sums, middle_sums, last_sums = (
        sums.sum(1) for sums in (first_sums, middle_sums, last_sums)
    )
    mod_rows = jnp.concatenate(
        [first_sums, middle_sums[2:3], middle_sums[:2], last_sums[:1], middle_sums[3:], last_sums[1:]]
    )
    mod_rows = mod_rows.reshape(8, cols, col_width).transpose(1, 0, 2)
    fc1_rel = bias_fc1.sum(0).reshape(chips, local_units)
    qkv_rel = bias_qkv.reshape(pairs, 3, 2, HD)
    qv_rel = jnp.stack([qkv_rel[:, 0], qkv_rel[:, 2]], 2).reshape(chips, local_heads * PAIR)
    hidden_rows = grid.to_absolute(jnp.concatenate([fc1_rel, qv_rel], 1)).reshape(
        cols, -1, col_width
    )
    pieces = jnp.concatenate([mod_rows, hidden_rows], 1)
    pieces = jnp.broadcast_to(pieces[None], (rows,) + pieces.shape).reshape(
        devices, -1, col_width
    )
    arrived = all_exchange(pieces)
    grad_modulation = arrived[:, :6].reshape(seqs, span, 6, col_width).sum(1)
    sums = arrived[:, 6:].sum(0)
    out_bias_grad = sums[0]
    fc2_bias_grad = sums[1]
    hidden_sums = sums[2:].reshape(-1)
    fc1_bias_grad = hidden_sums[:local_units]
    qv_bias_grad = hidden_sums[local_units:].reshape(local_heads, PAIR)
    mod_bias_grad = jnp.sum(grad_modulation, 0)
    grad_mod_flat = grad_modulation.reshape(seqs, 6 * col_width)
    mod_part_grad = lax.dot_general(
        cond_act.astype(F32), grad_mod_flat, TN, precision=PRECISE, preferred_element_type=F32
    ).reshape(row_width, 6, col_width)
    cond_part = lax.dot_general(
        grad_mod_flat,
        mod_flat.astype(F32),
        NT,
        precision=PRECISE,
        preferred_element_type=F32,
    )
    cond_pieces = lax.dynamic_update_slice_in_dim(
        jnp.zeros((seqs, D), F32), cond_part, grid.row * row_width, 1
    )
    cond_pieces = (
        cond_pieces.reshape(rows, seq_rows, cols, col_width)
        .transpose(0, 2, 1, 3)
        .reshape(devices, seq_rows, col_width)
    )
    grad_cond_act = all_exchange(cond_pieces).sum(0)
    _, silu_pull = jax.vjp(silu_fn, condition.astype(F32))
    condition_grad = silu_pull(grad_cond_act)[0]
    return (
        layer_out,
        tokens_grad,
        condition_grad,
        mod_part_grad,
        mod_bias_grad,
        qkv_part,
        qv_bias_grad,
        out_part,
        out_bias_grad,
        fc1_part.astype(F32),
        fc1_bias_grad,
        fc2_part.astype(F32).T,
        fc2_bias_grad,
    )


def solution(mesh):
    return jax.shard_map(
        per_device,
        mesh=mesh,
        in_specs=(
            P(("row", "col"), None),
            P("row", "col"),
            P("row", None, "col"),
            P(None, "col"),
            P("row", "col", None),
            P("col", None),
            P("col", None, "row"),
            P("col"),
            P("row", "col"),
            P("col"),
            P("col", "row"),
            P("col"),
            P(("row", "col"), None),
        ),
        out_specs=(
            P(("row", "col"), None),
            P(("row", "col"), None),
            P("row", "col"),
            P("row", None, "col"),
            P(None, "col"),
            P("row", "col", None),
            P("col", None),
            P("col", None, "row"),
            P("col"),
            P("row", "col"),
            P("col"),
            P("col", "row"),
            P("col"),
        ),
        check_vma=False,
    )
```

```python
import functools
import math

import jax
import jax.numpy as jnp
from jax import lax
from jax.experimental import pallas as pl
from jax.experimental.pallas import tpu as pltpu
from jax.sharding import PartitionSpec as P

D = 1024
HD = 64
LEN = 1024
PAIR = 2 * HD

EPSILON = 1e-06
PRECISE = lax.Precision.HIGHEST
NN = (((1,), (0,)), ((), ()))
NT = (((1,), (1,)), ((), ()))
TN = (((0,), (0,)), ((), ()))
F32 = jnp.float32
BF16 = jnp.bfloat16
QUERY_ROWS = 512
TOKEN_ROWS = 32
LARGE_BYTES = 4 * 1024 * 1024
VMEM_NEEDS = {
    "attend": 14,
    "attend_back": 20,
    "tokens": 14,
    "rows": 26,
    "rows_total": 20,
    "columns_product": 26,
    "assemble": 12,
}
SMALL_COST = pl.CostEstimate(flops=1000, bytes_accessed=1000, transcendentals=0)


def vmem_of(need):
    return VMEM_NEEDS[need] * 1024 * 1024


def is_large(array):
    return array.size * array.dtype.itemsize >= LARGE_BYTES


def large_in_hbm(call):
    def wrapped(*arrays):
        return call(
            *[
                pltpu.with_memory_space_constraint(a, pltpu.HBM) if is_large(a) else a
                for a in arrays
            ]
        )

    return wrapped


def large_out(shapes):
    return jax.tree.map(lambda a: pltpu.HBM(a.shape, a.dtype) if is_large(a) else a, shapes)


def dot(left, right, dims=NN):
    return lax.dot_general(left, right, dims, preferred_element_type=F32)


def silu_fn(values):
    return values * jax.nn.sigmoid(values)


def gelu_both(values):
    c = math.sqrt(2.0 / math.pi)
    square = values * values
    half = 0.5 + 0.5 * jnp.tanh(values * (c + (c * 0.044715) * square))
    gelu = values * half
    slope = half + gelu * (1.0 - half) * (2.0 * c + (6.0 * c * 0.044715) * square)
    return gelu, slope


def normalize(resid):
    average = jnp.mean(resid, 1, keepdims=True)
    spread = jnp.mean(resid * resid, 1, keepdims=True) - average * average
    inv_std = lax.rsqrt(spread + EPSILON)
    return ((resid - average) * inv_std, inv_std)


def normalize_back(grad_norm, normed, inv_std):
    average = jnp.mean(grad_norm, 1, keepdims=True)
    crossed = jnp.mean(grad_norm * normed, 1, keepdims=True)
    return inv_std * (grad_norm - average - normed * crossed)


def after(array, *earlier):
    return lax.optimization_barrier((array, *earlier))[0]


def head_lanes(shape, head):
    lane = lax.broadcasted_iota(jnp.int32, shape, 1)
    return lane < HD if head == 0 else lane >= HD


def attend_kernel(q_ref, k_ref, v_ref, *refs):
    mixed_ref, log_ref = refs[-2:]
    queries = q_ref[...] * jnp.asarray(HD**-0.5, BF16)
    key_rows = k_ref[...]
    values_across = v_ref[...].T
    mask = head_lanes(key_rows.shape, 0)
    zero = jnp.zeros_like(key_rows)
    keys = (jnp.where(mask, key_rows, zero), jnp.where(mask, zero, key_rows))
    length = queries.shape[0]
    for start in range(0, length, QUERY_ROWS):
        stop = start + QUERY_ROWS
        q_part = queries[start:stop]
        outs = []
        for head in range(2):
            scores = dot(keys[head], q_part, NT)
            top = jnp.max(scores, 0, keepdims=True)
            expon = jnp.exp(scores - top)
            total = jnp.sum(expon, 0, keepdims=True)
            out = dot(values_across[head * HD : (head + 1) * HD], expon.astype(BF16))
            outs.append(out / total)
            log_ref[0, 0, head : head + 1, start:stop] = top + jnp.log(total)
        mixed_ref[start:stop, :] = jnp.concatenate(outs, 0).T.astype(BF16)


def attend_back_kernel(q_ref, k_ref, v_ref, mixed_ref, grad_ref, log_ref, out_ref, sums_ref):
    scale = jnp.asarray(HD**-0.5, BF16)
    queries = q_ref[...] * scale
    key_rows = k_ref[...]
    value_rows = v_ref[...]
    grad_rows = grad_ref[...]
    mask = head_lanes(value_rows.shape, 0)
    zero = jnp.zeros_like(value_rows)
    keys = (jnp.where(mask, key_rows, zero), jnp.where(mask, zero, key_rows))
    values = (jnp.where(mask, value_rows, zero), jnp.where(mask, zero, value_rows))
    keys_across = (key_rows * scale).T
    product = grad_rows.astype(F32) * mixed_ref[...].astype(F32)
    picks = (
        lax.broadcasted_iota(jnp.int32, (8, PAIR), 0)
        == lax.broadcasted_iota(jnp.int32, (8, PAIR), 1) // HD
    ).astype(F32)
    inner = lax.dot_general(picks, product, NT, precision=PRECISE, preferred_element_type=F32)
    length = queries.shape[0]
    grad_k = [None, None]
    grad_v = [None, None]
    for start in range(0, length, QUERY_ROWS):
        stop = start + QUERY_ROWS
        q_part = queries[start:stop]
        g_part = grad_rows[start:stop]
        outs = []
        for head in range(2):
            scores = dot(keys[head], q_part, NT)
            probs = jnp.exp(scores - log_ref[0, 0, head : head + 1, start:stop])
            grad_probs = dot(values[head], g_part, NT)
            grad_scores = (probs * (grad_probs - inner[head : head + 1, start:stop])).astype(BF16)
            part_v = dot(probs.astype(BF16), g_part)
            part_k = dot(grad_scores, q_part)
            grad_v[head] = part_v if grad_v[head] is None else grad_v[head] + part_v
            grad_k[head] = part_k if grad_k[head] is None else grad_k[head] + part_k
            outs.append(dot(keys_across[head * HD : (head + 1) * HD], grad_scores))
        out_ref[start:stop, 0:PAIR] = jnp.concatenate(outs, 0).T.astype(BF16)
    out_ref[:, PAIR : 2 * PAIR] = jnp.where(mask, grad_k[0], grad_k[1]).astype(BF16)
    out_ref[:, 2 * PAIR :] = jnp.where(mask, grad_v[0], grad_v[1]).astype(BF16)
    sums_ref[0, 0] = jnp.sum(out_ref[...].astype(F32).reshape(length // 8, 8, 3 * PAIR), 0)


def attention_specs(first):
    part = lambda offset: pl.BlockSpec((LEN, PAIR), lambda s, p: (s, 3 * (p + first) + offset))
    plain = pl.BlockSpec((LEN, PAIR), lambda s, p: (s, p + first))
    logs = pl.BlockSpec((1, 1, 2, LEN), lambda s, p: (s, p + first, 0, 0))
    return [part(0), part(1), part(2)], plain, logs


def attend(projected, latents, pairs, first, count, earlier=()):
    parts, plain, logs = attention_specs(first)
    rows = projected.shape[0]
    call = pl.pallas_call(
        attend_kernel,
        grid=(latents, count),
        in_specs=parts + [pl.BlockSpec(memory_space=pl.ANY)] * len(earlier),
        out_specs=[plain, logs],
        out_shape=[
            jax.ShapeDtypeStruct((rows, pairs * PAIR), BF16),
            jax.ShapeDtypeStruct((latents, pairs, 2, LEN), F32),
        ],
        input_output_aliases={3 + i: i for i in range(len(earlier))},
        compiler_params=pltpu.CompilerParams(vmem_limit_bytes=vmem_of("attend")),
        cost_estimate=SMALL_COST,
        name="attend",
    )
    return large_in_hbm(call)(projected, projected, projected, *earlier)


def attend_back(projected, mixed, grad_mixed, log_totals, latents, first, count):
    parts, plain, logs = attention_specs(first)
    rows = projected.shape[0]
    call = pl.pallas_call(
        attend_back_kernel,
        grid=(latents, count),
        in_specs=[*parts, plain, plain, logs],
        out_specs=[
            pl.BlockSpec((LEN, 3 * PAIR), lambda s, p: (s, p)),
            pl.BlockSpec((1, 1, 8, 3 * PAIR), lambda s, p: (s, p, 0, 0)),
        ],
        out_shape=large_out([
            jax.ShapeDtypeStruct((rows, count * 3 * PAIR), BF16),
            jax.ShapeDtypeStruct((latents, count, 8, 3 * PAIR), F32),
        ]),
        compiler_params=pltpu.CompilerParams(vmem_limit_bytes=vmem_of("attend_back")),
        cost_estimate=SMALL_COST,
        name="attend_back",
    )
    return large_in_hbm(call)(projected, projected, projected, mixed, grad_mixed, log_totals)


def kernel_call(body, grid, in_specs, out_specs, out_shape, name, need):
    call = pl.pallas_call(
        body,
        grid=grid,
        in_specs=in_specs,
        out_specs=out_specs,
        out_shape=large_out(out_shape),
        compiler_params=pltpu.CompilerParams(vmem_limit_bytes=vmem_of(need)),
        cost_estimate=SMALL_COST,
        name=name,
    )
    return large_in_hbm(call)


def whole(array):
    return pl.BlockSpec(array.shape, lambda *step: (0,) * array.ndim)


def pieces_of(array, ids, width):
    return {i: (array, place, width) for place, i in enumerate(ids)}


def piece_spec(piece):
    array, block, width = piece
    return pl.BlockSpec((array.shape[0], width), lambda *step: (0, block))


def row_specs(local_rows, tile, width):
    count = local_rows // tile
    mine = pl.BlockSpec((tile, width), lambda i: (jnp.minimum(i, count - 1), 0))
    theirs = pl.BlockSpec((tile, width), lambda i: (jnp.maximum(i - count, 0), 0))
    return count, mine, theirs


def rows_product(pair, weights, extra, kind):
    local_rows, depth = pair[0].shape
    tile = min(512, local_rows)
    count, mine, theirs = row_specs(local_rows, tile, depth)
    widths = [piece[2] for piece in weights]
    width = sum(widths)
    total = 2 * local_rows

    def body(*refs):
        mine_ref, theirs_ref = refs[:2]
        weight_refs = refs[2 : 2 + len(weights)]
        extra_ref = refs[2 + len(weights)]
        out_refs = refs[3 + len(weights) :]
        step = pl.program_id(0)
        left = jnp.where(step < count, mine_ref[...], theirs_ref[...])
        if kind == "slope":

            @pl.when(step == 0)
            def _():
                out_refs[1][...] = jnp.zeros(out_refs[1].shape, F32)

        start = 0
        for ref, span in zip(weight_refs, widths):
            step_width = min(256, span)
            for low in range(0, span, step_width):
                cols = slice(start + low, start + low + step_width)
                product = dot(left, ref[:, low : low + step_width])
                if kind == "bias":
                    out_refs[0][:, cols] = (product + extra_ref[:, cols]).astype(BF16)
                elif kind == "gelu":
                    act, slope = gelu_both(product + extra_ref[:, cols])
                    out_refs[0][:, cols] = act.astype(BF16)
                    out_refs[1][:, cols] = slope.astype(BF16)
                else:
                    grad = (product * extra_ref[:, cols].astype(F32)).astype(BF16)
                    out_refs[0][:, cols] = grad
                    out_refs[1][:, cols] += jnp.sum(
                        grad.astype(F32).reshape(tile // 8, 8, step_width), 0
                    )
            start += span

    rows_out = pl.BlockSpec((tile, width), lambda i: (i, 0))
    low_shape = jax.ShapeDtypeStruct((total, width), BF16)
    if kind == "bias":
        out_specs, out_shape = [rows_out], [low_shape]
    elif kind == "gelu":
        out_specs, out_shape = [rows_out, rows_out], [low_shape, low_shape]
    else:
        out_specs = [rows_out, pl.BlockSpec((8, width), lambda i: (0, 0))]
        out_shape = [low_shape, jax.ShapeDtypeStruct((8, width), F32)]
    extra_spec = rows_out if kind == "slope" else whole(extra)
    return kernel_call(
        body,
        (2 * count,),
        [mine, theirs, *[piece_spec(w) for w in weights], extra_spec],
        out_specs,
        out_shape,
        "rows_" + kind,
        "rows",
    )(*pair, *[w[0] for w in weights], extra)


def columns_of(refs, start, stop):
    for ref in refs:
        if start < ref.shape[1]:
            return ref[:, start:stop]
        start, stop = start - ref.shape[1], stop - ref.shape[1]


def rows_total(lefts, weights):
    local_rows = lefts[0].shape[0] // 2
    tile = min(512, local_rows)
    count = local_rows // tile
    width = weights[0][0].shape[0]
    ends = set()
    for spans in ([a.shape[1] for a in lefts], [w[2] for w in weights]):
        end = 0
        for span in spans:
            end += span
            ends.add(end)
    ends = sorted(ends)

    def body(*refs):
        left_refs = refs[: len(lefts)]
        weight_refs = refs[len(lefts) : -2]
        mine_ref, theirs_ref = refs[-2:]
        total = None
        for start, stop in zip([0] + ends, ends):
            part = dot(columns_of(left_refs, start, stop), columns_of(weight_refs, start, stop), NT)
            total = part if total is None else total + part
        step = pl.program_id(0)

        @pl.when(step < count)
        def _():
            mine_ref[...] = total

        @pl.when(step >= count)
        def _():
            theirs_ref[...] = total.astype(BF16)

    return kernel_call(
        body,
        (2 * count,),
        [pl.BlockSpec((tile, a.shape[1]), lambda i: (i, 0)) for a in lefts]
        + [piece_spec(w) for w in weights],
        [
            pl.BlockSpec((tile, width), lambda i: (jnp.minimum(i, count - 1), 0)),
            pl.BlockSpec((tile, width), lambda i: (jnp.maximum(i - count, 0), 0)),
        ],
        [
            jax.ShapeDtypeStruct((local_rows, width), F32),
            jax.ShapeDtypeStruct((local_rows, width), BF16),
        ],
        "rows_total",
        "rows_total",
    )(*lefts, *[w[0] for w in weights])


def token_kernel(body, arrays, rows_of, out_types, sums, name):
    tokens = arrays[0].shape[0]
    tile = min(256, tokens)
    outs = len(out_types)

    def kernel(*refs):
        rows_ref = refs[len(arrays)]
        out_refs = refs[len(arrays) + 1 :]
        rows = [rows_ref[i : i + 1, :] for i in range(8)]
        if sums:
            sum_ref = out_refs[outs]

            @pl.when(pl.program_id(0) == 0)
            def _():
                sum_ref[...] = jnp.zeros(sum_ref.shape, F32)

        for start in range(0, tile, TOKEN_ROWS):
            lines = slice(start, start + TOKEN_ROWS)
            values = [ref[lines, :].astype(F32) for ref in refs[: len(arrays)]]
            results, columns = body(values, rows)
            for ref, result in zip(out_refs, results):
                ref[lines, :] = result.astype(ref.dtype)
            for i, column in enumerate(columns):
                sum_ref[i] += jnp.sum(column.reshape(TOKEN_ROWS // 8, 8, D), 0)

    tokens_spec = pl.BlockSpec((tile, D), lambda i: (i, 0))
    out_specs = [tokens_spec] * outs
    out_shape = [jax.ShapeDtypeStruct((tokens, D), t) for t in out_types]
    if sums:
        out_specs = out_specs + [pl.BlockSpec((sums, 8, D), lambda i: (0, 0, 0))]
        out_shape = out_shape + [jax.ShapeDtypeStruct((sums, 8, D), F32)]
    return kernel_call(
        kernel,
        (tokens // tile,),
        [tokens_spec] * len(arrays) + [whole(rows_of)],
        out_specs,
        out_shape,
        name,
        "tokens",
    )(*arrays, rows_of)


def middle_body(values, rows):
    mine, theirs, tokens = values
    gate, shift, scale, bias = rows[2], rows[3], rows[4], rows[6]
    attention_out = mine + theirs + bias
    normed, _ = normalize(tokens + gate * attention_out)
    return [attention_out, normed * (1.0 + scale) + shift], []


def middle_back_body(values, rows):
    mine, theirs, upstream, tokens, attention_out = values
    gate, scale = rows[2], rows[4]
    grad_hidden = mine + theirs
    normed, inv_std = normalize(tokens + gate * attention_out)
    grad = upstream + normalize_back(grad_hidden * (1.0 + scale), normed, inv_std)
    grad_attention = grad * gate
    return [grad, grad_attention], [
        grad_hidden,
        grad_hidden * normed,
        grad * attention_out,
        grad_attention,
    ]


def first_back_body(values, rows):
    mine, theirs, tokens, grad_resid = values
    scale = rows[1]
    grad_hidden = mine + theirs
    normed, inv_std = normalize(tokens)
    grad = grad_resid + normalize_back(grad_hidden * (1.0 + scale), normed, inv_std)
    return [grad], [grad_hidden, grad_hidden * normed]


def last_body(values, rows):
    mine, theirs, tokens, attention_out, upstream = values
    gate_attn, gate_feed, bias = rows[2], rows[5], rows[7]
    feed_out = mine + theirs + bias
    resid_mid = tokens + gate_attn * attention_out
    return [resid_mid + gate_feed * feed_out], [upstream * feed_out, upstream * gate_feed]


def columns_product(pair, right, added, outs, width):
    local_rows, depth = pair[0].shape
    rows = right.shape[0]
    tile = 256
    blocks = [i for ids in outs for i in ids]
    extra = list(added)
    per_extra = len(blocks) // max(1, len(extra))

    def body(mine_ref, theirs_ref, *refs):
        right_refs = refs[: len(blocks)]
        add_refs = refs[len(blocks) : len(blocks) + len(extra)]
        out_refs = refs[len(blocks) + len(extra) :]
        mine, theirs = mine_ref[...].T, theirs_ref[...].T
        number = 0
        for ref, ids in zip(out_refs, outs):
            for place in range(len(ids)):
                total = dot(mine, right_refs[number][:local_rows])
                total = total + dot(theirs, right_refs[number][local_rows:])
                if extra:
                    start = number % per_extra * width
                    part = add_refs[number // per_extra][:, start : start + width]
                    total = total + part.astype(F32)
                ref[:, place * width : (place + 1) * width] = total.astype(BF16)
                number += 1

    token_spec = pl.BlockSpec((local_rows, tile), lambda i: (0, i))

    def out_spec(count):
        return pl.BlockSpec((tile, count * width), lambda i: (i, 0))

    return kernel_call(
        body,
        (depth // tile,),
        [token_spec, token_spec]
        + [pl.BlockSpec((rows, width), lambda i, b=b: (0, b)) for b in blocks]
        + [out_spec(per_extra) for _ in extra],
        [out_spec(len(ids)) for ids in outs],
        [jax.ShapeDtypeStruct((depth, len(ids) * width), BF16) for ids in outs],
        "columns_product",
        "columns_product",
    )(*pair, *[right] * len(blocks), *extra)


def assemble(top, low, qkv_width, out_width):
    parts = [top[0], top[2], low[0], low[2]]
    ids = [top[1], top[3], low[1], low[3]]
    half, width = parts[0].shape
    block = qkv_width + out_width
    blocks = 2 * width // block
    tile = 128

    def body(a_ref, b_ref, c_ref, d_ref, qkv_ref, out_ref):
        for number, ref in enumerate((a_ref, b_ref, c_ref, d_ref)):
            for place, i in enumerate(ids[number]):
                start = place * block
                qkv_ref[number // 2, :, i * qkv_width : (i + 1) * qkv_width] = ref[
                    :, start : start + qkv_width
                ]
                out_ref[number // 2, :, i * out_width : (i + 1) * out_width] = ref[
                    :, start + qkv_width : start + block
                ]

    qkv, out = kernel_call(
        body,
        (half // tile,),
        [pl.BlockSpec((tile, width), lambda i: (i, 0))] * 4,
        [
            pl.BlockSpec((2, tile, blocks * qkv_width), lambda i: (0, i, 0)),
            pl.BlockSpec((2, tile, blocks * out_width), lambda i: (0, i, 0)),
        ],
        [
            jax.ShapeDtypeStruct((2, half, blocks * qkv_width), BF16),
            jax.ShapeDtypeStruct((2, half, blocks * out_width), BF16),
        ],
        "assemble",
        "assemble",
    )(*parts)
    return qkv.reshape(2 * half, -1), out.reshape(2 * half, -1)


class Grid:
    def __init__(self):
        self.rows = lax.axis_size("row")
        self.cols = lax.axis_size("col")
        self.chips = self.cols // 2
        self.bits = [1 << b for b in range(self.chips.bit_length() - 1)]
        self.orders = (self.bits, self.bits[::-1])
        self.row = lax.axis_index("row")
        self.col = lax.axis_index("col")
        self.core = self.col % 2
        source = lax.iota(jnp.int32, self.chips) ^ (self.col // 2)
        self.choose = (
            (2 * source + self.core)[:, None] == lax.iota(jnp.int32, self.cols)[None, :]
        ).astype(F32)

    def swap(self, array, flip):
        pairs = [(i, i ^ flip) for i in range(self.cols)]
        return lax.ppermute(array, "col", pairs)

    def swap_core(self, array):
        return self.swap(array, 1)

    def swap_chip(self, array, bit):
        return self.swap(array, 2 * bit)

    def to_relative(self, blocks):
        flat = blocks.reshape(self.cols, -1).astype(F32)
        picked = lax.dot_general(
            self.choose, flat, NN, precision=PRECISE, preferred_element_type=F32
        )
        return picked.reshape((self.chips,) + blocks.shape[1:])

    def to_absolute(self, blocks):
        flat = blocks.reshape(self.chips, -1)
        placed = lax.dot_general(
            self.choose, flat, TN, precision=PRECISE, preferred_element_type=F32
        )
        return placed.reshape((self.cols,) + blocks.shape[1:])

    def gather_rows(self, block):
        count = self.rows
        got = [block]
        for step in range(1, count):
            got.append(
                lax.ppermute(block, "row", [(i, (i + step) % count) for i in range(count)])
            )
        stacked = jnp.stack(got)
        ordered = [
            lax.dynamic_index_in_dim(stacked, (self.row - i) % count, 0, keepdims=False)
            for i in range(count)
        ]
        return jnp.concatenate(ordered, 0), got[-1]

    def scatter_rows(self, whole):
        count = self.rows
        blocks = whole.reshape(count, whole.shape[0] // count, whole.shape[1])
        total = lax.dynamic_index_in_dim(blocks, self.row, 0, keepdims=False).astype(F32)
        for step in range(1, count):
            sent = lax.dynamic_index_in_dim(blocks, (self.row + step) % count, 0, keepdims=False)
            total = total + lax.ppermute(
                sent, "row", [(i, (i + step) % count) for i in range(count)]
            ).astype(F32)
        return total

    def gather_early(self, block, order, late=()):
        held, ids = block, [0]
        for bit in order[:-1]:
            got = self.swap_chip(held, bit)
            if bit == order[-2]:
                got = after(got, *late)
            held = jnp.concatenate([held, got], 1)
            ids = ids + [bit ^ i for i in ids]
        return held, ids

    def early_ids(self, order):
        ids = [0]
        for bit in order[:-1]:
            ids = ids + [bit ^ i for i in ids]
        return ids

    def gather_last(self, held, ids, order):
        return self.swap_chip(held, order[-1]), [order[-1] ^ i for i in ids]

    def scatter_chips(self, keep, send, order, late=()):
        for bit in order[-2::-1]:
            got = self.swap_chip(send, bit)
            if bit == order[-2]:
                got = after(got, *late)
            total = keep.astype(F32) + got.astype(F32)
            if bit == order[0]:
                return total
            half = total.shape[1] // 2
            keep, send = total[:, :half], total[:, half:].astype(BF16)


def split_columns(array, ids):
    width = array.shape[1] // len(ids)
    return {i: array[:, n * width : (n + 1) * width] for n, i in enumerate(ids)}


def all_exchange(pieces):
    return lax.all_to_all(pieces, ("row", "col"), 0, 0, tiled=True)


def per_device(
    tokens,
    condition,
    mod_weight,
    mod_bias,
    qkv_weight,
    qv_bias,
    out_weight,
    out_bias,
    fc1_weight,
    fc1_bias,
    fc2_weight,
    fc2_bias,
    cotangent,
):
    grid = Grid()
    rows, cols, chips = grid.rows, grid.cols, grid.chips
    devices = rows * cols
    local_rows = tokens.shape[0]
    both_rows = 2 * local_rows
    latents = both_rows // LEN
    span = LEN // local_rows
    seq_rows = condition.shape[0]
    seqs = seq_rows * rows
    row_width = D // rows
    col_width = D // cols
    local_heads = qkv_weight.shape[1]
    local_units = fc1_weight.shape[1]
    plane_heads = local_heads * chips
    pairs = plane_heads // 2
    qkv_width = local_heads * 3 * HD
    out_width = local_heads * HD

    if local_heads % 2 == 0:
        qkv_local = (
            qkv_weight.reshape(row_width, local_heads // 2, 2, 3, HD)
            .transpose(0, 1, 3, 2, 4)
            .reshape(row_width, qkv_width)
        )
    else:
        qkv_local = qkv_weight.reshape(row_width, qkv_width)
    attn_local = jnp.concatenate(
        [qkv_local, out_weight.reshape(out_width, row_width).T], 1
    )
    attn_width = qkv_width + out_width
    fc1_local = fc1_weight
    fc2_local = fc2_weight.T

    small = jnp.concatenate(
        [
            condition.reshape(-1),
            fc1_bias,
            qv_bias.reshape(-1),
            out_bias,
            fc2_bias,
        ]
    )
    small_all = all_exchange(
        jnp.broadcast_to(small.reshape(1, -1, 128), (devices, small.size // 128, 128))
    )

    attn_rows, mark = grid.gather_rows(attn_local)
    fc1_rows = lax.all_gather(after(fc1_local, mark), "row", axis=0, tiled=True)
    fc2_rows = lax.all_gather(after(fc2_local, fc1_rows), "row", axis=0, tiled=True)
    half = D // 2
    top = grid.gather_early(attn_rows[:half], grid.orders[0])
    low = grid.gather_early(attn_rows[half:], grid.orders[1])
    small_all = small_all.reshape(rows, cols, -1)
    cut = seq_rows * col_width
    cond_all = (
        small_all[:, :, :cut]
        .reshape(rows, cols, seq_rows, col_width)
        .transpose(0, 2, 1, 3)
        .reshape(seqs, D)
    )
    biases = small_all[0, :, cut:]
    fc1_bias_all = biases[:, :local_units]
    qv_bias_all = biases[:, local_units : local_units + local_heads * PAIR]
    out_bias_all = biases[:, -2 * col_width : -col_width].reshape(1, D).astype(F32)
    fc2_bias_all = biases[:, -col_width:].reshape(1, D).astype(F32)

    cond_act = silu_fn(cond_all.astype(F32)).astype(BF16)
    cond_act = lax.dynamic_slice_in_dim(cond_act, grid.row * row_width, row_width, 1)
    mod_flat = mod_weight.reshape(row_width, 6 * col_width)
    own_bias = jnp.where(grid.row == 0, mod_bias.astype(F32), 0.0)
    mod_part = dot(cond_act, mod_flat).reshape(seqs, 6, col_width) + own_bias
    mod_part = jnp.broadcast_to(
        mod_part[:, None], (seqs, span, 6, col_width)
    ).reshape(devices, 6, col_width)
    modulation = (
        all_exchange(mod_part)
        .reshape(rows, cols, 6, col_width)
        .sum(0)
        .transpose(1, 0, 2)
        .reshape(6, 1, D)
    )
    shift_attn, scale_attn, gate_attn, shift_feed, scale_feed, gate_feed = modulation
    token_rows = jnp.concatenate([modulation.reshape(6, D), out_bias_all, fc2_bias_all], 0)

    top = top + grid.gather_last(*top, grid.orders[0])
    low = low + grid.gather_last(*low, grid.orders[1])
    if local_heads % 2 == 0:
        qkv_w, out_w = assemble(top, low, qkv_width, out_width)
    else:
        attn_top = {**split_columns(top[0], top[1]), **split_columns(top[2], top[3])}
        attn_low = {**split_columns(low[0], low[1]), **split_columns(low[2], low[3])}
        attn_blocks = [jnp.concatenate([attn_top[i], attn_low[i]], 0) for i in range(chips)]
        qkv_w = (
            jnp.stack([b[:, :qkv_width] for b in attn_blocks], 1)
            .reshape(D, pairs, 2, 3, HD)
            .transpose(0, 1, 3, 2, 4)
            .reshape(D, pairs * 3 * PAIR)
        )
        out_w = jnp.concatenate([b[:, qkv_width:] for b in attn_blocks], 1)

    fc1_bias_rel = grid.to_relative(fc1_bias_all).reshape(1, chips * local_units)
    qv_rel = grid.to_relative(qv_bias_all).reshape(pairs, 2, 2, HD).transpose(0, 2, 1, 3)
    qkv_bias_rel = jnp.concatenate(
        [qv_rel[:, :1], jnp.zeros_like(qv_rel[:, :1]), qv_rel[:, 1:]], 1
    ).reshape(1, pairs * 3 * PAIR)

    def both(mine):
        return (mine, grid.swap_core(mine))

    def own_total(lefts, weights):
        mine, theirs = rows_total(lefts, weights)
        return mine, grid.swap_core(theirs)

    def sum_rows(parts):
        return lax.psum_scatter(parts, "row", scatter_dimension=0, tiled=True)

    resid = tokens.astype(F32)
    normed_attn, _ = normalize(resid)
    hidden_attn = both((normed_attn * (1.0 + scale_attn) + shift_attn).astype(BF16))
    grad_feed_low = both((cotangent.astype(F32) * gate_feed).astype(BF16))

    (projected,) = rows_product(hidden_attn, [(qkv_w, 0, qkv_w.shape[1])], qkv_bias_rel, "bias")
    unit_half = local_units // 2

    def units_early(held, earlier, late):
        held = after(held, *earlier)
        parts = (held[:, :unit_half], held[:, unit_half:])
        return [grid.gather_early(part, order, late) for part, order in zip(parts, grid.orders)]

    def units_last(early, *earlier):
        return [
            grid.gather_last(after(held, *earlier), ids, order)
            for (held, ids), order in zip(early, grid.orders)
        ]

    def unit_pieces(early, last):
        found = [{**pieces_of(*e, unit_half), **pieces_of(*l, unit_half)} for e, l in zip(early, last)]
        return [found[part][i] for i in range(chips) for part in range(2)]

    fc1_early = units_early(fc1_rows, (top[2], low[2]), (projected,))
    fc1_last = units_last(fc1_early)
    fc1_got_last = [got for got, _ in fc1_last]
    projected = after(projected, *[held for held, _ in fc1_early])
    middle_pair = pairs // 2
    first_half = attend(projected, latents, pairs, 0, middle_pair)
    fc2_early = units_early(fc2_rows, (first_half[0], *fc1_got_last), ())
    mixed, log_totals = attend(
        after(projected, first_half[0], *fc1_got_last),
        latents,
        pairs,
        middle_pair,
        pairs - middle_pair,
        first_half,
    )
    fc2_last = units_last(fc2_early, mixed)
    mixed = after(mixed, *[held for held, _ in fc2_early])
    fc1_all = unit_pieces(fc1_early, fc1_last)
    fc2_all = unit_pieces(fc2_early, fc2_last)
    order1 = grid.orders[0]
    out_all = [(out_w, 0, out_w.shape[1])]
    totals = own_total([mixed], out_all)
    attention_out, hidden_feed = token_kernel(
        middle_body,
        [*totals, tokens],
        token_rows,
        [F32, BF16],
        0,
        "middle",
    )
    hidden_feed = both(hidden_feed)
    acts, slopes = rows_product(hidden_feed, fc1_all, fc1_bias_rel, "gelu")
    acts = after(acts, *[got for got, _ in fc2_last])

    def send_units(left, right, orders):
        count = len(orders)
        outs = [
            [count * (order[-1] ^ i) + part for i in grid.early_ids(order)]
            for part, order in enumerate(orders)
        ]
        sent = columns_product(left, right, [], outs, local_units // count)
        return [grid.swap_chip(a, order[-1]) for a, order in zip(sent, orders)], sent[0]

    def keep_units(left, right, got, orders):
        count = len(orders)
        outs = []
        for part, order in enumerate(orders):
            places = [count * i + part for i in grid.early_ids(order)]
            outs += [places[: len(places) // 2], places[len(places) // 2 :]]
        return columns_product(left, right, got, outs, local_units // count)

    def sum_chips(kept, orders, late):
        sums = [
            grid.scatter_chips(kept[2 * part], kept[2 * part + 1], order, late)
            for part, order in enumerate(orders)
        ]
        return jnp.concatenate(sums, 1).astype(BF16)

    fc2_got, fc2_sent = send_units(grad_feed_low, acts, grid.orders)
    grad_pre, bias_fc1 = rows_product(
        (after(grad_feed_low[0], fc2_sent), grad_feed_low[1]), fc2_all, slopes, "slope"
    )
    fc1_got, sent = send_units(hidden_feed, grad_pre, [order1])
    totals = own_total([after(grad_pre, sent, *fc2_got)], fc1_all)
    fc2_kept = keep_units(grad_feed_low, after(acts, totals[0]), fc2_got, grid.orders)
    grad_resid_mid, grad_attention_low, middle_sums = token_kernel(
        middle_back_body,
        [after(totals[0], fc2_kept[0]), totals[1], cotangent, tokens, attention_out],
        token_rows,
        [F32, BF16],
        4,
        "middle_back",
    )
    grad_attention_low = both(grad_attention_low)

    (grad_mixed,) = rows_product(
        grad_attention_low, out_all, jnp.zeros((1, out_w.shape[1]), F32), "bias"
    )
    (grad_out,) = columns_product(
        grad_attention_low, after(mixed, grad_mixed), [], [[0]], mixed.shape[1]
    )
    grad_mixed = after(grad_mixed, grad_out)
    grad_late, bias_late = attend_back(
        projected, mixed, grad_mixed, log_totals, latents, 1, pairs - 1
    )
    fc2_sums = sum_chips(fc2_kept, grid.orders, (grad_late,))
    fc1_kept = keep_units(hidden_feed, after(grad_pre, grad_late), fc1_got, [order1])
    late_chips = chips * (pairs - 1) // pairs
    qkv_late = columns_product(
        hidden_attn, grad_late, [], [[i] for i in range(late_chips)], qkv_width
    ) if (
        local_heads % 2 == 0
    ) else None
    early_input = after(grad_mixed, grad_late, fc2_sums, fc1_kept[0])
    grad_early, bias_early = attend_back(
        projected, mixed, early_input, log_totals, latents, 0, 1
    )
    fc1_sums = sum_chips(fc1_kept, [order1], (grad_early,))
    fc2_part = sum_rows(fc2_sums)
    fc1_part = sum_rows(fc1_sums)
    bias_qkv = jnp.concatenate([bias_early, bias_late], 1).sum((0, 2))
    if local_heads % 2 == 0:
        qkv_early = columns_product(hidden_attn, grad_early, [], [[0]], qkv_width)
        grad_qkv = [*qkv_early, *qkv_late]
    else:
        grad_projected = jnp.concatenate([grad_early, grad_late], 1)
        (grad_qkv,) = columns_product(
            hidden_attn, grad_projected, [], [[0]], 3 * PAIR * pairs
        )
        grad_qkv = (
            grad_qkv.reshape(D, pairs, 3, 2, HD).transpose(0, 1, 3, 2, 4).reshape(D, chips, qkv_width)
        )
        grad_qkv = [grad_qkv[:, i] for i in range(chips)]

    def pick(part, ids):
        lines = slice(0, half) if part == 0 else slice(half, D)
        return jnp.concatenate(
            [
                array
                for i in ids
                for array in (
                    grad_qkv[i][lines],
                    grad_out[lines, i * out_width : (i + 1) * out_width],
                )
            ],
            1,
        )

    attn_got = [
        grid.swap_chip(pick(number, gathered[3]), grid.orders[number][-1])
        for number, gathered in enumerate((top, low))
    ]
    attn_sums = []
    for number, gathered in enumerate((top, low)):
        order = grid.orders[number]
        kept = pick(number, gathered[1]).astype(F32) + attn_got[number].astype(F32)
        middle = kept.shape[1] // 2
        attn_sums.append(
            grid.scatter_chips(kept[:, :middle], kept[:, middle:].astype(BF16), order)
        )
    attn_part = grid.scatter_rows(jnp.concatenate(attn_sums, 0).astype(BF16))
    qkv_part = attn_part[:, :qkv_width]
    if local_heads % 2 == 0:
        qkv_part = qkv_part.reshape(row_width, local_heads // 2, 3, 2, HD).transpose(0, 1, 3, 2, 4)
    qkv_part = qkv_part.reshape(row_width, local_heads, 3 * HD)
    out_part = attn_part[:, qkv_width:].T.reshape(local_heads, HD, row_width)

    totals = own_total([after(grad_early, *attn_got), grad_late], [(qkv_w, 0, qkv_w.shape[1])])
    tokens_grad, first_sums = token_kernel(
        first_back_body, [*totals, tokens, grad_resid_mid], token_rows, [F32], 2, "first_back"
    )
    totals = own_total([after(acts, totals[0], fc2_part, *attn_sums)], fc2_all)
    layer_out, last_sums = token_kernel(
        last_body, [after(totals[0], fc1_part), totals[1], tokens, attention_out, cotangent], token_rows, [BF16], 2, "last"
    )

    first_sums, middle_sums, last_sums = (
        sums.sum(1) for sums in (first_sums, middle_sums, last_sums)
    )
    mod_rows = jnp.concatenate(
        [first_sums, middle_sums[2:3], middle_sums[:2], last_sums[:1], middle_sums[3:], last_sums[1:]]
    )
    mod_rows = mod_rows.reshape(8, cols, col_width).transpose(1, 0, 2)
    fc1_rel = bias_fc1.sum(0).reshape(chips, local_units)
    qkv_rel = bias_qkv.reshape(pairs, 3, 2, HD)
    qv_rel = jnp.stack([qkv_rel[:, 0], qkv_rel[:, 2]], 2).reshape(chips, local_heads * PAIR)
    hidden_rows = grid.to_absolute(jnp.concatenate([fc1_rel, qv_rel], 1)).reshape(
        cols, -1, col_width
    )
    pieces = jnp.concatenate([mod_rows, hidden_rows], 1)
    pieces = jnp.broadcast_to(pieces[None], (rows,) + pieces.shape).reshape(
        devices, -1, col_width
    )
    arrived = all_exchange(pieces)
    grad_modulation = arrived[:, :6].reshape(seqs, span, 6, col_width).sum(1)
    sums = arrived[:, 6:].sum(0)
    out_bias_grad = sums[0]
    fc2_bias_grad = sums[1]
    hidden_sums = sums[2:].reshape(-1)
    fc1_bias_grad = hidden_sums[:local_units]
    qv_bias_grad = hidden_sums[local_units:].reshape(local_heads, PAIR)
    mod_bias_grad = jnp.sum(grad_modulation, 0)
    grad_mod_flat = grad_modulation.reshape(seqs, 6 * col_width)
    mod_part_grad = lax.dot_general(
        cond_act.astype(F32), grad_mod_flat, TN, precision=PRECISE, preferred_element_type=F32
    ).reshape(row_width, 6, col_width)
    cond_part = lax.dot_general(
        grad_mod_flat,
        mod_flat.astype(F32),
        NT,
        precision=PRECISE,
        preferred_element_type=F32,
    )
    cond_pieces = lax.dynamic_update_slice_in_dim(
        jnp.zeros((seqs, D), F32), cond_part, grid.row * row_width, 1
    )
    cond_pieces = (
        cond_pieces.reshape(rows, seq_rows, cols, col_width)
        .transpose(0, 2, 1, 3)
        .reshape(devices, seq_rows, col_width)
    )
    grad_cond_act = all_exchange(cond_pieces).sum(0)
    _, silu_pull = jax.vjp(silu_fn, condition.astype(F32))
    condition_grad = silu_pull(grad_cond_act)[0]
    return (
        layer_out,
        tokens_grad,
        condition_grad,
        mod_part_grad,
        mod_bias_grad,
        qkv_part,
        qv_bias_grad,
        out_part,
        out_bias_grad,
        fc1_part.astype(F32),
        fc1_bias_grad,
        fc2_part.astype(F32).T,
        fc2_bias_grad,
    )


def solution(mesh):
    return jax.shard_map(
        per_device,
        mesh=mesh,
        in_specs=(
            P(("row", "col"), None),
            P("row", "col"),
            P("row", None, "col"),
            P(None, "col"),
            P("row", "col", None),
            P("col", None),
            P("col", None, "row"),
            P("col"),
            P("row", "col"),
            P("col"),
            P("col", "row"),
            P("col"),
            P(("row", "col"), None),
        ),
        out_specs=(
            P(("row", "col"), None),
            P(("row", "col"), None),
            P("row", "col"),
            P("row", None, "col"),
            P(None, "col"),
            P("row", "col", None),
            P("col", None),
            P("col", None, "row"),
            P("col"),
            P("row", "col"),
            P("col"),
            P("col", "row"),
            P("col"),
        ),
        check_vma=False,
    )
```

```python
import functools
import math

import jax
import jax.numpy as jnp
from jax import lax
from jax.experimental import pallas as pl
from jax.experimental.pallas import tpu as pltpu
from jax.sharding import PartitionSpec as P

D = 1024
HD = 64
LEN = 1024
PAIR = 2 * HD

EPSILON = 1e-06
PRECISE = lax.Precision.HIGHEST
NN = (((1,), (0,)), ((), ()))
NT = (((1,), (1,)), ((), ()))
TN = (((0,), (0,)), ((), ()))
F32 = jnp.float32
BF16 = jnp.bfloat16
QUERY_ROWS = 512
TOKEN_ROWS = 32
LARGE_BYTES = 4 * 1024 * 1024
VMEM_NEEDS = {
    "attend": 14,
    "attend_back": 20,
    "tokens": 14,
    "rows": 26,
    "rows_total": 20,
    "columns_product": 26,
    "assemble": 12,
}
SMALL_COST = pl.CostEstimate(flops=1000, bytes_accessed=1000, transcendentals=0)


def vmem_of(need):
    return VMEM_NEEDS[need] * 1024 * 1024


def is_large(array):
    return array.size * array.dtype.itemsize >= LARGE_BYTES


def large_in_hbm(call):
    def wrapped(*arrays):
        return call(
            *[
                pltpu.with_memory_space_constraint(a, pltpu.HBM) if is_large(a) else a
                for a in arrays
            ]
        )

    return wrapped


def large_out(shapes):
    return jax.tree.map(lambda a: pltpu.HBM(a.shape, a.dtype) if is_large(a) else a, shapes)


def dot(left, right, dims=NN):
    return lax.dot_general(left, right, dims, preferred_element_type=F32)


def silu_fn(values):
    return values * jax.nn.sigmoid(values)


def gelu_both(values):
    c = math.sqrt(2.0 / math.pi)
    square = values * values
    half = 0.5 + 0.5 * jnp.tanh(values * (c + (c * 0.044715) * square))
    gelu = values * half
    slope = half + gelu * (1.0 - half) * (2.0 * c + (6.0 * c * 0.044715) * square)
    return gelu, slope


def normalize(resid):
    average = jnp.mean(resid, 1, keepdims=True)
    spread = jnp.mean(resid * resid, 1, keepdims=True) - average * average
    inv_std = lax.rsqrt(spread + EPSILON)
    return ((resid - average) * inv_std, inv_std)


def normalize_back(grad_norm, normed, inv_std):
    average = jnp.mean(grad_norm, 1, keepdims=True)
    crossed = jnp.mean(grad_norm * normed, 1, keepdims=True)
    return inv_std * (grad_norm - average - normed * crossed)


def after(array, *earlier):
    return lax.optimization_barrier((array, *earlier))[0]


def head_lanes(shape, head):
    lane = lax.broadcasted_iota(jnp.int32, shape, 1)
    return lane < HD if head == 0 else lane >= HD


def attend_kernel(q_ref, k_ref, v_ref, *refs):
    mixed_ref, log_ref = refs[-2:]
    queries = q_ref[...] * jnp.asarray(HD**-0.5, BF16)
    key_rows = k_ref[...]
    values_across = v_ref[...].T
    mask = head_lanes(key_rows.shape, 0)
    zero = jnp.zeros_like(key_rows)
    keys = (jnp.where(mask, key_rows, zero), jnp.where(mask, zero, key_rows))
    length = queries.shape[0]
    for start in range(0, length, QUERY_ROWS):
        stop = start + QUERY_ROWS
        q_part = queries[start:stop]
        outs = []
        for head in range(2):
            scores = dot(keys[head], q_part, NT)
            top = jnp.max(scores, 0, keepdims=True)
            expon = jnp.exp(scores - top)
            total = jnp.sum(expon, 0, keepdims=True)
            out = dot(values_across[head * HD : (head + 1) * HD], expon.astype(BF16))
            outs.append(out / total)
            log_ref[0, 0, head : head + 1, start:stop] = top + jnp.log(total)
        mixed_ref[start:stop, :] = jnp.concatenate(outs, 0).T.astype(BF16)


def attend_back_kernel(q_ref, k_ref, v_ref, mixed_ref, grad_ref, log_ref, out_ref, sums_ref):
    scale = jnp.asarray(HD**-0.5, BF16)
    queries = q_ref[...] * scale
    key_rows = k_ref[...]
    value_rows = v_ref[...]
    grad_rows = grad_ref[...]
    mask = head_lanes(value_rows.shape, 0)
    zero = jnp.zeros_like(value_rows)
    keys = (jnp.where(mask, key_rows, zero), jnp.where(mask, zero, key_rows))
    values = (jnp.where(mask, value_rows, zero), jnp.where(mask, zero, value_rows))
    keys_across = (key_rows * scale).T
    product = grad_rows.astype(F32) * mixed_ref[...].astype(F32)
    picks = (
        lax.broadcasted_iota(jnp.int32, (8, PAIR), 0)
        == lax.broadcasted_iota(jnp.int32, (8, PAIR), 1) // HD
    ).astype(F32)
    inner = lax.dot_general(picks, product, NT, precision=PRECISE, preferred_element_type=F32)
    length = queries.shape[0]
    grad_k = [None, None]
    grad_v = [None, None]
    for start in range(0, length, QUERY_ROWS):
        stop = start + QUERY_ROWS
        q_part = queries[start:stop]
        g_part = grad_rows[start:stop]
        outs = []
        for head in range(2):
            scores = dot(keys[head], q_part, NT)
            probs = jnp.exp(scores - log_ref[0, 0, head : head + 1, start:stop])
            grad_probs = dot(values[head], g_part, NT)
            grad_scores = (probs * (grad_probs - inner[head : head + 1, start:stop])).astype(BF16)
            part_v = dot(probs.astype(BF16), g_part)
            part_k = dot(grad_scores, q_part)
            grad_v[head] = part_v if grad_v[head] is None else grad_v[head] + part_v
            grad_k[head] = part_k if grad_k[head] is None else grad_k[head] + part_k
            outs.append(dot(keys_across[head * HD : (head + 1) * HD], grad_scores))
        out_ref[start:stop, 0:PAIR] = jnp.concatenate(outs, 0).T.astype(BF16)
    out_ref[:, PAIR : 2 * PAIR] = jnp.where(mask, grad_k[0], grad_k[1]).astype(BF16)
    out_ref[:, 2 * PAIR :] = jnp.where(mask, grad_v[0], grad_v[1]).astype(BF16)
    sums_ref[0, 0] = jnp.sum(out_ref[...].astype(F32).reshape(length // 8, 8, 3 * PAIR), 0)


def attention_specs(first):
    part = lambda offset: pl.BlockSpec((LEN, PAIR), lambda s, p: (s, 3 * (p + first) + offset))
    plain = pl.BlockSpec((LEN, PAIR), lambda s, p: (s, p + first))
    logs = pl.BlockSpec((1, 1, 2, LEN), lambda s, p: (s, p + first, 0, 0))
    return [part(0), part(1), part(2)], plain, logs


def attend(projected, latents, pairs, first, count, earlier=()):
    parts, plain, logs = attention_specs(first)
    rows = projected.shape[0]
    call = pl.pallas_call(
        attend_kernel,
        grid=(latents, count),
        in_specs=parts + [pl.BlockSpec(memory_space=pl.ANY)] * len(earlier),
        out_specs=[plain, logs],
        out_shape=[
            jax.ShapeDtypeStruct((rows, pairs * PAIR), BF16),
            jax.ShapeDtypeStruct((latents, pairs, 2, LEN), F32),
        ],
        input_output_aliases={3 + i: i for i in range(len(earlier))},
        compiler_params=pltpu.CompilerParams(vmem_limit_bytes=vmem_of("attend")),
        cost_estimate=SMALL_COST,
        name="attend",
    )
    return large_in_hbm(call)(projected, projected, projected, *earlier)


def attend_back(projected, mixed, grad_mixed, log_totals, latents, first, count):
    parts, plain, logs = attention_specs(first)
    rows = projected.shape[0]
    call = pl.pallas_call(
        attend_back_kernel,
        grid=(latents, count),
        in_specs=[*parts, plain, plain, logs],
        out_specs=[
            pl.BlockSpec((LEN, 3 * PAIR), lambda s, p: (s, p)),
            pl.BlockSpec((1, 1, 8, 3 * PAIR), lambda s, p: (s, p, 0, 0)),
        ],
        out_shape=large_out([
            jax.ShapeDtypeStruct((rows, count * 3 * PAIR), BF16),
            jax.ShapeDtypeStruct((latents, count, 8, 3 * PAIR), F32),
        ]),
        compiler_params=pltpu.CompilerParams(vmem_limit_bytes=vmem_of("attend_back")),
        cost_estimate=SMALL_COST,
        name="attend_back",
    )
    return large_in_hbm(call)(projected, projected, projected, mixed, grad_mixed, log_totals)


def kernel_call(body, grid, in_specs, out_specs, out_shape, name, need):
    call = pl.pallas_call(
        body,
        grid=grid,
        in_specs=in_specs,
        out_specs=out_specs,
        out_shape=large_out(out_shape),
        compiler_params=pltpu.CompilerParams(vmem_limit_bytes=vmem_of(need)),
        cost_estimate=SMALL_COST,
        name=name,
    )
    return large_in_hbm(call)


def whole(array):
    return pl.BlockSpec(array.shape, lambda *step: (0,) * array.ndim)


def pieces_of(array, ids, width):
    return {i: (array, place, width) for place, i in enumerate(ids)}


def piece_spec(piece):
    array, block, width = piece
    return pl.BlockSpec((array.shape[0], width), lambda *step: (0, block))


def row_specs(local_rows, tile, width):
    count = local_rows // tile
    mine = pl.BlockSpec((tile, width), lambda i: (jnp.minimum(i, count - 1), 0))
    theirs = pl.BlockSpec((tile, width), lambda i: (jnp.maximum(i - count, 0), 0))
    return count, mine, theirs


def rows_product(pair, weights, extra, kind):
    local_rows, depth = pair[0].shape
    tile = min(512, local_rows)
    count, mine, theirs = row_specs(local_rows, tile, depth)
    widths = [piece[2] for piece in weights]
    width = sum(widths)
    total = 2 * local_rows

    def body(*refs):
        mine_ref, theirs_ref = refs[:2]
        weight_refs = refs[2 : 2 + len(weights)]
        extra_ref = refs[2 + len(weights)]
        out_refs = refs[3 + len(weights) :]
        step = pl.program_id(0)
        left = jnp.where(step < count, mine_ref[...], theirs_ref[...])
        if kind == "slope":

            @pl.when(step == 0)
            def _():
                out_refs[1][...] = jnp.zeros(out_refs[1].shape, F32)

        start = 0
        for ref, span in zip(weight_refs, widths):
            step_width = min(256, span)
            for low in range(0, span, step_width):
                cols = slice(start + low, start + low + step_width)
                product = dot(left, ref[:, low : low + step_width])
                if kind == "bias":
                    out_refs[0][:, cols] = (product + extra_ref[:, cols]).astype(BF16)
                elif kind == "gelu":
                    act, slope = gelu_both(product + extra_ref[:, cols])
                    out_refs[0][:, cols] = act.astype(BF16)
                    out_refs[1][:, cols] = slope.astype(BF16)
                else:
                    grad = (product * extra_ref[:, cols].astype(F32)).astype(BF16)
                    out_refs[0][:, cols] = grad
                    out_refs[1][:, cols] += jnp.sum(
                        grad.astype(F32).reshape(tile // 8, 8, step_width), 0
                    )
            start += span

    rows_out = pl.BlockSpec((tile, width), lambda i: (i, 0))
    low_shape = jax.ShapeDtypeStruct((total, width), BF16)
    if kind == "bias":
        out_specs, out_shape = [rows_out], [low_shape]
    elif kind == "gelu":
        out_specs, out_shape = [rows_out, rows_out], [low_shape, low_shape]
    else:
        out_specs = [rows_out, pl.BlockSpec((8, width), lambda i: (0, 0))]
        out_shape = [low_shape, jax.ShapeDtypeStruct((8, width), F32)]
    extra_spec = rows_out if kind == "slope" else whole(extra)
    return kernel_call(
        body,
        (2 * count,),
        [mine, theirs, *[piece_spec(w) for w in weights], extra_spec],
        out_specs,
        out_shape,
        "rows_" + kind,
        "rows",
    )(*pair, *[w[0] for w in weights], extra)


def columns_of(refs, start, stop):
    for ref in refs:
        if start < ref.shape[1]:
            return ref[:, start:stop]
        start, stop = start - ref.shape[1], stop - ref.shape[1]


def rows_total(lefts, weights):
    local_rows = lefts[0].shape[0] // 2
    tile = min(512, local_rows)
    count = local_rows // tile
    width = weights[0][0].shape[0]
    ends = set()
    for spans in ([a.shape[1] for a in lefts], [w[2] for w in weights]):
        end = 0
        for span in spans:
            end += span
            ends.add(end)
    ends = sorted(ends)

    def body(*refs):
        left_refs = refs[: len(lefts)]
        weight_refs = refs[len(lefts) : -2]
        mine_ref, theirs_ref = refs[-2:]
        total = None
        for start, stop in zip([0] + ends, ends):
            part = dot(columns_of(left_refs, start, stop), columns_of(weight_refs, start, stop), NT)
            total = part if total is None else total + part
        step = pl.program_id(0)

        @pl.when(step < count)
        def _():
            mine_ref[...] = total

        @pl.when(step >= count)
        def _():
            theirs_ref[...] = total.astype(BF16)

    return kernel_call(
        body,
        (2 * count,),
        [pl.BlockSpec((tile, a.shape[1]), lambda i: (i, 0)) for a in lefts]
        + [piece_spec(w) for w in weights],
        [
            pl.BlockSpec((tile, width), lambda i: (jnp.minimum(i, count - 1), 0)),
            pl.BlockSpec((tile, width), lambda i: (jnp.maximum(i - count, 0), 0)),
        ],
        [
            jax.ShapeDtypeStruct((local_rows, width), F32),
            jax.ShapeDtypeStruct((local_rows, width), BF16),
        ],
        "rows_total",
        "rows_total",
    )(*lefts, *[w[0] for w in weights])


def token_kernel(body, arrays, rows_of, out_types, sums, name):
    tokens = arrays[0].shape[0]
    tile = min(256, tokens)
    outs = len(out_types)

    def kernel(*refs):
        rows_ref = refs[len(arrays)]
        out_refs = refs[len(arrays) + 1 :]
        rows = [rows_ref[i : i + 1, :] for i in range(8)]
        if sums:
            sum_ref = out_refs[outs]

            @pl.when(pl.program_id(0) == 0)
            def _():
                sum_ref[...] = jnp.zeros(sum_ref.shape, F32)

        for start in range(0, tile, TOKEN_ROWS):
            lines = slice(start, start + TOKEN_ROWS)
            values = [ref[lines, :].astype(F32) for ref in refs[: len(arrays)]]
            results, columns = body(values, rows)
            for ref, result in zip(out_refs, results):
                ref[lines, :] = result.astype(ref.dtype)
            for i, column in enumerate(columns):
                sum_ref[i] += jnp.sum(column.reshape(TOKEN_ROWS // 8, 8, D), 0)

    tokens_spec = pl.BlockSpec((tile, D), lambda i: (i, 0))
    out_specs = [tokens_spec] * outs
    out_shape = [jax.ShapeDtypeStruct((tokens, D), t) for t in out_types]
    if sums:
        out_specs = out_specs + [pl.BlockSpec((sums, 8, D), lambda i: (0, 0, 0))]
        out_shape = out_shape + [jax.ShapeDtypeStruct((sums, 8, D), F32)]
    return kernel_call(
        kernel,
        (tokens // tile,),
        [tokens_spec] * len(arrays) + [whole(rows_of)],
        out_specs,
        out_shape,
        name,
        "tokens",
    )(*arrays, rows_of)


def middle_body(values, rows):
    mine, theirs, tokens = values
    gate, shift, scale, bias = rows[2], rows[3], rows[4], rows[6]
    attention_out = mine + theirs + bias
    normed, _ = normalize(tokens + gate * attention_out)
    return [attention_out, normed * (1.0 + scale) + shift], []


def middle_back_body(values, rows):
    mine, theirs, upstream, tokens, attention_out = values
    gate, scale = rows[2], rows[4]
    grad_hidden = mine + theirs
    normed, inv_std = normalize(tokens + gate * attention_out)
    grad = upstream + normalize_back(grad_hidden * (1.0 + scale), normed, inv_std)
    grad_attention = grad * gate
    return [grad, grad_attention], [
        grad_hidden,
        grad_hidden * normed,
        grad * attention_out,
        grad_attention,
    ]


def first_back_body(values, rows):
    mine, theirs, tokens, grad_resid = values
    scale = rows[1]
    grad_hidden = mine + theirs
    normed, inv_std = normalize(tokens)
    grad = grad_resid + normalize_back(grad_hidden * (1.0 + scale), normed, inv_std)
    return [grad], [grad_hidden, grad_hidden * normed]


def last_body(values, rows):
    mine, theirs, tokens, attention_out, upstream = values
    gate_attn, gate_feed, bias = rows[2], rows[5], rows[7]
    feed_out = mine + theirs + bias
    resid_mid = tokens + gate_attn * attention_out
    return [resid_mid + gate_feed * feed_out], [upstream * feed_out, upstream * gate_feed]


def columns_product(pair, right, added, outs, width):
    local_rows, depth = pair[0].shape
    rows = right.shape[0]
    tile = 256
    blocks = [i for ids in outs for i in ids]
    extra = list(added)
    per_extra = len(blocks) // max(1, len(extra))

    def body(mine_ref, theirs_ref, *refs):
        right_refs = refs[: len(blocks)]
        add_refs = refs[len(blocks) : len(blocks) + len(extra)]
        out_refs = refs[len(blocks) + len(extra) :]
        mine, theirs = mine_ref[...].T, theirs_ref[...].T
        number = 0
        for ref, ids in zip(out_refs, outs):
            for place in range(len(ids)):
                total = dot(mine, right_refs[number][:local_rows])
                total = total + dot(theirs, right_refs[number][local_rows:])
                if extra:
                    start = number % per_extra * width
                    part = add_refs[number // per_extra][:, start : start + width]
                    total = total + part.astype(F32)
                ref[:, place * width : (place + 1) * width] = total.astype(BF16)
                number += 1

    token_spec = pl.BlockSpec((local_rows, tile), lambda i: (0, i))

    def out_spec(count):
        return pl.BlockSpec((tile, count * width), lambda i: (i, 0))

    return kernel_call(
        body,
        (depth // tile,),
        [token_spec, token_spec]
        + [pl.BlockSpec((rows, width), lambda i, b=b: (0, b)) for b in blocks]
        + [out_spec(per_extra) for _ in extra],
        [out_spec(len(ids)) for ids in outs],
        [jax.ShapeDtypeStruct((depth, len(ids) * width), BF16) for ids in outs],
        "columns_product",
        "columns_product",
    )(*pair, *[right] * len(blocks), *extra)


def assemble(top, low, qkv_width, out_width):
    parts = [top[0], top[2], low[0], low[2]]
    ids = [top[1], top[3], low[1], low[3]]
    half, width = parts[0].shape
    block = qkv_width + out_width
    blocks = 2 * width // block
    tile = 128

    def body(a_ref, b_ref, c_ref, d_ref, qkv_ref, out_ref):
        for number, ref in enumerate((a_ref, b_ref, c_ref, d_ref)):
            for place, i in enumerate(ids[number]):
                start = place * block
                qkv_ref[number // 2, :, i * qkv_width : (i + 1) * qkv_width] = ref[
                    :, start : start + qkv_width
                ]
                out_ref[number // 2, :, i * out_width : (i + 1) * out_width] = ref[
                    :, start + qkv_width : start + block
                ]

    qkv, out = kernel_call(
        body,
        (half // tile,),
        [pl.BlockSpec((tile, width), lambda i: (i, 0))] * 4,
        [
            pl.BlockSpec((2, tile, blocks * qkv_width), lambda i: (0, i, 0)),
            pl.BlockSpec((2, tile, blocks * out_width), lambda i: (0, i, 0)),
        ],
        [
            jax.ShapeDtypeStruct((2, half, blocks * qkv_width), BF16),
            jax.ShapeDtypeStruct((2, half, blocks * out_width), BF16),
        ],
        "assemble",
        "assemble",
    )(*parts)
    return qkv.reshape(2 * half, -1), out.reshape(2 * half, -1)


class Grid:
    def __init__(self):
        self.rows = lax.axis_size("row")
        self.cols = lax.axis_size("col")
        self.chips = self.cols // 2
        self.bits = [1 << b for b in range(self.chips.bit_length() - 1)]
        self.orders = (self.bits, self.bits[::-1])
        self.row = lax.axis_index("row")
        self.col = lax.axis_index("col")
        self.core = self.col % 2
        source = lax.iota(jnp.int32, self.chips) ^ (self.col // 2)
        self.choose = (
            (2 * source + self.core)[:, None] == lax.iota(jnp.int32, self.cols)[None, :]
        ).astype(F32)

    def swap(self, array, flip):
        pairs = [(i, i ^ flip) for i in range(self.cols)]
        return lax.ppermute(array, "col", pairs)

    def swap_core(self, array):
        return self.swap(array, 1)

    def swap_chip(self, array, bit):
        return self.swap(array, 2 * bit)

    def to_relative(self, blocks):
        flat = blocks.reshape(self.cols, -1).astype(F32)
        picked = lax.dot_general(
            self.choose, flat, NN, precision=PRECISE, preferred_element_type=F32
        )
        return picked.reshape((self.chips,) + blocks.shape[1:])

    def to_absolute(self, blocks):
        flat = blocks.reshape(self.chips, -1)
        placed = lax.dot_general(
            self.choose, flat, TN, precision=PRECISE, preferred_element_type=F32
        )
        return placed.reshape((self.cols,) + blocks.shape[1:])

    def gather_rows(self, block):
        count = self.rows
        got = [block]
        for step in range(1, count):
            got.append(
                lax.ppermute(block, "row", [(i, (i + step) % count) for i in range(count)])
            )
        stacked = jnp.stack(got)
        ordered = [
            lax.dynamic_index_in_dim(stacked, (self.row - i) % count, 0, keepdims=False)
            for i in range(count)
        ]
        return jnp.concatenate(ordered, 0), got[-1]

    def scatter_rows(self, whole):
        count = self.rows
        blocks = whole.reshape(count, whole.shape[0] // count, whole.shape[1])
        total = lax.dynamic_index_in_dim(blocks, self.row, 0, keepdims=False).astype(F32)
        for step in range(1, count):
            sent = lax.dynamic_index_in_dim(blocks, (self.row + step) % count, 0, keepdims=False)
            total = total + lax.ppermute(
                sent, "row", [(i, (i + step) % count) for i in range(count)]
            ).astype(F32)
        return total

    def gather_early(self, block, order, late=()):
        held, ids = block, [0]
        for bit in order[:-1]:
            got = self.swap_chip(held, bit)
            if bit == order[-2]:
                got = after(got, *late)
            held = jnp.concatenate([held, got], 1)
            ids = ids + [bit ^ i for i in ids]
        return held, ids

    def early_ids(self, order):
        ids = [0]
        for bit in order[:-1]:
            ids = ids + [bit ^ i for i in ids]
        return ids

    def gather_last(self, held, ids, order):
        return self.swap_chip(held, order[-1]), [order[-1] ^ i for i in ids]

    def scatter_chips(self, keep, send, order, late=()):
        for bit in order[-2::-1]:
            got = self.swap_chip(send, bit)
            if bit == order[-2]:
                got = after(got, *late)
            total = keep.astype(F32) + got.astype(F32)
            if bit == order[0]:
                return total
            half = total.shape[1] // 2
            keep, send = total[:, :half], total[:, half:].astype(BF16)


def split_columns(array, ids):
    width = array.shape[1] // len(ids)
    return {i: array[:, n * width : (n + 1) * width] for n, i in enumerate(ids)}


def all_exchange(pieces):
    return lax.all_to_all(pieces, ("row", "col"), 0, 0, tiled=True)


def per_device(
    tokens,
    condition,
    mod_weight,
    mod_bias,
    qkv_weight,
    qv_bias,
    out_weight,
    out_bias,
    fc1_weight,
    fc1_bias,
    fc2_weight,
    fc2_bias,
    cotangent,
):
    grid = Grid()
    rows, cols, chips = grid.rows, grid.cols, grid.chips
    devices = rows * cols
    local_rows = tokens.shape[0]
    both_rows = 2 * local_rows
    latents = both_rows // LEN
    span = LEN // local_rows
    seq_rows = condition.shape[0]
    seqs = seq_rows * rows
    row_width = D // rows
    col_width = D // cols
    local_heads = qkv_weight.shape[1]
    local_units = fc1_weight.shape[1]
    plane_heads = local_heads * chips
    pairs = plane_heads // 2
    qkv_width = local_heads * 3 * HD
    out_width = local_heads * HD

    if local_heads % 2 == 0:
        qkv_local = (
            qkv_weight.reshape(row_width, local_heads // 2, 2, 3, HD)
            .transpose(0, 1, 3, 2, 4)
            .reshape(row_width, qkv_width)
        )
    else:
        qkv_local = qkv_weight.reshape(row_width, qkv_width)
    attn_local = jnp.concatenate(
        [qkv_local, out_weight.reshape(out_width, row_width).T], 1
    )
    attn_width = qkv_width + out_width
    fc1_local = fc1_weight
    fc2_local = fc2_weight.T

    small = jnp.concatenate(
        [
            condition.reshape(-1),
            fc1_bias,
            qv_bias.reshape(-1),
            out_bias,
            fc2_bias,
        ]
    )
    small_all = all_exchange(
        jnp.broadcast_to(small.reshape(1, -1, 128), (devices, small.size // 128, 128))
    )

    attn_rows, mark = grid.gather_rows(attn_local)
    fc1_rows = lax.all_gather(after(fc1_local, mark), "row", axis=0, tiled=True)
    fc2_rows = lax.all_gather(after(fc2_local, fc1_rows), "row", axis=0, tiled=True)
    half = D // 2
    top = grid.gather_early(attn_rows[:half], grid.orders[0])
    low = grid.gather_early(attn_rows[half:], grid.orders[1])
    small_all = small_all.reshape(rows, cols, -1)
    cut = seq_rows * col_width
    cond_all = (
        small_all[:, :, :cut]
        .reshape(rows, cols, seq_rows, col_width)
        .transpose(0, 2, 1, 3)
        .reshape(seqs, D)
    )
    biases = small_all[0, :, cut:]
    fc1_bias_all = biases[:, :local_units]
    qv_bias_all = biases[:, local_units : local_units + local_heads * PAIR]
    out_bias_all = biases[:, -2 * col_width : -col_width].reshape(1, D).astype(F32)
    fc2_bias_all = biases[:, -col_width:].reshape(1, D).astype(F32)

    cond_act = silu_fn(cond_all.astype(F32)).astype(BF16)
    cond_act = lax.dynamic_slice_in_dim(cond_act, grid.row * row_width, row_width, 1)
    mod_flat = mod_weight.reshape(row_width, 6 * col_width)
    own_bias = jnp.where(grid.row == 0, mod_bias.astype(F32), 0.0)
    mod_part = dot(cond_act, mod_flat).reshape(seqs, 6, col_width) + own_bias
    mod_part = jnp.broadcast_to(
        mod_part[:, None], (seqs, span, 6, col_width)
    ).reshape(devices, 6, col_width)
    modulation = (
        all_exchange(mod_part)
        .reshape(rows, cols, 6, col_width)
        .sum(0)
        .transpose(1, 0, 2)
        .reshape(6, 1, D)
    )
    shift_attn, scale_attn, gate_attn, shift_feed, scale_feed, gate_feed = modulation
    token_rows = jnp.concatenate([modulation.reshape(6, D), out_bias_all, fc2_bias_all], 0)

    top = top + grid.gather_last(*top, grid.orders[0])
    low = low + grid.gather_last(*low, grid.orders[1])
    if local_heads % 2 == 0:
        qkv_w, out_w = assemble(top, low, qkv_width, out_width)
    else:
        attn_top = {**split_columns(top[0], top[1]), **split_columns(top[2], top[3])}
        attn_low = {**split_columns(low[0], low[1]), **split_columns(low[2], low[3])}
        attn_blocks = [jnp.concatenate([attn_top[i], attn_low[i]], 0) for i in range(chips)]
        qkv_w = (
            jnp.stack([b[:, :qkv_width] for b in attn_blocks], 1)
            .reshape(D, pairs, 2, 3, HD)
            .transpose(0, 1, 3, 2, 4)
            .reshape(D, pairs * 3 * PAIR)
        )
        out_w = jnp.concatenate([b[:, qkv_width:] for b in attn_blocks], 1)

    fc1_bias_rel = grid.to_relative(fc1_bias_all).reshape(1, chips * local_units)
    qv_rel = grid.to_relative(qv_bias_all).reshape(pairs, 2, 2, HD).transpose(0, 2, 1, 3)
    qkv_bias_rel = jnp.concatenate(
        [qv_rel[:, :1], jnp.zeros_like(qv_rel[:, :1]), qv_rel[:, 1:]], 1
    ).reshape(1, pairs * 3 * PAIR)

    def both(mine):
        return (mine, grid.swap_core(mine))

    def own_total(lefts, weights):
        mine, theirs = rows_total(lefts, weights)
        return mine, grid.swap_core(theirs)

    def sum_rows(parts):
        return lax.psum_scatter(parts, "row", scatter_dimension=0, tiled=True)

    resid = tokens.astype(F32)
    normed_attn, _ = normalize(resid)
    hidden_attn = both((normed_attn * (1.0 + scale_attn) + shift_attn).astype(BF16))
    grad_feed_low = both((cotangent.astype(F32) * gate_feed).astype(BF16))

    (projected,) = rows_product(hidden_attn, [(qkv_w, 0, qkv_w.shape[1])], qkv_bias_rel, "bias")
    unit_half = local_units // 2

    def units_early(held, earlier, late):
        held = after(held, *earlier)
        parts = (held[:, :unit_half], held[:, unit_half:])
        return [grid.gather_early(part, order, late) for part, order in zip(parts, grid.orders)]

    def units_last(early, *earlier):
        return [
            grid.gather_last(after(held, *earlier), ids, order)
            for (held, ids), order in zip(early, grid.orders)
        ]

    def unit_pieces(early, last):
        found = [{**pieces_of(*e, unit_half), **pieces_of(*l, unit_half)} for e, l in zip(early, last)]
        return [found[part][i] for i in range(chips) for part in range(2)]

    fc1_early = units_early(fc1_rows, (top[2], low[2]), (projected,))
    fc1_last = units_last(fc1_early)
    fc1_got_last = [got for got, _ in fc1_last]
    projected = after(projected, *[held for held, _ in fc1_early])
    middle_pair = pairs // 2
    first_half = attend(projected, latents, pairs, 0, middle_pair)
    fc2_early = units_early(fc2_rows, (first_half[0], *fc1_got_last), ())
    mixed, log_totals = attend(
        after(projected, first_half[0], *fc1_got_last),
        latents,
        pairs,
        middle_pair,
        pairs - middle_pair,
        first_half,
    )
    fc2_last = units_last(fc2_early, mixed)
    mixed = after(mixed, *[held for held, _ in fc2_early])
    fc1_all = unit_pieces(fc1_early, fc1_last)
    fc2_all = unit_pieces(fc2_early, fc2_last)
    out_all = [(out_w, 0, out_w.shape[1])]
    totals = own_total([mixed], out_all)
    attention_out, hidden_feed = token_kernel(
        middle_body,
        [*totals, tokens],
        token_rows,
        [F32, BF16],
        0,
        "middle",
    )
    hidden_feed = both(hidden_feed)
    acts, slopes = rows_product(hidden_feed, fc1_all, fc1_bias_rel, "gelu")
    acts = after(acts, *[got for got, _ in fc2_last])

    def send_units(left, right, orders):
        count = len(orders)
        outs = [
            [count * (order[-1] ^ i) + part for i in grid.early_ids(order)]
            for part, order in enumerate(orders)
        ]
        sent = columns_product(left, right, [], outs, local_units // count)
        return [grid.swap_chip(a, order[-1]) for a, order in zip(sent, orders)], sent[0]

    def keep_units(left, right, got, orders):
        count = len(orders)
        outs = []
        for part, order in enumerate(orders):
            places = [count * i + part for i in grid.early_ids(order)]
            outs += [places[: len(places) // 2], places[len(places) // 2 :]]
        return columns_product(left, right, got, outs, local_units // count)

    def sum_chips(kept, orders, late):
        sums = [
            grid.scatter_chips(kept[2 * part], kept[2 * part + 1], order, late)
            for part, order in enumerate(orders)
        ]
        return jnp.concatenate(sums, 1).astype(BF16)

    fc2_got, fc2_sent = send_units(grad_feed_low, acts, grid.orders)
    grad_pre, bias_fc1 = rows_product(
        (after(grad_feed_low[0], fc2_sent), grad_feed_low[1]), fc2_all, slopes, "slope"
    )
    fc1_got, sent = send_units(hidden_feed, grad_pre, grid.orders)
    totals = own_total([after(grad_pre, sent, *fc2_got)], fc1_all)
    fc2_kept = keep_units(grad_feed_low, after(acts, totals[0]), fc2_got, grid.orders)
    grad_resid_mid, grad_attention_low, middle_sums = token_kernel(
        middle_back_body,
        [after(totals[0], fc2_kept[0]), totals[1], cotangent, tokens, attention_out],
        token_rows,
        [F32, BF16],
        4,
        "middle_back",
    )
    grad_attention_low = both(grad_attention_low)

    (grad_mixed,) = rows_product(
        grad_attention_low, out_all, jnp.zeros((1, out_w.shape[1]), F32), "bias"
    )
    (grad_out,) = columns_product(
        grad_attention_low, after(mixed, grad_mixed), [], [[0]], mixed.shape[1]
    )
    grad_mixed = after(grad_mixed, grad_out)
    grad_late, bias_late = attend_back(
        projected, mixed, grad_mixed, log_totals, latents, 1, pairs - 1
    )
    fc2_sums = sum_chips(fc2_kept, grid.orders, (grad_late,))
    fc1_kept = keep_units(hidden_feed, after(grad_pre, grad_late), fc1_got, grid.orders)
    late_chips = chips * (pairs - 1) // pairs
    qkv_late = columns_product(
        hidden_attn, grad_late, [], [[i] for i in range(late_chips)], qkv_width
    ) if (
        local_heads % 2 == 0
    ) else None
    early_input = after(grad_mixed, grad_late, fc2_sums, fc1_kept[0])
    grad_early, bias_early = attend_back(
        projected, mixed, early_input, log_totals, latents, 0, 1
    )
    fc1_sums = sum_chips(fc1_kept, grid.orders, (grad_early,))
    fc2_part = sum_rows(fc2_sums)
    fc1_part = sum_rows(fc1_sums)
    bias_qkv = jnp.concatenate([bias_early, bias_late], 1).sum((0, 2))
    if local_heads % 2 == 0:
        qkv_early = columns_product(hidden_attn, grad_early, [], [[0]], qkv_width)
        grad_qkv = [*qkv_early, *qkv_late]
    else:
        grad_projected = jnp.concatenate([grad_early, grad_late], 1)
        (grad_qkv,) = columns_product(
            hidden_attn, grad_projected, [], [[0]], 3 * PAIR * pairs
        )
        grad_qkv = (
            grad_qkv.reshape(D, pairs, 3, 2, HD).transpose(0, 1, 3, 2, 4).reshape(D, chips, qkv_width)
        )
        grad_qkv = [grad_qkv[:, i] for i in range(chips)]

    def pick(part, ids):
        lines = slice(0, half) if part == 0 else slice(half, D)
        return jnp.concatenate(
            [
                array
                for i in ids
                for array in (
                    grad_qkv[i][lines],
                    grad_out[lines, i * out_width : (i + 1) * out_width],
                )
            ],
            1,
        )

    attn_got = [
        grid.swap_chip(pick(number, gathered[3]), grid.orders[number][-1])
        for number, gathered in enumerate((top, low))
    ]
    attn_sums = []
    for number, gathered in enumerate((top, low)):
        order = grid.orders[number]
        kept = pick(number, gathered[1]).astype(F32) + attn_got[number].astype(F32)
        middle = kept.shape[1] // 2
        attn_sums.append(
            grid.scatter_chips(kept[:, :middle], kept[:, middle:].astype(BF16), order)
        )
    attn_part = grid.scatter_rows(jnp.concatenate(attn_sums, 0).astype(BF16))
    qkv_part = attn_part[:, :qkv_width]
    if local_heads % 2 == 0:
        qkv_part = qkv_part.reshape(row_width, local_heads // 2, 3, 2, HD).transpose(0, 1, 3, 2, 4)
    qkv_part = qkv_part.reshape(row_width, local_heads, 3 * HD)
    out_part = attn_part[:, qkv_width:].T.reshape(local_heads, HD, row_width)

    totals = own_total([after(grad_early, *attn_got), grad_late], [(qkv_w, 0, qkv_w.shape[1])])
    tokens_grad, first_sums = token_kernel(
        first_back_body, [*totals, tokens, grad_resid_mid], token_rows, [F32], 2, "first_back"
    )
    totals = own_total([after(acts, totals[0], fc2_part, *attn_sums)], fc2_all)
    layer_out, last_sums = token_kernel(
        last_body, [after(totals[0], fc1_part), totals[1], tokens, attention_out, cotangent], token_rows, [BF16], 2, "last"
    )

    first_sums, middle_sums, last_sums = (
        sums.sum(1) for sums in (first_sums, middle_sums, last_sums)
    )
    mod_rows = jnp.concatenate(
        [first_sums, middle_sums[2:3], middle_sums[:2], last_sums[:1], middle_sums[3:], last_sums[1:]]
    )
    mod_rows = mod_rows.reshape(8, cols, col_width).transpose(1, 0, 2)
    fc1_rel = bias_fc1.sum(0).reshape(chips, local_units)
    qkv_rel = bias_qkv.reshape(pairs, 3, 2, HD)
    qv_rel = jnp.stack([qkv_rel[:, 0], qkv_rel[:, 2]], 2).reshape(chips, local_heads * PAIR)
    hidden_rows = grid.to_absolute(jnp.concatenate([fc1_rel, qv_rel], 1)).reshape(
        cols, -1, col_width
    )
    pieces = jnp.concatenate([mod_rows, hidden_rows], 1)
    pieces = jnp.broadcast_to(pieces[None], (rows,) + pieces.shape).reshape(
        devices, -1, col_width
    )
    arrived = all_exchange(pieces)
    grad_modulation = arrived[:, :6].reshape(seqs, span, 6, col_width).sum(1)
    sums = arrived[:, 6:].sum(0)
    out_bias_grad = sums[0]
    fc2_bias_grad = sums[1]
    hidden_sums = sums[2:].reshape(-1)
    fc1_bias_grad = hidden_sums[:local_units]
    qv_bias_grad = hidden_sums[local_units:].reshape(local_heads, PAIR)
    mod_bias_grad = jnp.sum(grad_modulation, 0)
    grad_mod_flat = grad_modulation.reshape(seqs, 6 * col_width)
    mod_part_grad = lax.dot_general(
        cond_act.astype(F32), grad_mod_flat, TN, precision=PRECISE, preferred_element_type=F32
    ).reshape(row_width, 6, col_width)
    cond_part = lax.dot_general(
        grad_mod_flat,
        mod_flat.astype(F32),
        NT,
        precision=PRECISE,
        preferred_element_type=F32,
    )
    cond_pieces = lax.dynamic_update_slice_in_dim(
        jnp.zeros((seqs, D), F32), cond_part, grid.row * row_width, 1
    )
    cond_pieces = (
        cond_pieces.reshape(rows, seq_rows, cols, col_width)
        .transpose(0, 2, 1, 3)
        .reshape(devices, seq_rows, col_width)
    )
    grad_cond_act = all_exchange(cond_pieces).sum(0)
    _, silu_pull = jax.vjp(silu_fn, condition.astype(F32))
    condition_grad = silu_pull(grad_cond_act)[0]
    return (
        layer_out,
        tokens_grad,
        condition_grad,
        mod_part_grad,
        mod_bias_grad,
        qkv_part,
        qv_bias_grad,
        out_part,
        out_bias_grad,
        fc1_part.astype(F32),
        fc1_bias_grad,
        fc2_part.astype(F32).T,
        fc2_bias_grad,
    )


def solution(mesh):
    return jax.shard_map(
        per_device,
        mesh=mesh,
        in_specs=(
            P(("row", "col"), None),
            P("row", "col"),
            P("row", None, "col"),
            P(None, "col"),
            P("row", "col", None),
            P("col", None),
            P("col", None, "row"),
            P("col"),
            P("row", "col"),
            P("col"),
            P("col", "row"),
            P("col"),
            P(("row", "col"), None),
        ),
        out_specs=(
            P(("row", "col"), None),
            P(("row", "col"), None),
            P("row", "col"),
            P("row", None, "col"),
            P(None, "col"),
            P("row", "col", None),
            P("col", None),
            P("col", None, "row"),
            P("col"),
            P("row", "col"),
            P("col"),
            P("col", "row"),
            P("col"),
        ),
        check_vma=False,
    )
```
